32 devices in a mesh: section: 4 (over y, x), dp: 8 (over z, core).
Axes of the slice: x: 2, y: 2, z: 4, core: 2. Of those that a mesh axis runs over, the one named last changes fastest.
Arguments:
- tokens: bfloat16 [4096, 768], P('dp'), may hold values from -6 to 6
- cotangent: bfloat16 [4, 4096, 768], P('section', 'dp'), may hold values from -6 to 6
- positions: float32 [32, 3, 128], P('dp'), may hold values from -6 to 6
- conformer_group: int32 [32], P('dp'), may hold values from 0 to 1, as said below
- atom_counts: int32 [16], P('dp'), may hold values from 32 to 128, as said below
- path_dist: int32 [16, 128, 128], P('dp'), may hold values from 0 to 63
- edge_kind: int32 [16, 128, 128], P('dp'), may hold values from 0 to 31
- attn_in: bfloat16 [4, 768, 2304], P('section'), may hold values from -0.21875 to 0.21875
- attn_out: bfloat16 [4, 768, 768], P('section'), may hold values from -0.625 to 0.625
- ffn_up: bfloat16 [4, 768, 768], P('section'), may hold values from -0.21875 to 0.21875
- ffn_down: bfloat16 [4, 768, 768], P('section'), may hold values from -0.21875 to 0.21875
- norm_gain: bfloat16 [4, 768, 2], P('section'), may hold values from 0.25 to 1.75
- norm_shift: bfloat16 [4, 768, 2], P('section'), may hold values from -2 to 2
- kernel_proj: bfloat16 [128, 32], replicated, may hold values from -1.5 to 1.5
- path_table: bfloat16 [64, 32], replicated, may hold values from -3 to 3
- edge_table: bfloat16 [32, 32], replicated, may hold values from -3 to 3
Outputs:
- hidden: bfloat16 [4, 4096, 768], P('section', 'dp')
- input_grads: bfloat16 [4, 4096, 768], P('section', 'dp')
- grad_attn_in: float32 [4, 768, 2304], P('section', 'dp')
- grad_attn_out: float32 [4, 768, 768], P('section', 'dp')
- grad_ffn_up: float32 [4, 768, 768], P('section', 'dp')
- grad_ffn_down: float32 [4, 768, 768], P('section', 'dp')
- grad_norm_gain: float32 [4, 768, 2], P('section', 'dp')
- grad_norm_shift: float32 [4, 768, 2], P('section', 'dp')
- grad_kernel_proj: float32 [128, 32], P('section')
- grad_path_table: float32 [64, 32], P('section')
- grad_edge_table: float32 [32, 32], P('section')
The draws below stay inside these ranges and needn't reach their ends.
Inputs may be any that keep to these rules, and one draw needn't show every extreme that they name: `conformer_group`: values index the molecules of the same index of dp: each of its 2 molecules has exactly 2 conformers there. `atom_counts`: every index of dp holds a molecule with 128 atoms.
All inputs are finite; a program needn't handle non-finite values.
Results may differ from the reference program's by a relative error of at most 0.02.
Values may be sent and summed in bfloat16 or wider, within the bound.
A program may use at most 256 MiB of HBM per device.

```python
import math
import jax
import jax.numpy as jnp
from jax import lax

HEADS = 32
FF = 768
KERN = 128
SPD = 64
EDGES = 32
ATOMS = 128
SEQ_MB = 2
D = 768
LAYERS = 4
SEQ_DEV = 4
MOLS_DEV = 2
SEQS = 32
MOLS = 16
TOKENS = 4096


def draw_conformer_group(key, part):
    blocks = SEQS // SEQ_DEV
    keys = jax.random.split(key, blocks)
    base = jnp.arange(SEQ_DEV, dtype=jnp.int32) % MOLS_DEV
    shuffled = jax.vmap(lambda one_key: jax.random.permutation(one_key, base))(keys)
    return shuffled.reshape(SEQS).astype(jnp.int32)


def draw_atom_counts(key, part):
    blocks = MOLS // MOLS_DEV
    first_key, second_key = jax.random.split(key)
    drawn = jax.random.randint(first_key, (blocks, MOLS_DEV), ATOMS // 4, ATOMS + 1, dtype=jnp.int32)
    where_full = jax.random.randint(second_key, (blocks, 1), 0, MOLS_DEV, dtype=jnp.int32)
    slots = jnp.arange(MOLS_DEV, dtype=jnp.int32)[None, :]
    drawn = jnp.where(slots == where_full, ATOMS, drawn)
    return drawn.reshape(MOLS).astype(jnp.int32)


def with_ends(values, own_key, smallest, largest):
    longest = values.shape.index(max(values.shape))
    spots = []
    for shift in (0, 1):
        where = [jax.random.randint(jax.random.fold_in(own_key, axis), (), 0, length) for axis, length in enumerate(values.shape)]
        where[longest] = (where[longest] + shift) % values.shape[longest]
        spots.append(tuple(where))
    return values.at[spots[0]].set(smallest).at[spots[1]].set(largest)


def levels(key, dims, cuts, least, high):
    def one(dim, blocks):
        draws = jax.random.uniform(jax.random.fold_in(jax.random.fold_in(key, 6), dim), (blocks,), jnp.float32, least / len(cuts), high / len(cuts))
        return jnp.repeat(jnp.exp(draws), dims[dim] // blocks).reshape((-1,) + (1,) * (len(dims) - dim - 1))

    level = one(*cuts[0])
    for cut in cuts[1:]:
        level = level * one(*cut)
    return level


def normal_values(key, extent, spread, most, shards=(), held_as=jnp.bfloat16):
    loudness = levels(key, extent, shards, -0.22, 0.18) if shards else 1.0
    result = jax.random.normal(key, extent, jnp.float32) * spread * loudness
    return jnp.minimum(jnp.maximum(result, -most), most).astype(held_as)


def setup_inputs(seed: int = 0) -> dict:
    arg_keys = jax.random.split(jax.random.key(seed), 17)
    return {
        "tokens": normal_values(arg_keys[0], (TOKENS, D), 1.0, 6.0, ((0, 8),)),
        "cotangent": normal_values(arg_keys[1], (LAYERS, TOKENS, D), 1.0, 6.0, ((0, 4), (1, 8))),
        "positions": normal_values(arg_keys[2], (SEQS, 3, ATOMS), 1.5, 6.0, ((0, 8),), jnp.float32),
        "conformer_group": draw_conformer_group(jax.random.fold_in(arg_keys[16], 71), 0),
        "atom_counts": draw_atom_counts(jax.random.fold_in(arg_keys[16], 71), 0),
        "path_dist": with_ends(jax.random.randint(arg_keys[5], (MOLS, ATOMS, ATOMS), 0, SPD), jax.random.fold_in(arg_keys[5], 1), 0, SPD - 1).astype(jnp.int32),
        "edge_kind": with_ends(jax.random.randint(arg_keys[6], (MOLS, ATOMS, ATOMS), 0, EDGES), jax.random.fold_in(arg_keys[6], 1), 0, EDGES - 1).astype(jnp.int32),
        "attn_in": normal_values(arg_keys[7], (LAYERS, D, 3 * D), D ** -0.5, 0.21875, ((0, 4),)),
        "attn_out": normal_values(arg_keys[8], (LAYERS, D, D), (D // 8) ** -0.5, 0.625, ((0, 4),)),
        "ffn_up": normal_values(arg_keys[9], (LAYERS, D, FF), D ** -0.5, 0.21875, ((0, 4),)),
        "ffn_down": normal_values(arg_keys[10], (LAYERS, FF, D), FF ** -0.5, 0.21875, ((0, 4),)),
        "norm_gain": jnp.clip(1.0 + 0.15 * jax.random.normal(arg_keys[11], (LAYERS, D, 2), jnp.float32), 0.25, 1.75).astype(jnp.bfloat16),
        "norm_shift": normal_values(arg_keys[12], (LAYERS, D, 2), 0.3, 2.0, ((0, 4),)),
        "kernel_proj": normal_values(arg_keys[13], (KERN, HEADS), (KERN // 8) ** -0.5, 1.5),
        "path_table": normal_values(arg_keys[14], (SPD, HEADS), 0.5, 3.0),
        "edge_table": normal_values(arg_keys[15], (EDGES, HEADS), 0.5, 3.0),
    }


HIGH = lax.Precision.HIGHEST
EPS = 1e-05
NEG_BIG = -1e+30
KERN_SPAN = 8.0
KERN_WIDTH = 0.4

@jax.custom_vjp
def low(v):
    return lax.optimization_barrier(v.astype(jnp.bfloat16)).astype(jnp.float32)

@jax.custom_vjp
def low_back(v):
    return v

def low_keep(v):
    return (low(v), None)

def low_pass(kept, grad):
    return (grad,)

def back_keep(v):
    return (v, None)

def back_low(kept, grad):
    return (low(grad),)
low.defvjp(low_keep, low_pass)
low_back.defvjp(back_keep, back_low)

def gelu_tanh(values):
    return 0.5 * values * (1.0 + jnp.tanh(0.7978845608028654 * (values + 0.044715 * values * values * values)))

def kernels(positions, kernel_count):
    diffs = positions[:, :, :, None] - positions[:, :, None, :]
    dist = jnp.sqrt(lax.optimization_barrier(jnp.sum(diffs * diffs, axis=1)))
    centers = jnp.arange(kernel_count, dtype=jnp.float32) * (KERN_SPAN / kernel_count)
    scaled = (dist[:, None, :, :] - centers[None, :, None, None]) / KERN_WIDTH
    return jnp.exp(-0.5 * scaled * scaled)

def norm_fwd(values, gain, shift):
    center = values - lax.optimization_barrier(jnp.mean(values, axis=-1, keepdims=True))
    inv_std = lax.rsqrt(lax.optimization_barrier(jnp.mean(center * center, axis=-1, keepdims=True)) + EPS)
    return center * inv_std * gain + shift

def pair_bias(positions, path_blk, edge_blk, tables):
    kernel_proj, path_table, edge_table = tables
    feats = low(kernels(positions, kernel_proj.shape[0]))
    table_bias = jnp.transpose(path_table[path_blk] + edge_table[edge_blk], (0, 3, 1, 2))
    return low(jnp.einsum('kh,skij->shij', kernel_proj, feats, precision=HIGH) + table_bias)

def block_layer(layer_in, weights, bias, count_blk):
    attn_in, attn_out, ffn_up, ffn_down, gains, shifts = weights
    seq_count, heads, atom_slots = (bias.shape[0], bias.shape[1], bias.shape[2])
    width = attn_out.shape[0]
    head_dim = width // heads
    scale = 1.0 / math.sqrt(head_dim)
    shape_four = (seq_count, atom_slots, heads, head_dim)
    normed = low(norm_fwd(layer_in, gains[:, 0], shifts[:, 0]))
    qkv_all = low(low_back(jnp.dot(normed, attn_in, precision=HIGH)))
    queries = qkv_all[:, :width].reshape(shape_four)
    keys_all = qkv_all[:, width:2 * width].reshape(shape_four)
    values_all = qkv_all[:, 2 * width:].reshape(shape_four)
    scores = low_back(jnp.einsum('sihe,sjhe->shij', queries, keys_all, precision=HIGH) * scale + bias)
    key_live = jnp.arange(atom_slots, dtype=jnp.int32)[None, :] < count_blk[:, None]
    scores = jnp.where(key_live[:, None, None, :], scores, NEG_BIG)
    probs = low(jax.nn.softmax(scores, axis=-1))
    attended = jnp.einsum('shij,sjhe->sihe', probs, values_all, precision=HIGH)
    attended = low(low_back(attended.reshape(seq_count * atom_slots, width)))
    middle = layer_in + low_back(jnp.dot(attended, attn_out, precision=HIGH))
    normed_two = low(norm_fwd(middle, gains[:, 1], shifts[:, 1]))
    upper = low_back(jnp.dot(normed_two, ffn_up, precision=HIGH))
    return middle + low_back(jnp.dot(low(gelu_tanh(upper)), ffn_down, precision=HIGH))

def reference(tokens, cotangent, positions, conformer_group, atom_counts, path_dist, edge_kind, attn_in, attn_out, ffn_up, ffn_down, norm_gain, norm_shift, kernel_proj, path_table, edge_table):
    blocks = SEQS // SEQ_MB
    block_rows = SEQ_MB * ATOMS
    owner_idx = jnp.arange(SEQS, dtype=jnp.int32) // SEQ_DEV * MOLS_DEV + conformer_group.astype(jnp.int32)
    path_seq = path_dist[owner_idx].reshape(blocks, SEQ_MB, ATOMS, ATOMS)
    edge_seq = edge_kind[owner_idx].reshape(blocks, SEQ_MB, ATOMS, ATOMS)
    count_seq = atom_counts[owner_idx].reshape(blocks, SEQ_MB)
    coord_seq = positions.astype(jnp.float32).reshape(blocks, SEQ_MB, 3, ATOMS)
    token_blocks = tokens.astype(jnp.float32).reshape(blocks, block_rows, D)
    layer_weights = tuple((arr.astype(jnp.float32) for arr in (attn_in, attn_out, ffn_up, ffn_down, norm_gain, norm_shift)))
    table_weights = tuple((arr.astype(jnp.float32) for arr in (kernel_proj, path_table, edge_table)))
    probes = jnp.zeros((blocks, LAYERS, block_rows, D), jnp.float32)

    def forward(probe_all, weight_all, table_all):

        def one_block(pieces):
            token_blk, probe_blk, coord_blk, path_blk, edge_blk, count_blk = pieces
            bias = pair_bias(coord_blk, path_blk, edge_blk, table_all)
            carried = token_blk
            layer_outs = []
            for layer_num in range(LAYERS):
                layer_in = low_back(carried + probe_blk[layer_num])
                one_weights = tuple((arr[layer_num] for arr in weight_all))
                carried = low(block_layer(layer_in, one_weights, bias, count_blk))
                layer_outs.append(carried)
            return jnp.stack(layer_outs)
        return lax.map(jax.checkpoint(one_block), (token_blocks, probe_all, coord_seq, path_seq, edge_seq, count_seq))
    hidden_blocks, pullback = jax.vjp(forward, probes, layer_weights, table_weights)
    cot_blocks = cotangent.astype(jnp.float32).reshape(LAYERS, blocks, block_rows, D).transpose(1, 0, 2, 3)
    probe_grad, weight_grads, table_grads = pullback(cot_blocks)
    hidden = hidden_blocks.transpose(1, 0, 2, 3).reshape(LAYERS, SEQS * ATOMS, D).astype(jnp.bfloat16)
    input_grads = probe_grad.transpose(1, 0, 2, 3).reshape(LAYERS, SEQS * ATOMS, D).astype(jnp.bfloat16)
    return (hidden, input_grads, weight_grads[0], weight_grads[1], weight_grads[2], weight_grads[3], weight_grads[4], weight_grads[5], table_grads[0], table_grads[1], table_grads[2])
```

```python
import math

import jax
import jax.numpy as jnp
from jax import lax
from jax.sharding import PartitionSpec as P

MICRO = 2
SEQ_MB = 2


EPS = 1e-05
NEG_BIG = -1e30
KERN_SPAN = 8.0
KERN_WIDTH = 0.4
HIGH = lax.Precision.HIGHEST


def shifted(value, axis, steps):
    count = lax.axis_size(axis)
    first, last = (max(0, -steps), min(count, count - steps))
    return lax.ppermute(value, axis, [(source, source + steps) for source in range(first, last)])


def of_molecule(per_mol, group):
    picked = jnp.broadcast_to(per_mol[:1], group.shape + per_mol.shape[1:])
    for mol in range(1, per_mol.shape[0]):
        hit = (group == mol).reshape((-1,) + (1,) * (per_mol.ndim - 1))
        picked = jnp.where(hit, per_mol[mol : mol + 1], picked)
    return picked


def gelu_tanh(values):
    return (
        0.5
        * values
        * (1.0 + jnp.tanh(0.7978845608028654 * (values + 0.044715 * values * values * values)))
    )


def kernels(positions, kernel_count):
    diffs = positions[:, :, :, None] - positions[:, :, None, :]
    dist = jnp.sqrt(jnp.sum(diffs * diffs, axis=1))
    centers = jnp.arange(kernel_count, dtype=jnp.float32) * (KERN_SPAN / kernel_count)
    scaled = (dist[:, None, :, :] - centers[None, :, None, None]) / KERN_WIDTH
    return jnp.exp(-0.5 * scaled * scaled)


def norm_fwd(values, gain, shift):
    center = values - jnp.mean(values, axis=-1, keepdims=True)
    inv_std = lax.rsqrt(jnp.mean(center * center, axis=-1, keepdims=True) + EPS)
    normal_x = center * inv_std
    return (normal_x * gain + shift, normal_x, inv_std)


def norm_back(grad_out, normal_x, inv_std, gain):
    scaled = grad_out * gain
    grad_in = inv_std * (
        scaled
        - jnp.mean(scaled, axis=-1, keepdims=True)
        - normal_x * jnp.mean(scaled * normal_x, axis=-1, keepdims=True)
    )
    return (grad_in, jnp.sum(grad_out * normal_x, axis=0), jnp.sum(grad_out, axis=0))


def left_dot(first, second):
    return lax.dot_general(
        first, second, (((0,), (0,)), ((), ())), preferred_element_type=jnp.float32
    )


def right_dot(first, second):
    return lax.dot_general(
        first, second, (((1,), (1,)), ((), ())), preferred_element_type=jnp.float32
    )


def make_bias(micro_data, tables):
    positions, path_blk, edge_blk, count_blk = micro_data
    kernel_proj, path_table, edge_table = tables
    feats_low = kernels(positions, kernel_proj.shape[0]).astype(jnp.bfloat16)
    bias = jnp.einsum("kh,skij->shij", kernel_proj, feats_low, preferred_element_type=jnp.float32)
    looked = jnp.take(path_table.astype(jnp.float32), path_blk, axis=0) + jnp.take(
        edge_table.astype(jnp.float32), edge_blk, axis=0
    )
    bias = bias + jnp.transpose(looked, (0, 3, 1, 2))
    return bias.astype(jnp.bfloat16)


def table_grads(grad_bias, micro_data, tables):
    positions, path_blk, edge_blk, count_blk = micro_data
    kernel_proj, path_table, edge_table = tables
    heads = kernel_proj.shape[1]
    feats_wide = kernels(positions, kernel_proj.shape[0]).astype(jnp.bfloat16).astype(jnp.float32)
    grad_kernel = jnp.einsum("shij,skij->kh", grad_bias, feats_wide, precision=HIGH)
    pair_rows = jnp.transpose(grad_bias, (0, 2, 3, 1)).reshape(-1, heads)
    grad_path = jax.ops.segment_sum(
        pair_rows, path_blk.reshape(-1), num_segments=path_table.shape[0]
    )
    grad_edge = jax.ops.segment_sum(
        pair_rows, edge_blk.reshape(-1), num_segments=edge_table.shape[0]
    )
    return (grad_kernel, grad_path, grad_edge)


def layer_forward(layer_in, params, bias_low, count_blk):
    attn_in, attn_out, ffn_up, ffn_down, norm_gain, norm_shift = params
    seq_count, heads, atom_slots = (bias_low.shape[0], bias_low.shape[1], bias_low.shape[2])
    width = attn_out.shape[0]
    head_dim = width // heads
    scale = 1.0 / math.sqrt(head_dim)
    shape_four = (seq_count, atom_slots, heads, head_dim)
    gains = norm_gain.astype(jnp.float32)
    shifts = norm_shift.astype(jnp.float32)
    in_wide = layer_in.astype(jnp.float32)
    normed, normal_one, inv_one = norm_fwd(in_wide, gains[:, 0], shifts[:, 0])
    normed_low = normed.astype(jnp.bfloat16)
    qkv_low = jnp.dot(normed_low, attn_in, preferred_element_type=jnp.float32).astype(jnp.bfloat16)
    queries = qkv_low[:, :width].reshape(shape_four)
    keys_all = qkv_low[:, width : 2 * width].reshape(shape_four)
    values_all = qkv_low[:, 2 * width :].reshape(shape_four)
    scores = (
        jnp.einsum("sihe,sjhe->shij", queries, keys_all, preferred_element_type=jnp.float32) * scale
    )
    scores = scores + bias_low.astype(jnp.float32)
    key_live = jnp.arange(atom_slots, dtype=jnp.int32)[None, :] < count_blk[:, None]
    scores = jnp.where(key_live[:, None, None, :], scores, NEG_BIG)
    probs = jax.nn.softmax(scores, axis=-1)
    probs_low = probs.astype(jnp.bfloat16)
    attended = jnp.einsum(
        "shij,sjhe->sihe", probs_low, values_all, preferred_element_type=jnp.float32
    )
    attended_low = attended.reshape(seq_count * atom_slots, width).astype(jnp.bfloat16)
    middle = in_wide + jnp.dot(attended_low, attn_out, preferred_element_type=jnp.float32)
    normed_two, normal_two, inv_two = norm_fwd(middle, gains[:, 1], shifts[:, 1])
    normed_two_low = normed_two.astype(jnp.bfloat16)
    upper = jnp.dot(normed_two_low, ffn_up, preferred_element_type=jnp.float32)
    act_low = gelu_tanh(upper).astype(jnp.bfloat16)
    layer_out = middle + jnp.dot(act_low, ffn_down, preferred_element_type=jnp.float32)
    saved = (
        normed_low,
        normal_one,
        inv_one,
        queries,
        keys_all,
        values_all,
        probs,
        probs_low,
        attended_low,
        normal_two,
        inv_two,
        normed_two_low,
        upper,
        act_low,
    )
    return (layer_out.astype(jnp.bfloat16), saved)


def ffn_back(grad_out, saved, params):
    attn_in, attn_out, ffn_up, ffn_down, norm_gain, norm_shift = params
    (
        normed_low,
        normal_one,
        inv_one,
        queries,
        keys_all,
        values_all,
        probs,
        probs_low,
        attended_low,
        normal_two,
        inv_two,
        normed_two_low,
        upper,
        act_low,
    ) = saved
    gains = norm_gain.astype(jnp.float32)
    grad_low = grad_out.astype(jnp.bfloat16)
    grad_down = left_dot(act_low, grad_low)
    grad_act = right_dot(grad_low, ffn_down)
    grad_upper = jax.vjp(gelu_tanh, upper)[1](grad_act)[0].astype(jnp.bfloat16)
    grad_up = left_dot(normed_two_low, grad_upper)
    grad_normed_two = right_dot(grad_upper, ffn_up)
    back_two, gain_two, shift_two = norm_back(grad_normed_two, normal_two, inv_two, gains[:, 1])
    return (grad_out + back_two, grad_up, grad_down, gain_two, shift_two)


def attn_back(grad_middle, saved, params):
    attn_in, attn_out, ffn_up, ffn_down, norm_gain, norm_shift = params
    (
        normed_low,
        normal_one,
        inv_one,
        queries,
        keys_all,
        values_all,
        probs,
        probs_low,
        attended_low,
        normal_two,
        inv_two,
        normed_two_low,
        upper,
        act_low,
    ) = saved
    seq_count, atom_slots, heads, head_dim = queries.shape
    width = heads * head_dim
    all_rows = seq_count * atom_slots
    scale = 1.0 / math.sqrt(head_dim)
    gains = norm_gain.astype(jnp.float32)
    middle_low = grad_middle.astype(jnp.bfloat16)
    grad_out_proj = left_dot(attended_low, middle_low)
    grad_attended = right_dot(middle_low, attn_out).astype(jnp.bfloat16).reshape(queries.shape)
    grad_probs = jnp.einsum(
        "sihe,sjhe->shij", grad_attended, values_all, preferred_element_type=jnp.float32
    )
    grad_values = jnp.einsum(
        "shij,sihe->sjhe", probs_low, grad_attended, preferred_element_type=jnp.float32
    )
    grad_scores = probs * (grad_probs - jnp.sum(probs * grad_probs, axis=-1, keepdims=True))
    scores_low = grad_scores.astype(jnp.bfloat16)
    grad_queries = (
        jnp.einsum("shij,sjhe->sihe", scores_low, keys_all, preferred_element_type=jnp.float32)
        * scale
    )
    grad_keys = (
        jnp.einsum("shij,sihe->sjhe", scores_low, queries, preferred_element_type=jnp.float32)
        * scale
    )
    grad_qkv = jnp.concatenate(
        [
            grad_queries.reshape(all_rows, width),
            grad_keys.reshape(all_rows, width),
            grad_values.reshape(all_rows, width),
        ],
        axis=1,
    ).astype(jnp.bfloat16)
    grad_in_proj = left_dot(normed_low, grad_qkv)
    grad_normed = right_dot(grad_qkv, attn_in)
    back_one, gain_one, shift_one = norm_back(grad_normed, normal_one, inv_one, gains[:, 0])
    grad_layer_in = (grad_middle + back_one).astype(jnp.bfloat16)
    return (grad_layer_in, grad_in_proj, grad_out_proj, gain_one, shift_one, scores_low)


def pick_micro(stored, micro_idx):
    return lax.dynamic_index_in_dim(stored, micro_idx, 0, keepdims=False)


def keep_micro(stored, value, micro_idx, live):
    kept = jnp.where(live, value, pick_micro(stored, micro_idx))
    return lax.dynamic_update_index_in_dim(stored, kept, micro_idx, 0)


def on_device(
    tokens,
    cotangent,
    positions,
    conformer_group,
    atom_counts,
    path_dist,
    edge_kind,
    attn_in,
    attn_out,
    ffn_up,
    ffn_down,
    norm_gain,
    norm_shift,
    kernel_proj,
    path_table,
    edge_table,
):
    sections = lax.axis_size("section")
    section_num = lax.axis_index("section")
    params = (attn_in[0], attn_out[0], ffn_up[0], ffn_down[0], norm_gain[0], norm_shift[0])
    tables = (kernel_proj, path_table, edge_table)
    atom_slots = positions.shape[2]
    width = attn_out.shape[1]
    heads = kernel_proj.shape[1]
    micro_rows = SEQ_MB * atom_slots
    ticks = MICRO + sections - 1
    path_seq = of_molecule(path_dist, conformer_group)
    edge_seq = of_molecule(edge_kind, conformer_group)
    count_seq = of_molecule(atom_counts, conformer_group)
    cot_micro = cotangent[0].reshape(MICRO, micro_rows, width)
    bias_shape = (SEQ_MB, heads, atom_slots, atom_slots)

    def micro_slice(micro_idx):
        seq_start = micro_idx * SEQ_MB
        return tuple(
            (
                lax.dynamic_slice_in_dim(arr, seq_start, SEQ_MB, 0)
                for arr in (positions, path_seq, edge_seq, count_seq)
            )
        )

    incoming = jnp.zeros((micro_rows, width), jnp.bfloat16)
    bias_incoming = jnp.zeros(bias_shape, jnp.bfloat16)
    bias_store = jnp.zeros((MICRO,) + bias_shape, jnp.bfloat16)
    input_store = jnp.zeros((MICRO, micro_rows, width), jnp.bfloat16)
    output_store = jnp.zeros((MICRO, micro_rows, width), jnp.bfloat16)
    for tick_num in range(ticks):
        micro_num = tick_num - section_num
        live = (micro_num >= 0) & (micro_num < MICRO)
        micro_idx = jnp.clip(micro_num, 0, MICRO - 1)
        if tick_num < MICRO:
            first_in = tokens[tick_num * micro_rows : (tick_num + 1) * micro_rows]
        else:
            first_in = jnp.zeros((micro_rows, width), jnp.bfloat16)
        layer_in = jnp.where(section_num == 0, first_in, incoming)
        micro_data = micro_slice(micro_idx)
        bias_used = lax.cond(
            section_num == 0, lambda: make_bias(micro_data, tables), lambda: bias_incoming
        )
        layer_out = lax.cond(
            live,
            lambda: layer_forward(layer_in, params, bias_used, micro_data[3])[0],
            lambda: jnp.zeros((micro_rows, width), jnp.bfloat16),
        )
        bias_store = keep_micro(bias_store, bias_used, micro_idx, live)
        if tick_num < ticks - 1:
            incoming, bias_incoming = shifted((layer_out, bias_used), "section", 1)
        input_store = keep_micro(input_store, layer_in, micro_idx, live)
        output_store = keep_micro(output_store, layer_out, micro_idx, live)
    grad_incoming = jnp.zeros((micro_rows, width), jnp.bfloat16)
    bias_grad_in = jnp.zeros(bias_shape, jnp.float32)
    grad_store = jnp.zeros((MICRO, micro_rows, width), jnp.bfloat16)
    totals = tuple((jnp.zeros(arr.shape, jnp.float32) for arr in params[:4])) + tuple(
        (jnp.zeros((width,), jnp.float32) for unused in range(4))
    )
    table_tot = tuple((jnp.zeros(arr.shape, jnp.float32) for arr in tables))
    for tick_num in range(ticks):
        micro_num = tick_num - (sections - 1 - section_num)
        live = (micro_num >= 0) & (micro_num < MICRO)
        micro_idx = jnp.clip(micro_num, 0, MICRO - 1)
        grad_total = pick_micro(cot_micro, micro_idx).astype(jnp.float32) + grad_incoming.astype(
            jnp.float32
        )
        layer_in = pick_micro(input_store, micro_idx)
        micro_data = micro_slice(micro_idx)
        kept_bias = pick_micro(bias_store, micro_idx)
        grad_from_later = bias_grad_in

        def ffn_section():
            saved = layer_forward(layer_in, params, kept_bias, micro_data[3])[1]
            return (saved, ffn_back(grad_total, saved, params))

        def add_ffn(tot, ffn_part):
            grad_middle, grad_up, grad_down, gain_two, shift_two = ffn_part
            return (
                tot[0],
                tot[1],
                tot[2] + grad_up,
                tot[3] + grad_down,
                tot[4],
                tot[5] + gain_two,
                tot[6],
                tot[7] + shift_two,
            )

        def attn_step(tot, tabs, saved, grad_middle):
            grad_in, grad_in_proj, grad_out_proj, gain_one, shift_one, scores_low = attn_back(
                grad_middle, saved, params
            )
            tot = (
                tot[0] + grad_in_proj,
                tot[1] + grad_out_proj,
                tot[2],
                tot[3],
                tot[4] + gain_one,
                tot[5],
                tot[6] + shift_one,
                tot[7],
            )
            bias_send = scores_low.astype(jnp.float32) + grad_from_later

            def table_add(old_tabs):
                parts = table_grads(bias_send, micro_data, tables)
                return tuple((old + new for old, new in zip(old_tabs, parts)))

            tabs = lax.cond(section_num == 0, table_add, lambda old_tabs: old_tabs, tabs)
            return (tot, tabs, grad_in, bias_send)

        def spare_step(tot, tabs):
            return (
                tot,
                tabs,
                jnp.zeros((micro_rows, width), jnp.bfloat16),
                jnp.zeros(bias_shape, jnp.float32),
            )

        def full_step(tot, tabs):
            saved, ffn_part = ffn_section()
            return attn_step(add_ffn(tot, ffn_part), tabs, saved, ffn_part[0])

        totals, table_tot, grad_in, bias_send = lax.cond(
            live, full_step, spare_step, totals, table_tot
        )
        grad_store = keep_micro(grad_store, grad_in, micro_idx, live)
        if tick_num < ticks - 1:
            grad_incoming, bias_grad_in = (
                shifted(grad_in, "section", -1),
                shifted(bias_send.astype(jnp.bfloat16), "section", -1).astype(bias_send.dtype),
            )
    total_in, total_out, total_up, total_down, gain_one_t, gain_two_t, shift_one_t, shift_two_t = (
        totals
    )
    gain_tot = jnp.stack([gain_one_t, gain_two_t], axis=1)
    shift_tot = jnp.stack([shift_one_t, shift_two_t], axis=1)
    sums_all = (
        lax.psum_scatter(total_in, "dp", scatter_dimension=0, tiled=True),
        lax.psum_scatter(total_out, "dp", scatter_dimension=0, tiled=True),
        lax.psum_scatter(total_up, "dp", scatter_dimension=0, tiled=True),
        lax.psum_scatter(total_down, "dp", scatter_dimension=0, tiled=True),
        lax.psum_scatter(gain_tot, "dp", scatter_dimension=0, tiled=True),
        lax.psum_scatter(shift_tot, "dp", scatter_dimension=0, tiled=True),
    )
    sum_in, sum_out, sum_up, sum_down, sum_gain, sum_shift = sums_all
    molecule_sums = lax.psum((table_tot[0], table_tot[1], table_tot[2]), "dp")
    table_sums = (
        lax.psum_scatter(molecule_sums[0], "section", scatter_dimension=0, tiled=True),
        lax.psum_scatter(molecule_sums[1], "section", scatter_dimension=0, tiled=True),
        lax.psum_scatter(molecule_sums[2], "section", scatter_dimension=0, tiled=True),
    )
    hidden = output_store.reshape(1, MICRO * micro_rows, width)
    input_grads = grad_store.reshape(1, MICRO * micro_rows, width)
    return (
        hidden,
        input_grads,
        sum_in[None],
        sum_out[None],
        sum_up[None],
        sum_down[None],
        sum_gain[None],
        sum_shift[None],
        table_sums[0],
        table_sums[1],
        table_sums[2],
    )


def solution(mesh):
    in_specs = (
        P("dp", None),
        P("section", "dp", None),
        P("dp", None, None),
        P("dp"),
        P("dp"),
        P("dp", None, None),
        P("dp", None, None),
        P("section", None, None),
        P("section", None, None),
        P("section", None, None),
        P("section", None, None),
        P("section", None, None),
        P("section", None, None),
        P(),
        P(),
        P(),
    )
    out_specs = (
        P("section", "dp", None),
        P("section", "dp", None),
        P("section", "dp", None),
        P("section", "dp", None),
        P("section", "dp", None),
        P("section", "dp", None),
        P("section", "dp", None),
        P("section", "dp", None),
        P("section", None),
        P("section", None),
        P("section", None),
    )
    return jax.shard_map(
        on_device, mesh=mesh, in_specs=in_specs, out_specs=out_specs, check_vma=False
    )
```

```python
import functools
import math

import jax
import jax.numpy as jnp
from jax import lax
from jax.experimental import pallas as pl
from jax.experimental.pallas import tpu as pltpu
from jax.sharding import PartitionSpec as P

F32, BF16 = jnp.float32, jnp.bfloat16
MESH = pl.DeviceIdType.MESH
EPS = 1e-05
NEG_BIG = -1e30
KERN_SPAN = 8.0
KERN_WIDTH = 0.4
LOG2E = math.log2(math.e)
LANES = 128
DEPTH = 256


def dot(a, b):
    return jnp.dot(a, b, preferred_element_type=F32)


def dot_nt(a, b):
    return lax.dot_general(a, b, (((1,), (1,)), ((), ())), preferred_element_type=F32)


def rows_of(ref, m, n):
    return ref.at[pl.ds(pl.multiple_of(m * n, n), n), :]


def norm_parts(values):
    center = values - jnp.mean(values, axis=-1, keepdims=True)
    inv_std = lax.rsqrt(jnp.mean(center * center, axis=-1, keepdims=True) + EPS)
    return center * inv_std, inv_std


def norm_back(dy, xh, inv_std, gain):
    dxh = dy * gain
    return inv_std * (
        dxh
        - jnp.mean(dxh, axis=-1, keepdims=True)
        - xh * jnp.mean(dxh * xh, axis=-1, keepdims=True)
    )


def gelu(u):
    return 0.5 * u * (1.0 + jnp.tanh(0.7978845608028654 * (u + 0.044715 * u * u * u)))


def gelu_slope(u):
    sq = u * u
    t = jnp.tanh(0.7978845608028654 * (u + 0.044715 * sq * u))
    return 0.5 * (1.0 + t) + 0.5 * u * (1.0 - t * t) * (
        0.7978845608028654 * (1.0 + 3 * 0.044715 * sq)
    )


def pair_windows(head_dim):
    out = []
    for pair in range(8):
        lo, hi = pair * 2 * head_dim, pair * 2 * head_dim + 2 * head_dim - 1
        first = lo // LANES
        out.append((first, hi // LANES - first + 1, lo - first * LANES))
    return out


def both_heads(block, off, head_dim):
    lane = lax.broadcasted_iota(jnp.int32, (1, block.shape[1]), 1)
    one = ((lane >= off) & (lane < off + head_dim)).astype(F32).astype(BF16)
    two = ((lane >= off + head_dim) & (lane < off + 2 * head_dim)).astype(F32).astype(BF16)
    return jnp.concatenate([block * one, block * two], axis=0)


def features(dist8, path8, edge8, row, spd, edges, kern):
    atoms = dist8.shape[1]
    alpha = math.sqrt(0.5 * LOG2E) / KERN_WIDTH
    center = lax.broadcasted_iota(jnp.int32, (kern, atoms), 0).astype(F32) * (
        KERN_SPAN / kern * alpha
    )
    t = dist8[row : row + 1, :] * alpha - center
    gauss = jnp.exp2(-(t * t))
    path_id = lax.broadcasted_iota(jnp.int32, (spd, atoms), 0).astype(F32)
    edge_id = lax.broadcasted_iota(jnp.int32, (edges, atoms), 0).astype(F32)
    path = jnp.where(path8[row : row + 1, :] == path_id, 1.0, 0.0)
    edge = jnp.where(edge8[row : row + 1, :] == edge_id, 1.0, 0.0)
    rest = jnp.zeros((DEPTH - kern - spd - edges, atoms), F32)
    return jnp.concatenate([gauss, path, edge, rest], axis=0).astype(BF16)


def body(
    sections, micro, atoms, heads, kern, spd, edges,
    group, counts, tokens, cot, posn, path_in, edge_in, win, wout, wup, wdown, norms, tab,
    hidden, igrad, g_in, g_out, g_up, g_down, g_norm, g_tab,
    xs, grecv, a_s, qkv_s, o_s, mid_s, c_s, u_s, act_s, df_s, du_s, dat_s, dqkv_s,
    pairs, probs, dist_s, path_s, edge_s, tr_b, tr_f, dk_s, dv_s, left_s,
    fsend, frecv, bsend, brecv,
):
    width = wout.shape[0]
    head_dim = width // heads
    scale = 1.0 / math.sqrt(head_dim)
    windows = pair_windows(head_dim)
    s = lax.axis_index("section") if sections > 1 else 0
    d = lax.axis_index("dp") if sections > 1 else 0
    last = s == sections - 1

    if sections > 1:
        barrier = pltpu.get_barrier_semaphore()

        @pl.when(s > 0)
        def _():
            pl.semaphore_signal(barrier, inc=1, device_id=(s - 1, d), device_id_type=MESH)

        @pl.when(s < sections - 1)
        def _():
            pl.semaphore_signal(barrier, inc=1, device_id=(s + 1, d), device_id_type=MESH)

        pl.semaphore_wait(barrier, jnp.where((s > 0) & (s < sections - 1), 2, 1))

    def forward_copy(m):
        return pltpu.make_async_remote_copy(
            src_ref=rows_of(hidden, m, atoms), dst_ref=rows_of(xs, m, atoms),
            send_sem=fsend.at[m], recv_sem=frecv.at[m],
            device_id=(jnp.minimum(s + 1, sections - 1), d), device_id_type=MESH,
        )

    def backward_copy(m):
        return pltpu.make_async_remote_copy(
            src_ref=rows_of(igrad, m, atoms), dst_ref=rows_of(grecv, m, atoms),
            send_sem=bsend.at[m], recv_sem=brecv.at[m],
            device_id=(jnp.maximum(s - 1, 0), d), device_id_type=MESH,
        )

    @pl.when(s == 0)
    def _():
        xs[...] = tokens[...]

    @pl.when(last)
    def _():
        grecv[...] = jnp.zeros_like(grecv)

    g_norm[...] = jnp.zeros_like(g_norm)
    g_tab[...] = jnp.zeros_like(g_tab)

    def make_bias(m):
        mol = group[m]
        count = counts[mol]
        pos = posn[m]
        pos_t = jnp.transpose(jnp.concatenate([pos, jnp.zeros((5, atoms), F32)], axis=0))
        total = jnp.zeros((atoms, atoms), F32)
        for axis in range(3):
            diff = pos_t[:, axis : axis + 1] - pos[axis : axis + 1, :]
            total = total + diff * diff
        dist_s[m] = jnp.sqrt(total)
        path_s[m] = jnp.transpose(path_in[mol].astype(F32))
        edge_s[m] = jnp.transpose(edge_in[mol].astype(F32))
        out_ref = pairs.at[m]

        @pl.loop(0, atoms // 8)
        def _(t):
            eight = pl.ds(pl.multiple_of(t * 8, 8), 8)
            d8, p8, e8 = dist_s[m, eight, :], path_s[m, eight, :], edge_s[m, eight, :]
            for r in range(0, 8, 2):
                feats = jnp.concatenate(
                    [features(d8, p8, e8, r + q, spd, edges, kern) for q in range(2)], axis=1
                )
                got = dot(tab[...], feats) * LOG2E
                for q in range(2):
                    j = t * 8 + r + q
                    row = jnp.where(j < count, got[:, q * atoms : (q + 1) * atoms], NEG_BIG)
                    out_ref[pl.ds(j, heads, stride=atoms), :] = row

    def table_grads(m):
        in_ref = pairs.at[m]

        def step(t, acc):
            eight = pl.ds(pl.multiple_of(t * 8, 8), 8)
            d8, p8, e8 = dist_s[m, eight, :], path_s[m, eight, :], edge_s[m, eight, :]
            for r in range(0, 8, 2):
                feats = jnp.concatenate(
                    [features(d8, p8, e8, r + q, spd, edges, kern) for q in range(2)], axis=1
                )
                halves = []
                for q in range(2):
                    j = t * 8 + r + q
                    halves.append(in_ref[pl.ds(j, heads, stride=atoms), :])
                ds = jnp.concatenate(halves, axis=1).astype(BF16)
                acc = acc + dot_nt(feats, ds)
            return acc

        g_tab[...] += lax.fori_loop(0, atoms // 8, step, jnp.zeros((DEPTH, heads), F32))

    def forward(m):
        x = rows_of(xs, m, atoms)[...].astype(F32)
        xh, _ = norm_parts(x)
        a = (xh * norms[0:1, :] + norms[2:3, :]).astype(BF16)
        rows_of(a_s, m, atoms)[...] = a
        qkv = rows_of(qkv_s, m, atoms)
        for blk in range(3):
            got = dot(a, win[:, blk * width : (blk + 1) * width])
            qkv[:, blk * width : (blk + 1) * width] = got.astype(BF16)
            if blk == 2:
                tr_b[...] = jnp.transpose(got).astype(BF16)

        @pl.loop(0, heads // 16)
        def _(g):
            base = g * 16 * head_dim
            for pair, (tile, tiles, off) in enumerate(windows):
                lane = pl.multiple_of(base + tile * LANES, LANES)
                span = tiles * LANES
                rows = pl.ds(pl.multiple_of((g * 8 + pair) * atoms, atoms), atoms)
                one = pl.ds(pl.multiple_of((g * 8 + pair) * 2 * atoms, atoms), atoms)
                two = pl.ds(pl.multiple_of((g * 8 + pair) * 2 * atoms + atoms, atoms), atoms)
                qm = both_heads(qkv[:, pl.ds(lane, span)], off, head_dim)
                z = dot_nt(qkv[:, pl.ds(width + lane, span)], qm) * (scale * LOG2E)
                z = z + jnp.concatenate([pairs[m, one, :], pairs[m, two, :]], axis=1)
                e = jnp.exp2(z - jnp.max(z, axis=0, keepdims=True))
                p = (e * (1.0 / jnp.sum(e, axis=0, keepdims=True))).astype(BF16)
                probs[m, rows, :] = p
                first = pl.multiple_of(base + pair * 2 * head_dim, 16)
                got = dot(tr_b[pl.ds(first, 2 * head_dim), :], p)
                tr_f[pl.ds(first, head_dim), :] = got[:head_dim, :atoms]
                tr_f[pl.ds(pl.multiple_of(first + head_dim, 8), head_dim), :] = got[head_dim:, atoms:]

        o = jnp.transpose(tr_f[...]).astype(BF16)
        rows_of(o_s, m, atoms)[...] = o
        mid = x + dot(o, wout[...])
        rows_of(mid_s, m, atoms)[...] = mid
        xh, _ = norm_parts(mid)
        c = (xh * norms[1:2, :] + norms[3:4, :]).astype(BF16)
        rows_of(c_s, m, atoms)[...] = c
        u = dot(c, wup[...])
        rows_of(u_s, m, atoms)[...] = u
        act = gelu(u).astype(BF16)
        rows_of(act_s, m, atoms)[...] = act
        rows_of(hidden, m, atoms)[...] = (mid + dot(act, wdown[...])).astype(BF16)

    def backward(m):
        grad = rows_of(cot, m, atoms)[...].astype(F32) + rows_of(grecv, m, atoms)[...].astype(F32)
        df = grad.astype(BF16)
        rows_of(df_s, m, atoms)[...] = df
        du = (dot_nt(df, wdown[...]) * gelu_slope(rows_of(u_s, m, atoms)[...])).astype(BF16)
        rows_of(du_s, m, atoms)[...] = du
        dc = dot_nt(du, wup[...])
        xh, inv_std = norm_parts(rows_of(mid_s, m, atoms)[...])
        g_norm[1:2, :] += jnp.sum(dc * xh, axis=0, keepdims=True)
        g_norm[3:4, :] += jnp.sum(dc, axis=0, keepdims=True)
        dmid = grad + norm_back(dc, xh, inv_std, norms[1:2, :])
        rows_of(mid_s, m, atoms)[...] = dmid
        dat = dmid.astype(BF16)
        rows_of(dat_s, m, atoms)[...] = dat
        qkv = rows_of(qkv_s, m, atoms)
        dqkv = rows_of(dqkv_s, m, atoms)
        dqkv[:, 0:width] = dot_nt(dat, wout[...]).astype(BF16)
        tr_b[...] = jnp.transpose(qkv[:, width : 2 * width].astype(F32)).astype(BF16)
        dk_s[...] = jnp.zeros_like(dk_s)
        dv_s[...] = jnp.zeros_like(dv_s)

        @pl.loop(0, heads // 16)
        def _(g):
            base = g * 16 * head_dim
            for pair, (tile, tiles, off) in enumerate(windows):
                lane = pl.multiple_of(base + tile * LANES, LANES)
                span = tiles * LANES
                rows = pl.ds(pl.multiple_of((g * 8 + pair) * atoms, atoms), atoms)
                one = pl.ds(pl.multiple_of((g * 8 + pair) * 2 * atoms, atoms), atoms)
                two = pl.ds(pl.multiple_of((g * 8 + pair) * 2 * atoms + atoms, atoms), atoms)
                dom = both_heads(dqkv[:, pl.ds(lane, span)], off, head_dim)
                dp = dot_nt(qkv[:, pl.ds(2 * width + lane, span)], dom)
                p_low = probs[m, rows, :]
                p = p_low.astype(F32)
                pd = p * dp
                ds = pd - p * jnp.sum(pd, axis=0, keepdims=True)
                pairs[m, one, :] = ds[:, :atoms]
                pairs[m, two, :] = ds[:, atoms:]
                ds_low = ds.astype(BF16)
                dv_s[:, pl.ds(lane, span)] += dot(p_low, dom)
                qm = both_heads(qkv[:, pl.ds(lane, span)], off, head_dim)
                dk_s[:, pl.ds(lane, span)] += dot(ds_low, qm)
                first = pl.multiple_of(base + pair * 2 * head_dim, 16)
                got = dot(tr_b[pl.ds(first, 2 * head_dim), :], ds_low)
                tr_f[pl.ds(first, head_dim), :] = got[:head_dim, :atoms]
                tr_f[pl.ds(pl.multiple_of(first + head_dim, 8), head_dim), :] = got[head_dim:, atoms:]

        dqkv[:, 0:width] = (jnp.transpose(tr_f[...]) * scale).astype(BF16)
        dqkv[:, width : 2 * width] = (dk_s[...] * scale).astype(BF16)
        dqkv[:, 2 * width :] = dv_s[...].astype(BF16)
        da = dot_nt(dqkv[...], win[...])
        xh, inv_std = norm_parts(rows_of(xs, m, atoms)[...].astype(F32))
        g_norm[0:1, :] += jnp.sum(da * xh, axis=0, keepdims=True)
        g_norm[2:3, :] += jnp.sum(da, axis=0, keepdims=True)
        out = rows_of(mid_s, m, atoms)[...] + norm_back(da, xh, inv_std, norms[0:1, :])
        rows_of(igrad, m, atoms)[...] = out.astype(BF16)

    def weight_grads():
        for left, right, out in (
            (act_s, df_s, g_down), (c_s, du_s, g_up), (o_s, dat_s, g_out), (a_s, dqkv_s, g_in),
        ):
            for m in range(micro):
                part = left[m * atoms : (m + 1) * atoms, :].astype(F32)
                left_s[:, m * atoms : (m + 1) * atoms] = jnp.transpose(part).astype(BF16)

            @pl.loop(0, right.shape[1] // 256)
            def _(n):
                cols = pl.ds(pl.multiple_of(n * 256, 256), 256)
                out[:, cols] = dot(left_s[...], right[:, cols]).astype(out.dtype)

    heads_up = 2 * micro
    total = 4 * micro + 1

    @pl.loop(0, total)
    def _(t):
        first = s == 0
        tail = t - heads_up
        is_bias = jnp.where(first, (t < heads_up) & (t % 2 == 0), t < micro)
        is_fwd = jnp.where(
            last,
            (t >= micro) & (t < 3 * micro) & ((t - micro) % 2 == 0),
            jnp.where(first, (t < heads_up) & (t % 2 == 1), (t >= micro) & (t < heads_up)),
        )
        is_back = jnp.where(
            last,
            (t >= micro) & (t < 3 * micro) & ((t - micro) % 2 == 1),
            (tail >= 0) & (tail < 2 * micro - 1) & (tail % 2 == 0),
        )
        is_sum = jnp.where(last, t == 3 * micro, tail == 2 * micro - 1)
        is_tab = jnp.where(
            last,
            t > 3 * micro,
            ((tail >= 0) & (tail < 2 * micro - 1) & (tail % 2 == 1)) | (tail == 2 * micro),
        )
        m_bias = jnp.where(first, t // 2, t)
        m_fwd = jnp.where(last, (t - micro) // 2, jnp.where(first, t // 2, t - micro))
        m_back = jnp.where(last, (t - micro) // 2, tail // 2)
        m_tab = jnp.where(last, t - 3 * micro - 1, jnp.where(tail == 2 * micro, micro - 1, tail // 2))
        if sections == 1:
            is_bias, m_bias = t < micro, t

        @pl.when(is_bias)
        def _():
            make_bias(m_bias)

        @pl.when(is_fwd)
        def _():
            if sections > 1:
                @pl.when(s > 0)
                def _():
                    forward_copy(m_fwd).wait_recv()

            forward(m_fwd)
            if sections > 1:
                @pl.when(jnp.logical_not(last))
                def _():
                    forward_copy(m_fwd).start()

        @pl.when(is_back)
        def _():
            if sections > 1:
                @pl.when(jnp.logical_not(last))
                def _():
                    backward_copy(m_back).wait_recv()

            backward(m_back)
            if sections > 1:
                @pl.when(s > 0)
                def _():
                    backward_copy(m_back).start()

        @pl.when(is_sum)
        def _():
            weight_grads()

        @pl.when(is_tab)
        def _():
            table_grads(m_tab)

    if sections > 1:
        @pl.loop(0, micro)
        def _(m):
            @pl.when(jnp.logical_not(last))
            def _():
                forward_copy(m).wait_send()

            @pl.when(s > 0)
            def _():
                backward_copy(m).wait_send()


def layer_call(
    sections, grad_type, tokens, cot, posn, group, counts, path_in, edge_in, win, wout, wup, wdown, norms, tab,
    kern, spd, edges,
):
    micro, _, atoms = posn.shape
    rows, width = tokens.shape
    heads = tab.shape[0]
    shape = jax.ShapeDtypeStruct
    vmem, smem = pl.BlockSpec(memory_space=pltpu.VMEM), pl.BlockSpec(memory_space=pltpu.SMEM)
    outs = (
        shape((rows, width), BF16), shape((rows, width), BF16),
        shape(win.shape, grad_type), shape(wout.shape, grad_type), shape(wup.shape, grad_type),
        shape(wdown.shape, grad_type), shape((4, width), F32), shape((DEPTH, heads), F32),
    )
    low = lambda *dims: pltpu.VMEM(dims, BF16)
    wide = lambda *dims: pltpu.VMEM(dims, F32)
    pair_rows = heads // 2 * atoms
    scratch = [
        low(rows, width), low(rows, width), low(rows, width), low(rows, 3 * width), low(rows, width),
        wide(rows, width), low(rows, width), wide(rows, width), low(rows, width), low(rows, width),
        low(rows, width), low(rows, width), low(rows, 3 * width),
        wide(micro, 2 * pair_rows, atoms), low(micro, pair_rows, 2 * atoms),
        wide(micro, atoms, atoms), wide(micro, atoms, atoms), wide(micro, atoms, atoms),
        low(width, atoms), wide(width, atoms), wide(atoms, width), wide(atoms, width), low(width, rows),
    ] + [pltpu.SemaphoreType.DMA((micro,))] * 4
    params = dict(vmem_limit_bytes=60 * 2**20, has_side_effects=True)
    if sections > 1:
        params["collective_id"] = 0
    return pl.pallas_call(
        functools.partial(body, sections, micro, atoms, heads, kern, spd, edges),
        out_shape=outs,
        in_specs=[smem, smem] + [vmem] * 11,
        out_specs=[vmem] * len(outs),
        scratch_shapes=scratch,
        compiler_params=pltpu.CompilerParams(**params),
        name="sections",
    )(group, counts, tokens, cot, posn, path_in, edge_in, win, wout, wup, wdown, norms, tab)


def on_device(
    tokens, cotangent, positions, conformer_group, atom_counts, path_dist, edge_kind, attn_in, attn_out,
    ffn_up, ffn_down, norm_gain, norm_shift, kernel_proj, path_table, edge_table,
):
    sections = lax.axis_size("section")
    kern, heads = kernel_proj.shape
    spd, edges = path_table.shape[0], edge_table.shape[0]
    norms = jnp.concatenate([norm_gain[0].T, norm_shift[0].T], axis=0).astype(F32)
    rest = jnp.zeros((DEPTH - kern - spd - edges, heads), BF16)
    tab = jnp.concatenate([kernel_proj, path_table, edge_table, rest], axis=0).T
    hidden, igrad, *grads, g_norm, g_tab = layer_call(
        sections, BF16, tokens, cotangent[0], positions, conformer_group, atom_counts, path_dist, edge_kind,
        attn_in[0], attn_out[0], ffn_up[0], ffn_down[0], norms, tab, kern, spd, edges,
    )
    sums = [lax.psum_scatter(g, "dp", scatter_dimension=0, tiled=True)[None].astype(F32) for g in grads]
    norm_sum = lax.psum(g_norm, "dp").T
    share = norm_sum.shape[0] // lax.axis_size("dp")
    norm_sum = lax.dynamic_slice_in_dim(norm_sum, lax.axis_index("dp") * share, share, 0)[None]
    tab_sum = lax.psum(g_tab, ("section", "dp"))
    tabs, start = [], 0
    for count in (kern, spd, edges):
        own = count // sections
        tabs.append(lax.dynamic_slice_in_dim(tab_sum, start + lax.axis_index("section") * own, own, 0))
        start += count
    return (hidden[None], igrad[None], *sums, norm_sum[:, :, :2], norm_sum[:, :, 2:], *tabs)


def solution(mesh):
    in_specs = (
        P("dp", None),
        P("section", "dp", None),
        P("dp", None, None),
        P("dp"),
        P("dp"),
        P("dp", None, None),
        P("dp", None, None),
        P("section", None, None),
        P("section", None, None),
        P("section", None, None),
        P("section", None, None),
        P("section", None, None),
        P("section", None, None),
        P(),
        P(),
        P(),
    )
    out_specs = (
        P("section", "dp", None),
        P("section", "dp", None),
        P("section", "dp", None),
        P("section", "dp", None),
        P("section", "dp", None),
        P("section", "dp", None),
        P("section", "dp", None),
        P("section", "dp", None),
        P("section", None),
        P("section", None),
        P("section", None),
    )
    return jax.shard_map(
        on_device, mesh=mesh, in_specs=in_specs, out_specs=out_specs, check_vma=False
    )
```

```python
import functools
import math

import jax
import jax.numpy as jnp
from jax import lax
from jax.experimental import pallas as pl
from jax.experimental.pallas import tpu as pltpu
from jax.sharding import PartitionSpec as P

F32, BF16 = jnp.float32, jnp.bfloat16
MESH = pl.DeviceIdType.MESH
EPS = 1e-05
NEG_BIG = -1e30
KERN_SPAN = 8.0
KERN_WIDTH = 0.4
LOG2E = math.log2(math.e)
LANES = 128
DEPTH = 256


def dot(a, b):
    return jnp.dot(a, b, preferred_element_type=F32)


def dot_nt(a, b):
    return lax.dot_general(a, b, (((1,), (1,)), ((), ())), preferred_element_type=F32)


def rows_of(ref, m, n):
    return ref.at[pl.ds(pl.multiple_of(m * n, n), n), :]


def norm_parts(values):
    center = values - jnp.mean(values, axis=-1, keepdims=True)
    inv_std = lax.rsqrt(jnp.mean(center * center, axis=-1, keepdims=True) + EPS)
    return center * inv_std, inv_std


def norm_back(dy, xh, inv_std, gain):
    dxh = dy * gain
    return inv_std * (
        dxh
        - jnp.mean(dxh, axis=-1, keepdims=True)
        - xh * jnp.mean(dxh * xh, axis=-1, keepdims=True)
    )


def gelu(u):
    return 0.5 * u * (1.0 + jnp.tanh(0.7978845608028654 * (u + 0.044715 * u * u * u)))


def gelu_slope(u):
    sq = u * u
    t = jnp.tanh(0.7978845608028654 * (u + 0.044715 * sq * u))
    return 0.5 * (1.0 + t) + 0.5 * u * (1.0 - t * t) * (
        0.7978845608028654 * (1.0 + 3 * 0.044715 * sq)
    )


def pair_windows(head_dim):
    out = []
    for pair in range(8):
        lo, hi = pair * 2 * head_dim, pair * 2 * head_dim + 2 * head_dim - 1
        first = lo // LANES
        out.append((first, hi // LANES - first + 1, lo - first * LANES))
    return out


def both_heads(block, off, head_dim):
    lane = lax.broadcasted_iota(jnp.int32, (1, block.shape[1]), 1)
    one = ((lane >= off) & (lane < off + head_dim)).astype(F32).astype(BF16)
    two = ((lane >= off + head_dim) & (lane < off + 2 * head_dim)).astype(F32).astype(BF16)
    return jnp.concatenate([block * one, block * two], axis=0)


def features(dist8, path8, edge8, row, spd, edges, kern):
    atoms = dist8.shape[1]
    alpha = math.sqrt(0.5 * LOG2E) / KERN_WIDTH
    center = lax.broadcasted_iota(jnp.int32, (kern, atoms), 0).astype(F32) * (
        KERN_SPAN / kern * alpha
    )
    t = dist8[row : row + 1, :] * alpha - center
    gauss = jnp.exp2(-(t * t))
    path_id = lax.broadcasted_iota(jnp.int32, (spd, atoms), 0).astype(F32)
    edge_id = lax.broadcasted_iota(jnp.int32, (edges, atoms), 0).astype(F32)
    path = jnp.where(path8[row : row + 1, :] == path_id, 1.0, 0.0)
    edge = jnp.where(edge8[row : row + 1, :] == edge_id, 1.0, 0.0)
    rest = jnp.zeros((DEPTH - kern - spd - edges, atoms), F32)
    return jnp.concatenate([gauss, path, edge, rest], axis=0).astype(BF16)


def body(
    sections, chips, micro, atoms, heads, kern, spd, edges,
    group, counts, tokens, cot, posn, path_in, edge_in, win, wout, wup, wdown, norms, tab,
    *refs,
):
    hidden, igrad, *refs = refs
    if chips:
        (s_in, s_out, s_up, s_down, s_norm, s_tab, grads, g_norm, g_tab, *refs) = refs
    else:
        (grads, g_norm, g_tab, *refs) = refs
    (
        xs, grecv, a_s, qkv_s, o_s, mid_s, c_s, u_s, act_s, df_s, du_s, dat_s, dqkv_s,
        pairs, probs, dist_s, path_s, edge_s, tr_b, tr_f, dk_s, dv_s, left_s,
        fsend, frecv, bsend, brecv, *refs,
    ) = refs
    if chips:
        (
            core_in, line_in, norm_core, norm_sum, norm_in, tab_own, tab_core, tab_sum, tab_sec, tab_line,
            core_send, core_recv, line_send, line_recv, back_send, back_recv,
            nc_sem, nz_send, nz_recv, tc_sem, ts_send, ts_recv, tz_send, tz_recv,
        ) = refs
    width = wout.shape[0]
    head_dim = width // heads
    scale = 1.0 / math.sqrt(head_dim)
    windows = pair_windows(head_dim)
    s = lax.axis_index("section") if sections > 1 else 0
    d = lax.axis_index("dp") if sections > 1 else 0
    last = s == sections - 1

    z, c = d // 2, d % 2

    def to(sec, dp, src, dst, send, recv):
        return pltpu.make_async_remote_copy(
            src_ref=src, dst_ref=dst, send_sem=send, recv_sem=recv, device_id=(sec, dp), device_id_type=MESH
        )

    if chips:
        barrier = pltpu.get_barrier_semaphore()
        pl.semaphore_signal(barrier, inc=1, device_id=(s, 2 * z + 1 - c), device_id_type=MESH)
        for other in range(1, sections):
            pl.semaphore_signal(
                barrier, inc=1, device_id=((s + other) % sections, d), device_id_type=MESH
            )
        for other in range(1, chips):
            pl.semaphore_signal(
                barrier, inc=1, device_id=(s, (d + 2 * other) % (2 * chips)), device_id_type=MESH
            )
        pl.semaphore_wait(barrier, sections + chips - 1)
    elif sections > 1:
        barrier = pltpu.get_barrier_semaphore()

        @pl.when(s > 0)
        def _():
            pl.semaphore_signal(barrier, inc=1, device_id=(s - 1, d), device_id_type=MESH)

        @pl.when(s < sections - 1)
        def _():
            pl.semaphore_signal(barrier, inc=1, device_id=(s + 1, d), device_id_type=MESH)

        pl.semaphore_wait(barrier, jnp.where((s > 0) & (s < sections - 1), 2, 1))

    def forward_copy(m):
        return pltpu.make_async_remote_copy(
            src_ref=rows_of(hidden, m, atoms), dst_ref=rows_of(xs, m, atoms),
            send_sem=fsend.at[m], recv_sem=frecv.at[m],
            device_id=(jnp.minimum(s + 1, sections - 1), d), device_id_type=MESH,
        )

    def backward_copy(m):
        return pltpu.make_async_remote_copy(
            src_ref=rows_of(igrad, m, atoms), dst_ref=rows_of(grecv, m, atoms),
            send_sem=bsend.at[m], recv_sem=brecv.at[m],
            device_id=(jnp.maximum(s - 1, 0), d), device_id_type=MESH,
        )

    @pl.when(s == 0)
    def _():
        xs[...] = tokens[...]

    @pl.when(last)
    def _():
        grecv[...] = jnp.zeros_like(grecv)

    g_norm[...] = jnp.zeros_like(g_norm)
    g_tab[...] = jnp.zeros_like(g_tab)

    def make_bias(m):
        mol = group[m]
        count = counts[mol]
        pos = posn[m]
        pos_t = jnp.transpose(jnp.concatenate([pos, jnp.zeros((5, atoms), F32)], axis=0))
        total = jnp.zeros((atoms, atoms), F32)
        for axis in range(3):
            diff = pos_t[:, axis : axis + 1] - pos[axis : axis + 1, :]
            total = total + diff * diff
        dist_s[m] = jnp.sqrt(total)
        path_s[m] = jnp.transpose(path_in[mol].astype(F32))
        edge_s[m] = jnp.transpose(edge_in[mol].astype(F32))
        out_ref = pairs.at[m]

        @pl.loop(0, atoms // 8)
        def _(t):
            eight = pl.ds(pl.multiple_of(t * 8, 8), 8)
            d8, p8, e8 = dist_s[m, eight, :], path_s[m, eight, :], edge_s[m, eight, :]
            for r in range(0, 8, 2):
                feats = jnp.concatenate(
                    [features(d8, p8, e8, r + q, spd, edges, kern) for q in range(2)], axis=1
                )
                got = dot(tab[...], feats) * LOG2E
                for q in range(2):
                    j = t * 8 + r + q
                    row = jnp.where(j < count, got[:, q * atoms : (q + 1) * atoms], NEG_BIG)
                    out_ref[pl.ds(j, heads, stride=atoms), :] = row

    def table_grads(m):
        in_ref = pairs.at[m]

        def step(t, acc):
            eight = pl.ds(pl.multiple_of(t * 8, 8), 8)
            d8, p8, e8 = dist_s[m, eight, :], path_s[m, eight, :], edge_s[m, eight, :]
            for r in range(0, 8, 2):
                feats = jnp.concatenate(
                    [features(d8, p8, e8, r + q, spd, edges, kern) for q in range(2)], axis=1
                )
                halves = []
                for q in range(2):
                    j = t * 8 + r + q
                    halves.append(in_ref[pl.ds(j, heads, stride=atoms), :])
                ds = jnp.concatenate(halves, axis=1).astype(BF16)
                acc = acc + dot_nt(feats, ds)
            return acc

        g_tab[...] += lax.fori_loop(0, atoms // 8, step, jnp.zeros((DEPTH, heads), F32))

    def forward(m):
        x = rows_of(xs, m, atoms)[...].astype(F32)
        xh, _ = norm_parts(x)
        a = (xh * norms[0:1, :] + norms[2:3, :]).astype(BF16)
        rows_of(a_s, m, atoms)[...] = a
        qkv = rows_of(qkv_s, m, atoms)
        for blk in range(3):
            got = dot(a, win[:, blk * width : (blk + 1) * width])
            qkv[:, blk * width : (blk + 1) * width] = got.astype(BF16)
            if blk == 2:
                tr_b[...] = jnp.transpose(got).astype(BF16)

        @pl.loop(0, heads // 16)
        def _(g):
            base = g * 16 * head_dim
            for pair, (tile, tiles, off) in enumerate(windows):
                lane = pl.multiple_of(base + tile * LANES, LANES)
                span = tiles * LANES
                rows = pl.ds(pl.multiple_of((g * 8 + pair) * atoms, atoms), atoms)
                one = pl.ds(pl.multiple_of((g * 8 + pair) * 2 * atoms, atoms), atoms)
                two = pl.ds(pl.multiple_of((g * 8 + pair) * 2 * atoms + atoms, atoms), atoms)
                qm = both_heads(qkv[:, pl.ds(lane, span)], off, head_dim)
                z = dot_nt(qkv[:, pl.ds(width + lane, span)], qm) * (scale * LOG2E)
                z = z + jnp.concatenate([pairs[m, one, :], pairs[m, two, :]], axis=1)
                e = jnp.exp2(z - jnp.max(z, axis=0, keepdims=True))
                p = (e * (1.0 / jnp.sum(e, axis=0, keepdims=True))).astype(BF16)
                probs[m, rows, :] = p
                first = pl.multiple_of(base + pair * 2 * head_dim, 16)
                got = dot(tr_b[pl.ds(first, 2 * head_dim), :], p)
                tr_f[pl.ds(first, head_dim), :] = got[:head_dim, :atoms]
                tr_f[pl.ds(pl.multiple_of(first + head_dim, 8), head_dim), :] = got[head_dim:, atoms:]

        o = jnp.transpose(tr_f[...]).astype(BF16)
        rows_of(o_s, m, atoms)[...] = o
        mid = x + dot(o, wout[...])
        rows_of(mid_s, m, atoms)[...] = mid
        xh, _ = norm_parts(mid)
        c = (xh * norms[1:2, :] + norms[3:4, :]).astype(BF16)
        rows_of(c_s, m, atoms)[...] = c
        u = dot(c, wup[...])
        rows_of(u_s, m, atoms)[...] = u
        act = gelu(u).astype(BF16)
        rows_of(act_s, m, atoms)[...] = act
        rows_of(hidden, m, atoms)[...] = (mid + dot(act, wdown[...])).astype(BF16)

    def backward(m):
        grad = rows_of(cot, m, atoms)[...].astype(F32) + rows_of(grecv, m, atoms)[...].astype(F32)
        df = grad.astype(BF16)
        rows_of(df_s, m, atoms)[...] = df
        du = (dot_nt(df, wdown[...]) * gelu_slope(rows_of(u_s, m, atoms)[...])).astype(BF16)
        rows_of(du_s, m, atoms)[...] = du
        dc = dot_nt(du, wup[...])
        xh, inv_std = norm_parts(rows_of(mid_s, m, atoms)[...])
        g_norm[1:2, :] += jnp.sum(dc * xh, axis=0, keepdims=True)
        g_norm[3:4, :] += jnp.sum(dc, axis=0, keepdims=True)
        dmid = grad + norm_back(dc, xh, inv_std, norms[1:2, :])
        rows_of(mid_s, m, atoms)[...] = dmid
        dat = dmid.astype(BF16)
        rows_of(dat_s, m, atoms)[...] = dat
        qkv = rows_of(qkv_s, m, atoms)
        dqkv = rows_of(dqkv_s, m, atoms)
        dqkv[:, 0:width] = dot_nt(dat, wout[...]).astype(BF16)
        tr_b[...] = jnp.transpose(qkv[:, width : 2 * width].astype(F32)).astype(BF16)
        dk_s[...] = jnp.zeros_like(dk_s)
        dv_s[...] = jnp.zeros_like(dv_s)

        @pl.loop(0, heads // 16)
        def _(g):
            base = g * 16 * head_dim
            for pair, (tile, tiles, off) in enumerate(windows):
                lane = pl.multiple_of(base + tile * LANES, LANES)
                span = tiles * LANES
                rows = pl.ds(pl.multiple_of((g * 8 + pair) * atoms, atoms), atoms)
                one = pl.ds(pl.multiple_of((g * 8 + pair) * 2 * atoms, atoms), atoms)
                two = pl.ds(pl.multiple_of((g * 8 + pair) * 2 * atoms + atoms, atoms), atoms)
                dom = both_heads(dqkv[:, pl.ds(lane, span)], off, head_dim)
                dp = dot_nt(qkv[:, pl.ds(2 * width + lane, span)], dom)
                p_low = probs[m, rows, :]
                p = p_low.astype(F32)
                pd = p * dp
                ds = pd - p * jnp.sum(pd, axis=0, keepdims=True)
                pairs[m, one, :] = ds[:, :atoms]
                pairs[m, two, :] = ds[:, atoms:]
                ds_low = ds.astype(BF16)
                dv_s[:, pl.ds(lane, span)] += dot(p_low, dom)
                qm = both_heads(qkv[:, pl.ds(lane, span)], off, head_dim)
                dk_s[:, pl.ds(lane, span)] += dot(ds_low, qm)
                first = pl.multiple_of(base + pair * 2 * head_dim, 16)
                got = dot(tr_b[pl.ds(first, 2 * head_dim), :], ds_low)
                tr_f[pl.ds(first, head_dim), :] = got[:head_dim, :atoms]
                tr_f[pl.ds(pl.multiple_of(first + head_dim, 8), head_dim), :] = got[head_dim:, atoms:]

        dqkv[:, 0:width] = (jnp.transpose(tr_f[...]) * scale).astype(BF16)
        dqkv[:, width : 2 * width] = (dk_s[...] * scale).astype(BF16)
        dqkv[:, 2 * width :] = dv_s[...].astype(BF16)
        da = dot_nt(dqkv[...], win[...])
        xh, inv_std = norm_parts(rows_of(xs, m, atoms)[...].astype(F32))
        g_norm[0:1, :] += jnp.sum(da * xh, axis=0, keepdims=True)
        g_norm[2:3, :] += jnp.sum(da, axis=0, keepdims=True)
        out = rows_of(mid_s, m, atoms)[...] + norm_back(da, xh, inv_std, norms[0:1, :])
        rows_of(igrad, m, atoms)[...] = out.astype(BF16)

    parts = grads.shape[-1] // width
    share = grads.shape[2]

    def chunk(n):
        return pl.ds(n * width if isinstance(n, int) else pl.multiple_of(n * width, LANES), width)

    def core_copy(n):
        return to(
            s, 2 * z + 1 - c, grads.at[:, 1 - c, :, chunk(n)], core_in.at[:, :, chunk(n)],
            core_send.at[n], core_recv.at[n],
        )

    def right_copy(n, target):
        return to(
            s, jnp.minimum(d + 2, 2 * chips - 1), grads.at[target, c, :, chunk(n)],
            line_in.at[target + 1, :, chunk(n)], line_send.at[n, target], line_recv.at[n, target],
        )

    def left_copy(n, target):
        return to(
            s, jnp.maximum(d - 2, 0), grads.at[target, c, :, chunk(n)],
            line_in.at[target, :, chunk(n)], back_send.at[n, target], back_recv.at[n, target],
        )

    def add_in(target, slot, cols):
        both = grads[target, c, :, cols].astype(F32) + line_in[slot, :, cols].astype(F32)
        grads[target, c, :, cols] = both.astype(BF16)

    def settle(n):
        core_copy(n).wait_recv()
        for target in range(chips):
            both = grads[target, c, :, chunk(n)].astype(F32) + core_in[target, :, chunk(n)].astype(F32)
            grads[target, c, :, chunk(n)] = both.astype(BF16)

        @pl.when(z == 0)
        def _():
            for target in range(chips - 1, 0, -1):
                right_copy(n, target).start()

        @pl.when(z == chips - 1)
        def _():
            for target in range(chips - 1):
                left_copy(n, target).start()

    def norm_copy():
        return to(s, 2 * z + 1 - c, g_norm, norm_core, nc_sem.at[0], nc_sem.at[1])

    def weight_grads():
        if chips:
            norm_copy().start()
        jobs = [(act_s, df_s, 0), (c_s, du_s, 0), (o_s, dat_s, 0)] + [(a_s, dqkv_s, q) for q in range(3)]
        for n, (left, right, col) in enumerate(jobs):
            if col == 0:
                for m in range(micro):
                    part = left[m * atoms : (m + 1) * atoms, :].astype(F32)
                    left_s[:, m * atoms : (m + 1) * atoms] = jnp.transpose(part).astype(BF16)

            @pl.loop(0, width // 256)
            def _(q):
                cols = pl.ds(pl.multiple_of(col * width + q * 256, 256), 256)
                got = dot(left_s[...], right[:, cols]).astype(BF16)
                cols = pl.ds(pl.multiple_of(n * width + q * 256, 256), 256)
                grads[:, :, :, cols] = got.reshape(grads.shape[:3] + (256,))

            if chips:
                core_copy(n).start()
                if n:
                    settle(n - 1)
        if chips:
            settle(parts - 1)

    def norm_window(dp):
        first = jnp.minimum(dp * share // LANES, width // LANES - 2)
        return pl.ds(pl.multiple_of(first * LANES, LANES), 2 * LANES)

    def norm_line(there, here):
        return to(
            s, 2 * there + c, norm_sum.at[:, norm_window(2 * there + c)], norm_in.at[here],
            nz_send.at[there], nz_recv.at[here],
        )

    def tab_copy():
        return to(s, 2 * z + 1 - c, tab_own, tab_core, tc_sem.at[0], tc_sem.at[1])

    def tab_section(there, here):
        return to(there, d, tab_sum.at[0], tab_sec.at[here], ts_send.at[there], ts_recv.at[here])

    def tab_chip(there, here):
        return to(s, 2 * there + c, tab_sum.at[1], tab_line.at[here], tz_send.at[there], tz_recv.at[here])

    def others(mine, count, act):
        for other in range(count):
            @pl.when(other != mine)
            def _():
                act(other)

    def reduce_all():
        wide_tab = jnp.concatenate(
            [g_tab[...], jnp.zeros((DEPTH, LANES - heads), F32)], axis=1
        )
        tab_own[...] = jnp.transpose(wide_tab)[:heads, :]
        tab_copy().start()
        norm_copy().wait_recv()
        norm_sum[...] = g_norm[...] + norm_core[...]
        norm_in[z] = norm_sum[:, norm_window(d)]
        others(z, chips, lambda o: norm_line(o, z).start())

        def relay(n):
            for target in range(chips - 1, 0, -1):
                @pl.when((z > 0) & (z < target))
                def _():
                    right_copy(n, target).wait_recv()
                    add_in(target, target + 1, chunk(n))
                    right_copy(n, target).start()

            for target in range(chips - 1):
                @pl.when((z < chips - 1) & (z > target))
                def _():
                    left_copy(n, target).wait_recv()
                    add_in(target, target, chunk(n))
                    left_copy(n, target).start()

            @pl.when(z > 0)
            def _():
                right_copy(n, z).wait_recv()

            @pl.when(z < chips - 1)
            def _():
                left_copy(n, z).wait_recv()

            cols = chunk(n)
            mine = grads[z, c, :, cols].astype(F32)
            mine = mine + jnp.where(z > 0, line_in[z + 1, :, cols].astype(F32), 0.0)
            mine = mine + jnp.where(z < chips - 1, line_in[z, :, cols].astype(F32), 0.0)
            return mine

        @pl.loop(0, parts)
        def _(n):
            @pl.when(n == 1)
            def _():
                tab_copy().wait_recv()
                tab_sum[0] = tab_own[...] + tab_core[...]
                tab_sec[s] = tab_sum[0]
                others(s, sections, lambda o: tab_section(o, s).start())

            @pl.when(n == parts // 2 + 1)
            def _():
                others(s, sections, lambda o: tab_section(o, o).wait_recv())
                tab_sum[1] = sum(tab_sec[o] for o in range(sections))
                tab_line[z] = tab_sum[1]
                others(z, chips, lambda o: tab_chip(o, z).start())

            mine = relay(n)
            for k, (ref, col) in enumerate(
                [(s_down, 0), (s_up, 0), (s_out, 0)] + [(s_in, q) for q in range(3)]
            ):
                @pl.when(n == k)
                def _():
                    ref[:, col * width : (col + 1) * width] = mine

        others(z, chips, lambda o: norm_line(o, o).wait_recv())
        s_norm[...] = sum(norm_in[o] for o in range(chips))
        others(z, chips, lambda o: tab_chip(o, o).wait_recv())
        s_tab[...] = sum(tab_line[o] for o in range(chips))

        norm_copy().wait_send()
        tab_copy().wait_send()
        others(z, chips, lambda o: norm_line(o, z).wait_send())
        others(s, sections, lambda o: tab_section(o, s).wait_send())
        others(z, chips, lambda o: tab_chip(o, z).wait_send())

        @pl.loop(0, parts)
        def _(n):
            core_copy(n).wait_send()
            for target in range(chips):
                @pl.when(target > z)
                def _():
                    right_copy(n, target).wait_send()

                @pl.when(target < z)
                def _():
                    left_copy(n, target).wait_send()

    heads_up = 2 * micro
    total = 4 * micro + 1

    @pl.loop(0, total)
    def _(t):
        first = s == 0
        tail = t - heads_up
        is_bias = jnp.where(first, (t < heads_up) & (t % 2 == 0), t < micro)
        is_fwd = jnp.where(
            last,
            (t >= micro) & (t < 3 * micro) & ((t - micro) % 2 == 0),
            jnp.where(first, (t < heads_up) & (t % 2 == 1), (t >= micro) & (t < heads_up)),
        )
        is_back = jnp.where(
            last,
            (t >= micro) & (t < 3 * micro) & ((t - micro) % 2 == 1),
            (tail >= 0) & (tail < 2 * micro - 1) & (tail % 2 == 0),
        )
        is_sum = jnp.where(last, t == 3 * micro, tail == 2 * micro - 1)
        is_tab = jnp.where(
            last,
            t > 3 * micro,
            ((tail >= 0) & (tail < 2 * micro - 1) & (tail % 2 == 1)) | (tail == 2 * micro),
        )
        m_bias = jnp.where(first, t // 2, t)
        m_fwd = jnp.where(last, (t - micro) // 2, jnp.where(first, t // 2, t - micro))
        m_back = jnp.where(last, (t - micro) // 2, tail // 2)
        m_tab = jnp.where(last, t - 3 * micro - 1, jnp.where(tail == 2 * micro, micro - 1, tail // 2))
        if sections == 1:
            is_bias, m_bias = t < micro, t

        @pl.when(is_bias)
        def _():
            make_bias(m_bias)

        @pl.when(is_fwd)
        def _():
            if sections > 1:
                @pl.when(s > 0)
                def _():
                    forward_copy(m_fwd).wait_recv()

            forward(m_fwd)
            if sections > 1:
                @pl.when(jnp.logical_not(last))
                def _():
                    forward_copy(m_fwd).start()

        @pl.when(is_back)
        def _():
            if sections > 1:
                @pl.when(jnp.logical_not(last))
                def _():
                    backward_copy(m_back).wait_recv()

            backward(m_back)
            if sections > 1:
                @pl.when(s > 0)
                def _():
                    backward_copy(m_back).start()

        @pl.when(is_sum)
        def _():
            weight_grads()

        @pl.when(is_tab)
        def _():
            table_grads(m_tab)

    if chips:
        reduce_all()

    if sections > 1:
        @pl.loop(0, micro)
        def _(m):
            @pl.when(jnp.logical_not(last))
            def _():
                forward_copy(m).wait_send()

            @pl.when(s > 0)
            def _():
                backward_copy(m).wait_send()


def layer_call(
    sections, chips, tokens, cot, posn, group, counts, path_in, edge_in, win, wout, wup, wdown, norms, tab,
    kern, spd, edges,
):
    micro, _, atoms = posn.shape
    rows, width = tokens.shape
    heads = tab.shape[0]
    shape = jax.ShapeDtypeStruct
    vmem, smem = pl.BlockSpec(memory_space=pltpu.VMEM), pl.BlockSpec(memory_space=pltpu.SMEM)
    low = lambda *dims: pltpu.VMEM(dims, BF16)
    wide = lambda *dims: pltpu.VMEM(dims, F32)
    sems = lambda *dims: pltpu.SemaphoreType.DMA(dims)
    parts = 3 + win.shape[1] // width
    pair_rows = heads // 2 * atoms
    outs = [shape((rows, width), BF16), shape((rows, width), BF16)]
    share = width // (2 * chips) if chips else width
    grads = (chips, 2, share, parts * width) if chips else (1, 1, width, parts * width)
    local = [(grads, BF16), ((8, width), F32), ((DEPTH, heads), F32)]
    scratch = []
    if chips:
        outs += [shape((share, w.shape[1]), F32) for w in (win, wout, wup, wdown)]
        outs += [shape((8, 2 * LANES), F32), shape((heads, DEPTH), F32)]
        scratch += [pltpu.VMEM(dims, kind) for dims, kind in local]
    else:
        outs += [shape(dims, kind) for dims, kind in local]
    scratch += [
        low(rows, width), low(rows, width), low(rows, width), low(rows, 3 * width), low(rows, width),
        wide(rows, width), low(rows, width), wide(rows, width), low(rows, width), low(rows, width),
        low(rows, width), low(rows, width), low(rows, 3 * width),
        wide(micro, 2 * pair_rows, atoms), low(micro, pair_rows, 2 * atoms),
        wide(micro, atoms, atoms), wide(micro, atoms, atoms), wide(micro, atoms, atoms),
        low(width, atoms), wide(width, atoms), wide(atoms, width), wide(atoms, width), low(width, rows),
    ] + [sems(micro)] * 4
    if chips:
        scratch += [
            low(chips, share, parts * width), low(chips + 1, share, parts * width),
            wide(8, width), wide(8, width), wide(chips, 8, 2 * LANES),
            wide(heads, DEPTH), wide(heads, DEPTH), wide(2, heads, DEPTH),
            wide(sections, heads, DEPTH), wide(chips, heads, DEPTH),
            sems(parts), sems(parts), sems(parts, chips), sems(parts, chips), sems(parts, chips), sems(parts, chips),
            sems(2), sems(chips), sems(chips), sems(2), sems(sections), sems(sections), sems(chips), sems(chips),
        ]
    params = dict(vmem_limit_bytes=60 * 2**20, has_side_effects=True)
    if sections > 1:
        params["collective_id"] = 0
    return pl.pallas_call(
        functools.partial(body, sections, chips, micro, atoms, heads, kern, spd, edges),
        out_shape=outs,
        in_specs=[smem, smem] + [vmem] * 11,
        out_specs=[vmem] * len(outs),
        scratch_shapes=scratch,
        compiler_params=pltpu.CompilerParams(**params),
        name="sections",
    )(group, counts, tokens, cot, posn, path_in, edge_in, win, wout, wup, wdown, norms, tab)


def on_device(
    tokens, cotangent, positions, conformer_group, atom_counts, path_dist, edge_kind, attn_in, attn_out,
    ffn_up, ffn_down, norm_gain, norm_shift, kernel_proj, path_table, edge_table,
):
    sections, count = lax.axis_size("section"), lax.axis_size("dp")
    section, place = lax.axis_index("section"), lax.axis_index("dp")
    kern, heads = kernel_proj.shape
    spd, edges = path_table.shape[0], edge_table.shape[0]
    width = attn_out.shape[1]
    share = width // count
    chips = count // 2 if count <= 8 and share % 16 == 0 and share <= LANES else 0
    norms = jnp.concatenate([norm_gain[0].T, norm_shift[0].T], axis=0).astype(F32)
    rest = jnp.zeros((DEPTH - kern - spd - edges, heads), BF16)
    tab = jnp.concatenate([kernel_proj, path_table, edge_table, rest], axis=0).T
    hidden, igrad, *sums = layer_call(
        sections, chips, tokens, cotangent[0], positions, conformer_group, atom_counts, path_dist, edge_kind,
        attn_in[0], attn_out[0], ffn_up[0], ffn_down[0], norms, tab, kern, spd, edges,
    )
    if chips:
        *sums, norm_sum, tab_sum = sums
        first = jnp.minimum(place * share // LANES, width // LANES - 2) * LANES
        norm_sum = lax.dynamic_slice_in_dim(norm_sum[:4], place * share - first, share, 1).T[None]
        tab_sum = tab_sum.T
    else:
        grads, g_norm, g_tab = sums
        split = lambda a, n: grads[0, 0, :, a * width : (a + n) * width]
        sums = [
            lax.psum_scatter(g, "dp", scatter_dimension=0, tiled=True).astype(F32)
            for g in (split(3, 3), split(2, 1), split(1, 1), split(0, 1))
        ]
        norm_sum = lax.psum(g_norm[:4], "dp").T
        norm_sum = lax.dynamic_slice_in_dim(norm_sum, place * share, share, 0)[None]
        tab_sum = lax.psum(g_tab, ("section", "dp"))
    tabs, start = [], 0
    for rows in (kern, spd, edges):
        own = rows // sections
        tabs.append(lax.dynamic_slice_in_dim(tab_sum, start + section * own, own, 0))
        start += rows
    return (hidden[None], igrad[None], *(g[None] for g in sums), norm_sum[:, :, :2], norm_sum[:, :, 2:], *tabs)


def solution(mesh):
    in_specs = (
        P("dp", None),
        P("section", "dp", None),
        P("dp", None, None),
        P("dp"),
        P("dp"),
        P("dp", None, None),
        P("dp", None, None),
        P("section", None, None),
        P("section", None, None),
        P("section", None, None),
        P("section", None, None),
        P("section", None, None),
        P("section", None, None),
        P(),
        P(),
        P(),
    )
    out_specs = (
        P("section", "dp", None),
        P("section", "dp", None),
        P("section", "dp", None),
        P("section", "dp", None),
        P("section", "dp", None),
        P("section", "dp", None),
        P("section", "dp", None),
        P("section", "dp", None),
        P("section", None),
        P("section", None),
        P("section", None),
    )
    return jax.shard_map(
        on_device, mesh=mesh, in_specs=in_specs, out_specs=out_specs, check_vma=False
    )
```

```python
import functools
import math

import jax
import jax.numpy as jnp
from jax import lax
from jax.experimental import pallas as pl
from jax.experimental.pallas import tpu as pltpu
from jax.sharding import PartitionSpec as P

F32, BF16 = jnp.float32, jnp.bfloat16
MESH = pl.DeviceIdType.MESH
EPS = 1e-05
NEG_BIG = -1e30
KERN_SPAN = 8.0
KERN_WIDTH = 0.4
LOG2E = math.log2(math.e)
LANES = 128
DEPTH = 256
LAG = 3


def dot(a, b):
    return jnp.dot(a, b, preferred_element_type=F32)


def dot_nt(a, b):
    return lax.dot_general(a, b, (((1,), (1,)), ((), ())), preferred_element_type=F32)


def rows_of(ref, m, n):
    return ref.at[pl.ds(pl.multiple_of(m * n, n), n), :]


def norm_parts(values):
    center = values - jnp.mean(values, axis=-1, keepdims=True)
    inv_std = lax.rsqrt(jnp.mean(center * center, axis=-1, keepdims=True) + EPS)
    return center * inv_std, inv_std


def norm_back(dy, xh, inv_std, gain):
    dxh = dy * gain
    return inv_std * (
        dxh
        - jnp.mean(dxh, axis=-1, keepdims=True)
        - xh * jnp.mean(dxh * xh, axis=-1, keepdims=True)
    )


def gelu(u):
    return 0.5 * u * (1.0 + jnp.tanh(0.7978845608028654 * (u + 0.044715 * u * u * u)))


def gelu_slope(u):
    sq = u * u
    t = jnp.tanh(0.7978845608028654 * (u + 0.044715 * sq * u))
    return 0.5 * (1.0 + t) + 0.5 * u * (1.0 - t * t) * (
        0.7978845608028654 * (1.0 + 3 * 0.044715 * sq)
    )


def pair_windows(head_dim):
    out = []
    for pair in range(8):
        lo, hi = pair * 2 * head_dim, pair * 2 * head_dim + 2 * head_dim - 1
        first = lo // LANES
        out.append((first, hi // LANES - first + 1, lo - first * LANES))
    return out


def both_heads(block, off, head_dim):
    lane = lax.broadcasted_iota(jnp.int32, (1, block.shape[1]), 1)
    one = ((lane >= off) & (lane < off + head_dim)).astype(F32).astype(BF16)
    two = ((lane >= off + head_dim) & (lane < off + 2 * head_dim)).astype(F32).astype(BF16)
    return jnp.concatenate([block * one, block * two], axis=0)


def tile_pairs(tile, windows):
    return [
        (pair, (first - tile) * LANES + off)
        for pair, (first, tiles, off) in enumerate(windows)
        if first <= tile < first + tiles
    ]


def features(dist8, path8, edge8, row, spd, edges, kern):
    atoms = dist8.shape[1]
    alpha = math.sqrt(0.5 * LOG2E) / KERN_WIDTH
    center = lax.broadcasted_iota(jnp.int32, (kern, atoms), 0).astype(F32) * (
        KERN_SPAN / kern * alpha
    )
    t = dist8[row : row + 1, :] * alpha - center
    gauss = jnp.exp2(-(t * t))
    path_id = lax.broadcasted_iota(jnp.int32, (spd, atoms), 0).astype(F32)
    edge_id = lax.broadcasted_iota(jnp.int32, (edges, atoms), 0).astype(F32)
    path = jnp.where(path8[row : row + 1, :] == path_id, 1.0, 0.0)
    edge = jnp.where(edge8[row : row + 1, :] == edge_id, 1.0, 0.0)
    rest = jnp.zeros((DEPTH - kern - spd - edges, atoms), F32)
    return jnp.concatenate([gauss, path, edge, rest], axis=0).astype(BF16)


def body(
    sections, chips, micro, atoms, heads, kern, spd, edges,
    group, counts, tokens, cot, posn, path_in, edge_in, win, wout, wup, wdown, norms, tab,
    *refs,
):
    hidden, igrad, *refs = refs
    if chips:
        (sums, s_norm, s_tab, grads, g_norm, g_tab, *refs) = refs
    else:
        (grads, g_norm, g_tab, *refs) = refs
    (
        xs, grecv, a_s, qkv_s, o_s, mid_s, c_s, u_s, act_s, df_s, du_s, dat_s, dqkv_s,
        pairs, probs, dist_s, path_s, edge_s, tr_b, tr_f, ds_s, left_s,
        fsend, frecv, bsend, brecv, *refs,
    ) = refs
    if chips:
        (
            core_in, line_in, norm_core, norm_sum, norm_in, tab_own, tab_core, tab_sum, tab_sec, tab_line,
            core_send, core_recv, line_send, line_recv, back_send, back_recv,
            nc_sem, nz_send, nz_recv, tc_sem, ts_send, ts_recv, tz_send, tz_recv,
        ) = refs
    width = wout.shape[0]
    head_dim = width // heads
    scale = 1.0 / math.sqrt(head_dim)
    windows = pair_windows(head_dim)
    s = lax.axis_index("section") if sections > 1 else 0
    d = lax.axis_index("dp") if sections > 1 else 0
    last = s == sections - 1

    z, c = d // 2, d % 2

    def to(sec, dp, src, dst, send, recv):
        return pltpu.make_async_remote_copy(
            src_ref=src, dst_ref=dst, send_sem=send, recv_sem=recv, device_id=(sec, dp), device_id_type=MESH
        )

    if chips:
        barrier = pltpu.get_barrier_semaphore()
        pl.semaphore_signal(barrier, inc=1, device_id=(s, 2 * z + 1 - c), device_id_type=MESH)
        for other in range(1, sections):
            pl.semaphore_signal(
                barrier, inc=1, device_id=((s + other) % sections, d), device_id_type=MESH
            )
        for other in range(1, chips):
            pl.semaphore_signal(
                barrier, inc=1, device_id=(s, (d + 2 * other) % (2 * chips)), device_id_type=MESH
            )
        pl.semaphore_wait(barrier, sections + chips - 1)
    elif sections > 1:
        barrier = pltpu.get_barrier_semaphore()

        @pl.when(s > 0)
        def _():
            pl.semaphore_signal(barrier, inc=1, device_id=(s - 1, d), device_id_type=MESH)

        @pl.when(s < sections - 1)
        def _():
            pl.semaphore_signal(barrier, inc=1, device_id=(s + 1, d), device_id_type=MESH)

        pl.semaphore_wait(barrier, jnp.where((s > 0) & (s < sections - 1), 2, 1))

    def forward_copy(m):
        return pltpu.make_async_remote_copy(
            src_ref=rows_of(hidden, m, atoms), dst_ref=rows_of(xs, m, atoms),
            send_sem=fsend.at[m], recv_sem=frecv.at[m],
            device_id=(jnp.minimum(s + 1, sections - 1), d), device_id_type=MESH,
        )

    def backward_copy(m):
        return pltpu.make_async_remote_copy(
            src_ref=rows_of(igrad, m, atoms), dst_ref=rows_of(grecv, m, atoms),
            send_sem=bsend.at[m], recv_sem=brecv.at[m],
            device_id=(jnp.maximum(s - 1, 0), d), device_id_type=MESH,
        )

    def head_rows(g, head):
        return pl.ds(pl.multiple_of((g * 16 + head) * atoms, atoms), atoms)

    def pair_rows(g, pair):
        return pl.ds(pl.multiple_of((g * 8 + pair) * atoms, atoms), atoms)

    @pl.when(s == 0)
    def _():
        xs[...] = tokens[...]

    @pl.when(last)
    def _():
        grecv[...] = jnp.zeros_like(grecv)

    g_norm[...] = jnp.zeros_like(g_norm)
    g_tab[...] = jnp.zeros_like(g_tab)

    def make_bias(m):
        mol = group[m]
        count = counts[mol]
        pos = posn[m]
        pos_t = jnp.transpose(jnp.concatenate([pos, jnp.zeros((5, atoms), F32)], axis=0))
        total = jnp.zeros((atoms, atoms), F32)
        for axis in range(3):
            diff = pos_t[:, axis : axis + 1] - pos[axis : axis + 1, :]
            total = total + diff * diff
        dist_s[m] = jnp.sqrt(total)
        path_s[m] = jnp.transpose(path_in[mol].astype(F32))
        edge_s[m] = jnp.transpose(edge_in[mol].astype(F32))
        out_ref = pairs.at[m]

        @pl.loop(0, atoms // 8)
        def _(t):
            eight = pl.ds(pl.multiple_of(t * 8, 8), 8)
            d8, p8, e8 = dist_s[m, eight, :], path_s[m, eight, :], edge_s[m, eight, :]
            for r in range(0, 8, 2):
                feats = jnp.concatenate(
                    [features(d8, p8, e8, r + q, spd, edges, kern) for q in range(2)], axis=1
                )
                got = dot(tab[...], feats) * LOG2E
                for q in range(2):
                    j = t * 8 + r + q
                    row = jnp.where(j < count, got[:, q * atoms : (q + 1) * atoms], NEG_BIG)
                    out_ref[pl.ds(j, heads, stride=atoms), :] = row

    def table_grads(m):
        in_ref = pairs.at[m]

        def step(t, acc):
            eight = pl.ds(pl.multiple_of(t * 8, 8), 8)
            d8, p8, e8 = dist_s[m, eight, :], path_s[m, eight, :], edge_s[m, eight, :]
            for r in range(0, 8, 2):
                feats = jnp.concatenate(
                    [features(d8, p8, e8, r + q, spd, edges, kern) for q in range(2)], axis=1
                )
                halves = []
                for q in range(2):
                    j = t * 8 + r + q
                    halves.append(in_ref[pl.ds(j, heads, stride=atoms), :])
                ds = jnp.concatenate(halves, axis=1).astype(BF16)
                acc = acc + dot_nt(feats, ds)
            return acc

        g_tab[...] += lax.fori_loop(0, atoms // 8, step, jnp.zeros((DEPTH, heads), F32))

    def forward(m):
        x = rows_of(xs, m, atoms)[...].astype(F32)
        xh, _ = norm_parts(x)
        a = (xh * norms[0:1, :] + norms[2:3, :]).astype(BF16)
        rows_of(a_s, m, atoms)[...] = a
        qkv = rows_of(qkv_s, m, atoms)
        for blk in range(3):
            got = dot(a, win[:, blk * width : (blk + 1) * width])
            qkv[:, blk * width : (blk + 1) * width] = got.astype(BF16)
            if blk == 2:
                tr_b[...] = jnp.transpose(got).astype(BF16)

        @pl.loop(0, heads // 16)
        def _(g):
            base = g * 16 * head_dim
            for pair, (tile, tiles, off) in enumerate(windows):
                lane = pl.multiple_of(base + tile * LANES, LANES)
                span = tiles * LANES
                qm = both_heads(qkv[:, pl.ds(lane, span)], off, head_dim)
                z = dot_nt(qkv[:, pl.ds(width + lane, span)], qm) * (scale * LOG2E)
                for q in range(2):
                    pairs[m, head_rows(g, 2 * pair + q), :] += z[:, q * atoms : (q + 1) * atoms]
            for head in range(16):
                z = pairs[m, head_rows(g, head), :]
                e = jnp.exp2(z - jnp.max(z, axis=0, keepdims=True))
                p = (e * (1.0 / jnp.sum(e, axis=0, keepdims=True))).astype(BF16)
                probs[m, pair_rows(g, head // 2), head % 2 * atoms : (head % 2 + 1) * atoms] = p
            for pair in range(8):
                first = pl.multiple_of(base + pair * 2 * head_dim, 16)
                got = dot(tr_b[pl.ds(first, 2 * head_dim), :], probs[m, pair_rows(g, pair), :])
                tr_f[pl.ds(first, head_dim), :] = got[:head_dim, :atoms]
                tr_f[pl.ds(pl.multiple_of(first + head_dim, 8), head_dim), :] = got[head_dim:, atoms:]

        o = jnp.transpose(tr_f[...]).astype(BF16)
        rows_of(o_s, m, atoms)[...] = o
        mid = x + dot(o, wout[...])
        rows_of(mid_s, m, atoms)[...] = mid
        xh, _ = norm_parts(mid)
        c = (xh * norms[1:2, :] + norms[3:4, :]).astype(BF16)
        rows_of(c_s, m, atoms)[...] = c
        u = dot(c, wup[...])
        rows_of(u_s, m, atoms)[...] = u
        act = gelu(u).astype(BF16)
        rows_of(act_s, m, atoms)[...] = act
        rows_of(hidden, m, atoms)[...] = (mid + dot(act, wdown[...])).astype(BF16)

    def backward(m):
        grad = rows_of(cot, m, atoms)[...].astype(F32) + rows_of(grecv, m, atoms)[...].astype(F32)
        df = grad.astype(BF16)
        rows_of(df_s, m, atoms)[...] = df
        du = (dot_nt(df, wdown[...]) * gelu_slope(rows_of(u_s, m, atoms)[...])).astype(BF16)
        rows_of(du_s, m, atoms)[...] = du
        dc = dot_nt(du, wup[...])
        xh, inv_std = norm_parts(rows_of(mid_s, m, atoms)[...])
        g_norm[1:2, :] += jnp.sum(dc * xh, axis=0, keepdims=True)
        g_norm[3:4, :] += jnp.sum(dc, axis=0, keepdims=True)
        dmid = grad + norm_back(dc, xh, inv_std, norms[1:2, :])
        rows_of(mid_s, m, atoms)[...] = dmid
        dat = dmid.astype(BF16)
        rows_of(dat_s, m, atoms)[...] = dat
        qkv = rows_of(qkv_s, m, atoms)
        dqkv = rows_of(dqkv_s, m, atoms)
        dqkv[:, 0:width] = dot_nt(dat, wout[...]).astype(BF16)
        tr_b[...] = jnp.transpose(qkv[:, width : 2 * width].astype(F32)).astype(BF16)

        @pl.loop(0, heads // 16)
        def _(g):
            base = g * 16 * head_dim
            for pair, (tile, tiles, off) in enumerate(windows):
                lane = pl.multiple_of(base + tile * LANES, LANES)
                span = tiles * LANES
                dom = both_heads(dqkv[:, pl.ds(lane, span)], off, head_dim)
                dp = dot_nt(qkv[:, pl.ds(2 * width + lane, span)], dom)
                for q in range(2):
                    pairs[m, head_rows(g, 2 * pair + q), :] = dp[:, q * atoms : (q + 1) * atoms]
            for head in range(16):
                half = pl.ds(head % 2 * atoms, atoms)
                p = probs[m, pair_rows(g, head // 2), half].astype(F32)
                pd = p * pairs[m, head_rows(g, head), :]
                ds = pd - p * jnp.sum(pd, axis=0, keepdims=True)
                pairs[m, head_rows(g, head), :] = ds
                ds_s[head // 2, :, half] = ds.astype(BF16)
            for tile in range(16 * head_dim // LANES):
                lane = pl.multiple_of(base + tile * LANES, LANES)
                inside = tile_pairs(tile, windows)
                left = jnp.concatenate([probs[m, pair_rows(g, pair), :] for pair, _ in inside], axis=1)
                block = dqkv[:, pl.ds(lane, LANES)]
                right = jnp.concatenate([both_heads(block, off, head_dim) for _, off in inside], axis=0)
                dqkv[:, pl.ds(2 * width + lane, LANES)] = dot(left, right).astype(BF16)
                left = jnp.concatenate([ds_s[pair] for pair, _ in inside], axis=1)
                block = qkv[:, pl.ds(lane, LANES)]
                right = jnp.concatenate([both_heads(block, off, head_dim) for _, off in inside], axis=0)
                dqkv[:, pl.ds(width + lane, LANES)] = (dot(left, right) * scale).astype(BF16)
            for pair in range(8):
                first = pl.multiple_of(base + pair * 2 * head_dim, 16)
                got = dot(tr_b[pl.ds(first, 2 * head_dim), :], ds_s[pair])
                tr_f[pl.ds(first, head_dim), :] = got[:head_dim, :atoms]
                tr_f[pl.ds(pl.multiple_of(first + head_dim, 8), head_dim), :] = got[head_dim:, atoms:]

        dqkv[:, 0:width] = (jnp.transpose(tr_f[...]) * scale).astype(BF16)
        da = dot_nt(dqkv[...], win[...])
        xh, inv_std = norm_parts(rows_of(xs, m, atoms)[...].astype(F32))
        g_norm[0:1, :] += jnp.sum(da * xh, axis=0, keepdims=True)
        g_norm[2:3, :] += jnp.sum(da, axis=0, keepdims=True)
        out = rows_of(mid_s, m, atoms)[...] + norm_back(da, xh, inv_std, norms[0:1, :])
        rows_of(igrad, m, atoms)[...] = out.astype(BF16)

    parts = grads.shape[-1] // width
    share = grads.shape[2]

    def chunk(n):
        return pl.ds(n * width if isinstance(n, int) else pl.multiple_of(n * width, LANES), width)

    def core_copy(n):
        return to(
            s, 2 * z + 1 - c, grads.at[:, 1 - c, :, chunk(n)], core_in.at[:, :, chunk(n)],
            core_send.at[n], core_recv.at[n],
        )

    def right_copy(n, target):
        return to(
            s, jnp.minimum(d + 2, 2 * chips - 1), grads.at[target, c, :, chunk(n)],
            line_in.at[target + 1, :, chunk(n)], line_send.at[n, target], line_recv.at[n, target],
        )

    def left_copy(n, target):
        return to(
            s, jnp.maximum(d - 2, 0), grads.at[target, c, :, chunk(n)],
            line_in.at[target, :, chunk(n)], back_send.at[n, target], back_recv.at[n, target],
        )

    def add_in(target, slot, cols):
        both = grads[target, c, :, cols].astype(F32) + line_in[slot, :, cols].astype(F32)
        grads[target, c, :, cols] = both.astype(BF16)

    def settle(n):
        core_copy(n).wait_recv()
        for target in range(chips):
            both = grads[target, c, :, chunk(n)].astype(F32) + core_in[target, :, chunk(n)].astype(F32)
            grads[target, c, :, chunk(n)] = both.astype(BF16)

            @pl.when(z == target)
            def _():
                sums[:, chunk(n)] = both

        @pl.when(z == 0)
        def _():
            right_copy(n, chips - 1).start()

        @pl.when(z == chips - 1)
        def _():
            left_copy(n, 0).start()

    def norm_copy():
        return to(s, 2 * z + 1 - c, g_norm, norm_core, nc_sem.at[0], nc_sem.at[1])

    def weight_grads():
        if chips:
            norm_copy().start()
        jobs = [(act_s, df_s, 0), (c_s, du_s, 0), (o_s, dat_s, 0)] + [(a_s, dqkv_s, q) for q in range(3)]
        for n, (left, right, col) in enumerate(jobs):
            if col == 0:
                for m in range(micro):
                    part = left[m * atoms : (m + 1) * atoms, :].astype(F32)
                    left_s[:, m * atoms : (m + 1) * atoms] = jnp.transpose(part).astype(BF16)

            @pl.loop(0, width // 256)
            def _(q):
                cols = pl.ds(pl.multiple_of(col * width + q * 256, 256), 256)
                got = dot(left_s[...], right[:, cols]).astype(BF16)
                cols = pl.ds(pl.multiple_of(n * width + q * 256, 256), 256)
                grads[:, :, :, cols] = got.reshape(grads.shape[:3] + (256,))

            if chips:
                core_copy(n).start()
                if n:
                    settle(n - 1)
        if chips:
            settle(parts - 1)

    def norm_window(dp):
        first = jnp.minimum(dp * share // LANES, width // LANES - 2)
        return pl.ds(pl.multiple_of(first * LANES, LANES), 2 * LANES)

    def norm_line(there, here):
        return to(
            s, 2 * there + c, norm_sum.at[:, norm_window(2 * there + c)], norm_in.at[here],
            nz_send.at[there], nz_recv.at[here],
        )

    def tab_copy():
        return to(s, 2 * z + 1 - c, tab_own, tab_core, tc_sem.at[0], tc_sem.at[1])

    def tab_section(there, here):
        return to(there, d, tab_sum.at[0], tab_sec.at[here], ts_send.at[there], ts_recv.at[here])

    def tab_chip(there, here):
        return to(s, 2 * there + c, tab_sum.at[1], tab_line.at[here], tz_send.at[there], tz_recv.at[here])

    def others(mine, count, act):
        for other in range(count):
            @pl.when(other != mine)
            def _():
                act(other)

    def reduce_all():
        wide_tab = jnp.concatenate(
            [g_tab[...], jnp.zeros((DEPTH, LANES - heads), F32)], axis=1
        )
        tab_own[...] = jnp.transpose(wide_tab)[:heads, :]
        tab_copy().start()
        norm_copy().wait_recv()
        norm_sum[...] = g_norm[...] + norm_core[...]
        norm_in[z] = norm_sum[:, norm_window(d)]
        others(z, chips, lambda o: norm_line(o, z).start())

        steps = (chips - 1) * parts

        def end_send(i, act):
            hop, n = i // parts, i % parts

            @pl.when(z == 0)
            def _():
                act(right_copy(n, chips - 1 - hop))

            @pl.when(z == chips - 1)
            def _():
                act(left_copy(n, hop))

        @pl.loop(0, steps)
        def _(i):
            @pl.when(i == 1)
            def _():
                tab_copy().wait_recv()
                tab_sum[0] = tab_own[...] + tab_core[...]
                tab_sec[s] = tab_sum[0]
                others(s, sections, lambda o: tab_section(o, s).start())

            @pl.when(i == steps - parts)
            def _():
                others(s, sections, lambda o: tab_section(o, o).wait_recv())
                tab_sum[1] = sum(tab_sec[o] for o in range(sections))
                tab_line[z] = tab_sum[1]
                others(z, chips, lambda o: tab_chip(o, z).start())

            at_right, at_left = i - LAG * (z - 1), i - LAG * (chips - 2 - z)
            right, right_n = chips - 1 - at_right // parts, at_right % parts
            left, left_n = at_left // parts, at_left % parts

            @pl.when((z > 0) & (at_right >= 0) & (z <= right))
            def _():
                cols = chunk(right_n)
                right_copy(right_n, right).wait_recv()

                @pl.when(z < right)
                def _():
                    add_in(right, right + 1, cols)
                    right_copy(right_n, right).start()

                @pl.when(z == right)
                def _():
                    sums[:, cols] += line_in[right + 1, :, cols].astype(F32)

            @pl.when((z < chips - 1) & (at_left >= 0) & (z >= left))
            def _():
                cols = chunk(left_n)
                left_copy(left_n, left).wait_recv()

                @pl.when(z > left)
                def _():
                    add_in(left, left, cols)
                    left_copy(left_n, left).start()

                @pl.when(z == left)
                def _():
                    sums[:, cols] += line_in[left, :, cols].astype(F32)

            end_send(i, lambda copy: copy.wait_send())

            @pl.when(i + parts < steps)
            def _():
                end_send(i + parts, lambda copy: copy.start())

        others(z, chips, lambda o: norm_line(o, o).wait_recv())
        s_norm[...] = sum(norm_in[o] for o in range(chips))
        others(z, chips, lambda o: tab_chip(o, o).wait_recv())
        s_tab[...] = sum(tab_line[o] for o in range(chips))

        norm_copy().wait_send()
        tab_copy().wait_send()
        others(z, chips, lambda o: norm_line(o, z).wait_send())
        others(s, sections, lambda o: tab_section(o, s).wait_send())
        others(z, chips, lambda o: tab_chip(o, z).wait_send())

        @pl.loop(0, parts)
        def _(n):
            core_copy(n).wait_send()
            for target in range(chips):
                @pl.when((target > z) & (z > 0))
                def _():
                    right_copy(n, target).wait_send()

                @pl.when((target < z) & (z < chips - 1))
                def _():
                    left_copy(n, target).wait_send()

    heads_up = 2 * micro
    total = 4 * micro + 1

    @pl.loop(0, total)
    def _(t):
        first = s == 0
        tail = t - heads_up
        is_bias = jnp.where(first, (t < heads_up) & (t % 2 == 0), t < micro)
        is_fwd = jnp.where(
            last,
            (t >= micro) & (t < 3 * micro) & ((t - micro) % 2 == 0),
            jnp.where(first, (t < heads_up) & (t % 2 == 1), (t >= micro) & (t < heads_up)),
        )
        is_back = jnp.where(
            last,
            (t >= micro) & (t < 3 * micro) & ((t - micro) % 2 == 1),
            (tail >= 0) & (tail < 2 * micro - 1) & (tail % 2 == 0),
        )
        is_sum = jnp.where(last, t == 3 * micro, tail == 2 * micro - 1)
        is_tab = jnp.where(
            last,
            t > 3 * micro,
            ((tail >= 0) & (tail < 2 * micro - 1) & (tail % 2 == 1)) | (tail == 2 * micro),
        )
        m_bias = jnp.where(first, t // 2, t)
        m_fwd = jnp.where(last, (t - micro) // 2, jnp.where(first, t // 2, t - micro))
        m_back = jnp.where(last, (t - micro) // 2, tail // 2)
        m_tab = jnp.where(last, t - 3 * micro - 1, jnp.where(tail == 2 * micro, micro - 1, tail // 2))
        if sections == 1:
            is_bias, m_bias = t < micro, t

        @pl.when(is_bias)
        def _():
            make_bias(m_bias)

        @pl.when(is_fwd)
        def _():
            if sections > 1:
                @pl.when(s > 0)
                def _():
                    forward_copy(m_fwd).wait_recv()

            forward(m_fwd)
            if sections > 1:
                @pl.when(jnp.logical_not(last))
                def _():
                    forward_copy(m_fwd).start()

        @pl.when(is_back)
        def _():
            if sections > 1:
                @pl.when(jnp.logical_not(last))
                def _():
                    backward_copy(m_back).wait_recv()

            backward(m_back)
            if sections > 1:
                @pl.when(s > 0)
                def _():
                    backward_copy(m_back).start()

        @pl.when(is_sum)
        def _():
            weight_grads()

        @pl.when(is_tab)
        def _():
            table_grads(m_tab)

    if chips:
        reduce_all()

    if sections > 1:
        @pl.loop(0, micro)
        def _(m):
            @pl.when(jnp.logical_not(last))
            def _():
                forward_copy(m).wait_send()

            @pl.when(s > 0)
            def _():
                backward_copy(m).wait_send()


def layer_call(
    sections, chips, tokens, cot, posn, group, counts, path_in, edge_in, win, wout, wup, wdown, norms, tab,
    kern, spd, edges,
):
    micro, _, atoms = posn.shape
    rows, width = tokens.shape
    heads = tab.shape[0]
    shape = jax.ShapeDtypeStruct
    vmem, smem = pl.BlockSpec(memory_space=pltpu.VMEM), pl.BlockSpec(memory_space=pltpu.SMEM)
    low = lambda *dims: pltpu.VMEM(dims, BF16)
    wide = lambda *dims: pltpu.VMEM(dims, F32)
    sems = lambda *dims: pltpu.SemaphoreType.DMA(dims)
    parts = 3 + win.shape[1] // width
    all_pairs = heads // 2 * atoms
    outs = [shape((rows, width), BF16), shape((rows, width), BF16)]
    share = width // (2 * chips) if chips else width
    grads = (chips, 2, share, parts * width) if chips else (1, 1, width, parts * width)
    local = [(grads, BF16), ((8, width), F32), ((DEPTH, heads), F32)]
    scratch = []
    if chips:
        outs += [shape((share, parts * width), F32)]
        outs += [shape((8, 2 * LANES), F32), shape((heads, DEPTH), F32)]
        scratch += [pltpu.VMEM(dims, kind) for dims, kind in local]
    else:
        outs += [shape(dims, kind) for dims, kind in local]
    scratch += [
        low(rows, width), low(rows, width), low(rows, width), low(rows, 3 * width), low(rows, width),
        wide(rows, width), low(rows, width), wide(rows, width), low(rows, width), low(rows, width),
        low(rows, width), low(rows, width), low(rows, 3 * width),
        wide(micro, 2 * all_pairs, atoms), low(micro, all_pairs, 2 * atoms),
        wide(micro, atoms, atoms), wide(micro, atoms, atoms), wide(micro, atoms, atoms),
        low(width, atoms), wide(width, atoms), low(8, atoms, 2 * atoms), low(width, rows),
    ] + [sems(micro)] * 4
    if chips:
        scratch += [
            low(chips, share, parts * width), low(chips + 1, share, parts * width),
            wide(8, width), wide(8, width), wide(chips, 8, 2 * LANES),
            wide(heads, DEPTH), wide(heads, DEPTH), wide(2, heads, DEPTH),
            wide(sections, heads, DEPTH), wide(chips, heads, DEPTH),
            sems(parts), sems(parts), sems(parts, chips), sems(parts, chips), sems(parts, chips), sems(parts, chips),
            sems(2), sems(chips), sems(chips), sems(2), sems(sections), sems(sections), sems(chips), sems(chips),
        ]
    params = dict(vmem_limit_bytes=60 * 2**20, has_side_effects=True)
    if sections > 1:
        params["collective_id"] = 0
    return pl.pallas_call(
        functools.partial(body, sections, chips, micro, atoms, heads, kern, spd, edges),
        out_shape=outs,
        in_specs=[smem, smem] + [vmem] * 11,
        out_specs=[vmem] * len(outs),
        scratch_shapes=scratch,
        compiler_params=pltpu.CompilerParams(**params),
        name="sections",
    )(group, counts, tokens, cot, posn, path_in, edge_in, win, wout, wup, wdown, norms, tab)


def finish_body(
    width, kern, spd, edges, sections,
    place, hidden, igrad, sums, norm, tab,
    hidden_o, igrad_o, in_o, out_o, up_o, down_o, gain_o, shift_o, kern_o, path_o, edge_o, tab_s, norm_s,
):
    hidden_o[...] = hidden[...]
    igrad_o[...] = igrad[...]
    down_o[...] = sums[:, 0:width]
    up_o[...] = sums[:, width : 2 * width]
    out_o[...] = sums[:, 2 * width : 3 * width]
    in_o[...] = sums[:, 3 * width :]
    norm_s[...] = jnp.transpose(norm[...])
    rows = norm_s[pl.ds(pl.multiple_of(place[1], 8), gain_o.shape[0]), :]
    gain_o[...] = rows[:, 0:2]
    shift_o[...] = rows[:, 2:4]
    tab_s[...] = jnp.transpose(tab[...])
    start = 0
    for count, ref in ((kern, kern_o), (spd, path_o), (edges, edge_o)):
        own = count // sections
        ref[...] = tab_s[pl.ds(pl.multiple_of(start + place[0] * own, 8), own), :]
        start += count


def finish(hidden, igrad, sums, norm, tab, place, kern, spd, edges, sections):
    width, heads = hidden.shape[1], tab.shape[0]
    share = sums.shape[0]
    shape = jax.ShapeDtypeStruct
    vmem, smem = pl.BlockSpec(memory_space=pltpu.VMEM), pl.BlockSpec(memory_space=pltpu.SMEM)
    outs = (
        [shape(hidden.shape, BF16), shape(igrad.shape, BF16), shape((share, sums.shape[1] - 3 * width), F32)]
        + [shape((share, width), F32)] * 3
        + [shape((share, 2), F32)] * 2
        + [shape((count // sections, heads), F32) for count in (kern, spd, edges)]
    )
    return pl.pallas_call(
        functools.partial(finish_body, width, kern, spd, edges, sections),
        out_shape=outs,
        in_specs=[smem] + [vmem] * 5,
        out_specs=[vmem] * len(outs),
        scratch_shapes=[pltpu.VMEM((DEPTH, heads), F32), pltpu.VMEM((2 * LANES, 8), F32)],
        compiler_params=pltpu.CompilerParams(vmem_limit_bytes=32 * 2**20),
        name="finish",
    )(place, hidden, igrad, sums, norm, tab)


def on_device(
    tokens, cotangent, positions, conformer_group, atom_counts, path_dist, edge_kind, attn_in, attn_out,
    ffn_up, ffn_down, norm_gain, norm_shift, kernel_proj, path_table, edge_table,
):
    sections, count = lax.axis_size("section"), lax.axis_size("dp")
    section, place = lax.axis_index("section"), lax.axis_index("dp")
    kern, heads = kernel_proj.shape
    spd, edges = path_table.shape[0], edge_table.shape[0]
    width = attn_out.shape[1]
    share = width // count
    chips = count // 2 if count <= 8 and share % 16 == 0 and share <= LANES else 0
    norms = jnp.concatenate([norm_gain[0].T, norm_shift[0].T], axis=0).astype(F32)
    rest = jnp.zeros((DEPTH - kern - spd - edges, heads), BF16)
    tab = jnp.concatenate([kernel_proj, path_table, edge_table, rest], axis=0).T
    hidden, igrad, *sums = layer_call(
        sections, chips, tokens, cotangent[0], positions, conformer_group, atom_counts, path_dist, edge_kind,
        attn_in[0], attn_out[0], ffn_up[0], ffn_down[0], norms, tab, kern, spd, edges,
    )
    if chips:
        first = jnp.minimum(place * share // LANES, width // LANES - 2) * LANES
        where = jnp.stack([section, place * share - first]).astype(jnp.int32)
        outs = finish(hidden, igrad, *sums, where, kern, spd, edges, sections)
        return tuple(o[None] for o in outs[:8]) + tuple(outs[8:])
    grads, g_norm, g_tab = sums
    split = lambda a, n: grads[0, 0, :, a * width : (a + n) * width]
    sums = [
        lax.psum_scatter(g, "dp", scatter_dimension=0, tiled=True).astype(F32)
        for g in (split(3, 3), split(2, 1), split(1, 1), split(0, 1))
    ]
    norm_sum = lax.psum(g_norm[:4], "dp").T
    norm_sum = lax.dynamic_slice_in_dim(norm_sum, place * share, share, 0)[None]
    tab_sum = lax.psum(g_tab, ("section", "dp"))
    tabs, start = [], 0
    for rows in (kern, spd, edges):
        own = rows // sections
        tabs.append(lax.dynamic_slice_in_dim(tab_sum, start + section * own, own, 0))
        start += rows
    return (hidden[None], igrad[None], *(g[None] for g in sums), norm_sum[:, :, :2], norm_sum[:, :, 2:], *tabs)


def solution(mesh):
    in_specs = (
        P("dp", None),
        P("section", "dp", None),
        P("dp", None, None),
        P("dp"),
        P("dp"),
        P("dp", None, None),
        P("dp", None, None),
        P("section", None, None),
        P("section", None, None),
        P("section", None, None),
        P("section", None, None),
        P("section", None, None),
        P("section", None, None),
        P(),
        P(),
        P(),
    )
    out_specs = (
        P("section", "dp", None),
        P("section", "dp", None),
        P("section", "dp", None),
        P("section", "dp", None),
        P("section", "dp", None),
        P("section", "dp", None),
        P("section", "dp", None),
        P("section", "dp", None),
        P("section", None),
        P("section", None),
        P("section", None),
    )
    return jax.shard_map(
        on_device, mesh=mesh, in_specs=in_specs, out_specs=out_specs, check_vma=False
    )
```

```python
import functools
import math

import jax
import jax.numpy as jnp
from jax import lax
from jax.experimental import pallas as pl
from jax.experimental.pallas import tpu as pltpu
from jax.sharding import PartitionSpec as P

F32, BF16 = jnp.float32, jnp.bfloat16
MESH = pl.DeviceIdType.MESH
EPS = 1e-05
NEG_BIG = -1e30
KERN_SPAN = 8.0
KERN_WIDTH = 0.4
LOG2E = math.log2(math.e)
LANES = 128
DEPTH = 256
LAG = 3


def dot(a, b):
    return jnp.dot(a, b, preferred_element_type=F32)


def dot_nt(a, b):
    return lax.dot_general(a, b, (((1,), (1,)), ((), ())), preferred_element_type=F32)


def rows_of(ref, m, n):
    return ref.at[pl.ds(pl.multiple_of(m * n, n), n), :]


def norm_parts(values):
    center = values - jnp.mean(values, axis=-1, keepdims=True)
    inv_std = lax.rsqrt(jnp.mean(center * center, axis=-1, keepdims=True) + EPS)
    return center * inv_std, inv_std


def norm_back(dy, xh, inv_std, gain):
    dxh = dy * gain
    return inv_std * (
        dxh
        - jnp.mean(dxh, axis=-1, keepdims=True)
        - xh * jnp.mean(dxh * xh, axis=-1, keepdims=True)
    )


def gelu(u):
    return 0.5 * u * (1.0 + jnp.tanh(0.7978845608028654 * (u + 0.044715 * u * u * u)))


def gelu_slope(u):
    sq = u * u
    t = jnp.tanh(0.7978845608028654 * (u + 0.044715 * sq * u))
    return 0.5 * (1.0 + t) + 0.5 * u * (1.0 - t * t) * (
        0.7978845608028654 * (1.0 + 3 * 0.044715 * sq)
    )


def pair_windows(head_dim):
    out = []
    for pair in range(8):
        lo, hi = pair * 2 * head_dim, pair * 2 * head_dim + 2 * head_dim - 1
        first = lo // LANES
        out.append((first, hi // LANES - first + 1, lo - first * LANES))
    return out


def both_heads(block, off, head_dim):
    lane = lax.broadcasted_iota(jnp.int32, (1, block.shape[1]), 1)
    one = ((lane >= off) & (lane < off + head_dim)).astype(F32).astype(BF16)
    two = ((lane >= off + head_dim) & (lane < off + 2 * head_dim)).astype(F32).astype(BF16)
    return jnp.concatenate([block * one, block * two], axis=0)


def tile_pairs(tile, windows):
    return [
        (pair, (first - tile) * LANES + off)
        for pair, (first, tiles, off) in enumerate(windows)
        if first <= tile < first + tiles
    ]


def features(dist8, path8, edge8, row, spd, edges, kern):
    atoms = dist8.shape[1]
    alpha = math.sqrt(0.5 * LOG2E) / KERN_WIDTH
    center = lax.broadcasted_iota(jnp.int32, (kern, atoms), 0).astype(F32) * (
        KERN_SPAN / kern * alpha
    )
    t = dist8[row : row + 1, :] * alpha - center
    gauss = jnp.exp2(-(t * t))
    path_id = lax.broadcasted_iota(jnp.int32, (spd, atoms), 0).astype(F32)
    edge_id = lax.broadcasted_iota(jnp.int32, (edges, atoms), 0).astype(F32)
    path = jnp.where(path8[row : row + 1, :] == path_id, 1.0, 0.0)
    edge = jnp.where(edge8[row : row + 1, :] == edge_id, 1.0, 0.0)
    rest = jnp.zeros((DEPTH - kern - spd - edges, atoms), F32)
    return jnp.concatenate([gauss, path, edge, rest], axis=0).astype(BF16)


def body(
    sections, chips, micro, atoms, heads, kern, spd, edges,
    group, counts, posn, path_in, edge_in, gains, shifts, kern_in, path_tab, edge_tab,
    tokens, cot_in, win_in, wout_in, wup_in, wdown_in,
    *refs,
):
    hidden, igrad, *refs = refs
    if chips:
        (sums, s_norm, s_tab, grads, g_norm, g_tab, *refs) = refs
    else:
        (grads, g_norm, g_tab, *refs) = refs
    (
        xs, grecv, a_s, qkv_s, o_s, mid_s, c_s, u_s, act_s, df_s, du_s, dat_s, dqkv_s,
        pairs, probs, dist_s, path_s, edge_s, tr_b, tr_f, ds_s, left_s,
        cot, win, wout, wup, wdown, norms, tab_f, tab, load_sem, fsend, frecv, bsend, brecv, *refs,
    ) = refs
    if chips:
        (
            core_in, line_in, norm_core, norm_sum, norm_in, tab_own, tab_core, tab_sum, tab_sec, tab_line,
            core_send, core_recv, line_send, line_recv, back_send, back_recv,
            nc_sem, nz_send, nz_recv, tc_sem, ts_send, ts_recv, tz_send, tz_recv,
        ) = refs
    width = wout.shape[0]
    head_dim = width // heads
    scale = 1.0 / math.sqrt(head_dim)
    windows = pair_windows(head_dim)
    s = lax.axis_index("section") if sections > 1 else 0
    d = lax.axis_index("dp") if sections > 1 else 0
    last = s == sections - 1

    z, c = d // 2, d % 2

    def to(sec, dp, src, dst, send, recv):
        return pltpu.make_async_remote_copy(
            src_ref=src, dst_ref=dst, send_sem=send, recv_sem=recv, device_id=(sec, dp), device_id_type=MESH
        )

    if chips:
        barrier = pltpu.get_barrier_semaphore()
        pl.semaphore_signal(barrier, inc=1, device_id=(s, 2 * z + 1 - c), device_id_type=MESH)
        for other in range(1, sections):
            pl.semaphore_signal(
                barrier, inc=1, device_id=((s + other) % sections, d), device_id_type=MESH
            )
        for other in range(1, chips):
            pl.semaphore_signal(
                barrier, inc=1, device_id=(s, (d + 2 * other) % (2 * chips)), device_id_type=MESH
            )
        pl.semaphore_wait(barrier, sections + chips - 1)
    elif sections > 1:
        barrier = pltpu.get_barrier_semaphore()

        @pl.when(s > 0)
        def _():
            pl.semaphore_signal(barrier, inc=1, device_id=(s - 1, d), device_id_type=MESH)

        @pl.when(s < sections - 1)
        def _():
            pl.semaphore_signal(barrier, inc=1, device_id=(s + 1, d), device_id_type=MESH)

        pl.semaphore_wait(barrier, jnp.where((s > 0) & (s < sections - 1), 2, 1))

    def forward_copy(m):
        return pltpu.make_async_remote_copy(
            src_ref=rows_of(hidden, m, atoms), dst_ref=rows_of(xs, m, atoms),
            send_sem=fsend.at[m], recv_sem=frecv.at[m],
            device_id=(jnp.minimum(s + 1, sections - 1), d), device_id_type=MESH,
        )

    def backward_copy(m):
        return pltpu.make_async_remote_copy(
            src_ref=rows_of(igrad, m, atoms), dst_ref=rows_of(grecv, m, atoms),
            send_sem=bsend.at[m], recv_sem=brecv.at[m],
            device_id=(jnp.maximum(s - 1, 0), d), device_id_type=MESH,
        )

    def head_rows(g, head):
        return pl.ds(pl.multiple_of((g * 16 + head) * atoms, atoms), atoms)

    def pair_rows(g, pair):
        return pl.ds(pl.multiple_of((g * 8 + pair) * atoms, atoms), atoms)

    loads = [(win_in, win), (wout_in, wout), (wup_in, wup), (wdown_in, wdown), (cot_in, cot)]

    def load(k):
        return pltpu.make_async_copy(*loads[k], load_sem.at[k])

    def load_tokens():
        return pltpu.make_async_copy(tokens, xs, load_sem.at[len(loads)])

    @pl.when(s == 0)
    def _():
        load_tokens().start()

    for k in range(len(loads)):
        load(k).start()

    norms[0:2, :] = gains[...].astype(F32)
    norms[2:4, :] = shifts[...].astype(F32)
    square = jnp.concatenate([edge_tab[...].astype(F32), jnp.zeros((heads, LANES - heads), F32)], axis=1)
    square = jnp.concatenate([square, jnp.zeros((LANES - edges, LANES), F32)], axis=0)
    tab_f[...] = jnp.zeros_like(tab_f)
    tab_f[:, 0:kern] = kern_in[...].astype(F32)
    tab_f[:, kern : kern + spd] = path_tab[...].astype(F32)
    tab_f[:, kern + spd : kern + spd + edges] = jnp.transpose(square)[:heads, :edges]
    tab[...] = tab_f[...].astype(BF16)

    @pl.when(last)
    def _():
        grecv[...] = jnp.zeros_like(grecv)

    g_norm[...] = jnp.zeros_like(g_norm)
    g_tab[...] = jnp.zeros_like(g_tab)

    def make_bias(unit):
        m, half = unit // 2, unit % 2
        mol = group[m]
        count = counts[mol]

        @pl.when(half == 0)
        def _():
            pos = jnp.concatenate([posn[axis, pl.ds(m, 1), :] for axis in range(3)], axis=0)
            pos_t = jnp.transpose(jnp.concatenate([pos, jnp.zeros((5, atoms), F32)], axis=0))
            total = jnp.zeros((atoms, atoms), F32)
            for axis in range(3):
                diff = pos_t[:, axis : axis + 1] - pos[axis : axis + 1, :]
                total = total + diff * diff
            dist_s[m] = jnp.sqrt(total)
            path_s[m] = jnp.transpose(path_in[mol].astype(F32))
            edge_s[m] = jnp.transpose(edge_in[mol].astype(F32))

        out_ref = pairs.at[m]

        @pl.loop(0, atoms // 16)
        def _(step):
            t = half * (atoms // 16) + step
            eight = pl.ds(pl.multiple_of(t * 8, 8), 8)
            d8, p8, e8 = dist_s[m, eight, :], path_s[m, eight, :], edge_s[m, eight, :]
            for r in range(0, 8, 2):
                feats = jnp.concatenate(
                    [features(d8, p8, e8, r + q, spd, edges, kern) for q in range(2)], axis=1
                )
                got = dot(tab[...], feats) * LOG2E
                for q in range(2):
                    j = t * 8 + r + q
                    row = jnp.where(j < count, got[:, q * atoms : (q + 1) * atoms], NEG_BIG)
                    out_ref[pl.ds(j, heads, stride=atoms), :] = row

    tab_blocks = micro * (atoms // 8)

    def table_grads(block):
        m, t = block // (atoms // 8), block % (atoms // 8)
        in_ref = pairs.at[m]
        eight = pl.ds(pl.multiple_of(t * 8, 8), 8)
        d8, p8, e8 = dist_s[m, eight, :], path_s[m, eight, :], edge_s[m, eight, :]
        acc = jnp.zeros((DEPTH, heads), F32)
        for r in range(0, 8, 2):
            feats = jnp.concatenate(
                [features(d8, p8, e8, r + q, spd, edges, kern) for q in range(2)], axis=1
            )
            halves = [in_ref[pl.ds(t * 8 + r + q, heads, stride=atoms), :] for q in range(2)]
            acc = acc + dot_nt(feats, jnp.concatenate(halves, axis=1).astype(BF16))
        g_tab[...] += acc

    def forward(m):
        x = rows_of(xs, m, atoms)[...].astype(F32)
        xh, _ = norm_parts(x)
        a = (xh * norms[0:1, :] + norms[2:3, :]).astype(BF16)
        rows_of(a_s, m, atoms)[...] = a
        qkv = rows_of(qkv_s, m, atoms)
        for blk in range(3):
            got = dot(a, win[:, blk * width : (blk + 1) * width])
            qkv[:, blk * width : (blk + 1) * width] = got.astype(BF16)
            if blk == 2:
                tr_b[...] = jnp.transpose(got).astype(BF16)

        @pl.loop(0, heads // 16)
        def _(g):
            base = g * 16 * head_dim
            for pair, (tile, tiles, off) in enumerate(windows):
                lane = pl.multiple_of(base + tile * LANES, LANES)
                span = tiles * LANES
                qm = both_heads(qkv[:, pl.ds(lane, span)], off, head_dim)
                z = dot_nt(qkv[:, pl.ds(width + lane, span)], qm) * (scale * LOG2E)
                for q in range(2):
                    pairs[m, head_rows(g, 2 * pair + q), :] += z[:, q * atoms : (q + 1) * atoms]
            for head in range(16):
                z = pairs[m, head_rows(g, head), :]
                e = jnp.exp2(z - jnp.max(z, axis=0, keepdims=True))
                p = (e * (1.0 / jnp.sum(e, axis=0, keepdims=True))).astype(BF16)
                probs[m, pair_rows(g, head // 2), head % 2 * atoms : (head % 2 + 1) * atoms] = p
            for pair in range(8):
                first = pl.multiple_of(base + pair * 2 * head_dim, 16)
                got = dot(tr_b[pl.ds(first, 2 * head_dim), :], probs[m, pair_rows(g, pair), :])
                tr_f[pl.ds(first, head_dim), :] = got[:head_dim, :atoms]
                tr_f[pl.ds(pl.multiple_of(first + head_dim, 8), head_dim), :] = got[head_dim:, atoms:]

        o = jnp.transpose(tr_f[...]).astype(BF16)
        rows_of(o_s, m, atoms)[...] = o
        mid = x + dot(o, wout[...])
        rows_of(mid_s, m, atoms)[...] = mid
        xh, _ = norm_parts(mid)
        c = (xh * norms[1:2, :] + norms[3:4, :]).astype(BF16)
        rows_of(c_s, m, atoms)[...] = c
        u = dot(c, wup[...])
        rows_of(u_s, m, atoms)[...] = u
        act = gelu(u).astype(BF16)
        rows_of(act_s, m, atoms)[...] = act
        rows_of(hidden, m, atoms)[...] = (mid + dot(act, wdown[...])).astype(BF16)

    def backward(m):
        grad = rows_of(cot, m, atoms)[...].astype(F32) + rows_of(grecv, m, atoms)[...].astype(F32)
        df = grad.astype(BF16)
        rows_of(df_s, m, atoms)[...] = df
        du = (dot_nt(df, wdown[...]) * gelu_slope(rows_of(u_s, m, atoms)[...])).astype(BF16)
        rows_of(du_s, m, atoms)[...] = du
        dc = dot_nt(du, wup[...])
        xh, inv_std = norm_parts(rows_of(mid_s, m, atoms)[...])
        g_norm[1:2, :] += jnp.sum(dc * xh, axis=0, keepdims=True)
        g_norm[3:4, :] += jnp.sum(dc, axis=0, keepdims=True)
        dmid = grad + norm_back(dc, xh, inv_std, norms[1:2, :])
        rows_of(mid_s, m, atoms)[...] = dmid
        dat = dmid.astype(BF16)
        rows_of(dat_s, m, atoms)[...] = dat
        qkv = rows_of(qkv_s, m, atoms)
        dqkv = rows_of(dqkv_s, m, atoms)
        dqkv[:, 0:width] = dot_nt(dat, wout[...]).astype(BF16)
        tr_b[...] = jnp.transpose(qkv[:, width : 2 * width].astype(F32)).astype(BF16)

        @pl.loop(0, heads // 16)
        def _(g):
            base = g * 16 * head_dim
            for pair, (tile, tiles, off) in enumerate(windows):
                lane = pl.multiple_of(base + tile * LANES, LANES)
                span = tiles * LANES
                dom = both_heads(dqkv[:, pl.ds(lane, span)], off, head_dim)
                dp = dot_nt(qkv[:, pl.ds(2 * width + lane, span)], dom)
                for q in range(2):
                    pairs[m, head_rows(g, 2 * pair + q), :] = dp[:, q * atoms : (q + 1) * atoms]
            for head in range(16):
                half = pl.ds(head % 2 * atoms, atoms)
                p = probs[m, pair_rows(g, head // 2), half].astype(F32)
                pd = p * pairs[m, head_rows(g, head), :]
                ds = pd - p * jnp.sum(pd, axis=0, keepdims=True)
                pairs[m, head_rows(g, head), :] = ds
                ds_s[head // 2, :, half] = ds.astype(BF16)
            for tile in range(16 * head_dim // LANES):
                lane = pl.multiple_of(base + tile * LANES, LANES)
                inside = tile_pairs(tile, windows)
                left = jnp.concatenate([probs[m, pair_rows(g, pair), :] for pair, _ in inside], axis=1)
                block = dqkv[:, pl.ds(lane, LANES)]
                right = jnp.concatenate([both_heads(block, off, head_dim) for _, off in inside], axis=0)
                dqkv[:, pl.ds(2 * width + lane, LANES)] = dot(left, right).astype(BF16)
                left = jnp.concatenate([ds_s[pair] for pair, _ in inside], axis=1)
                block = qkv[:, pl.ds(lane, LANES)]
                right = jnp.concatenate([both_heads(block, off, head_dim) for _, off in inside], axis=0)
                dqkv[:, pl.ds(width + lane, LANES)] = (dot(left, right) * scale).astype(BF16)
            for pair in range(8):
                first = pl.multiple_of(base + pair * 2 * head_dim, 16)
                got = dot(tr_b[pl.ds(first, 2 * head_dim), :], ds_s[pair])
                tr_f[pl.ds(first, head_dim), :] = got[:head_dim, :atoms]
                tr_f[pl.ds(pl.multiple_of(first + head_dim, 8), head_dim), :] = got[head_dim:, atoms:]

        dqkv[:, 0:width] = (jnp.transpose(tr_f[...]) * scale).astype(BF16)
        da = dot_nt(dqkv[...], win[...])
        xh, inv_std = norm_parts(rows_of(xs, m, atoms)[...].astype(F32))
        g_norm[0:1, :] += jnp.sum(da * xh, axis=0, keepdims=True)
        g_norm[2:3, :] += jnp.sum(da, axis=0, keepdims=True)
        out = rows_of(mid_s, m, atoms)[...] + norm_back(da, xh, inv_std, norms[0:1, :])
        rows_of(igrad, m, atoms)[...] = out.astype(BF16)

    parts = grads.shape[-1] // width
    share = grads.shape[2]

    def chunk(n):
        return pl.ds(n * width if isinstance(n, int) else pl.multiple_of(n * width, LANES), width)

    def core_copy(n):
        return to(
            s, 2 * z + 1 - c, grads.at[:, 1 - c, :, chunk(n)], core_in.at[:, :, chunk(n)],
            core_send.at[n], core_recv.at[n],
        )

    def right_copy(n, target):
        return to(
            s, jnp.minimum(d + 2, 2 * chips - 1), grads.at[target, c, :, chunk(n)],
            line_in.at[target + 1, :, chunk(n)], line_send.at[n, target], line_recv.at[n, target],
        )

    def left_copy(n, target):
        return to(
            s, jnp.maximum(d - 2, 0), grads.at[target, c, :, chunk(n)],
            line_in.at[target, :, chunk(n)], back_send.at[n, target], back_recv.at[n, target],
        )

    def add_in(target, slot, cols):
        both = grads[target, c, :, cols].astype(F32) + line_in[slot, :, cols].astype(F32)
        grads[target, c, :, cols] = both.astype(BF16)

    def settle(n):
        core_copy(n).wait_recv()
        for target in range(chips):
            both = grads[target, c, :, chunk(n)].astype(F32) + core_in[target, :, chunk(n)].astype(F32)
            grads[target, c, :, chunk(n)] = both.astype(BF16)

            @pl.when(z == target)
            def _():
                sums[:, chunk(n)] = both

        @pl.when(z == 0)
        def _():
            right_copy(n, chips - 1).start()

        @pl.when(z == chips - 1)
        def _():
            left_copy(n, 0).start()

    def norm_copy():
        return to(s, 2 * z + 1 - c, g_norm, norm_core, nc_sem.at[0], nc_sem.at[1])

    def weight_grads():
        if chips:
            norm_copy().start()
        jobs = [(act_s, df_s, 0), (c_s, du_s, 0), (o_s, dat_s, 0)] + [(a_s, dqkv_s, q) for q in range(3)]
        for n, (left, right, col) in enumerate(jobs):
            if col == 0:
                for m in range(micro):
                    part = left[m * atoms : (m + 1) * atoms, :].astype(F32)
                    left_s[:, m * atoms : (m + 1) * atoms] = jnp.transpose(part).astype(BF16)

            @pl.loop(0, width // 256)
            def _(q):
                cols = pl.ds(pl.multiple_of(col * width + q * 256, 256), 256)
                got = dot(left_s[...], right[:, cols]).astype(BF16)
                cols = pl.ds(pl.multiple_of(n * width + q * 256, 256), 256)
                grads[:, :, :, cols] = got.reshape(grads.shape[:3] + (256,))

            if chips:
                core_copy(n).start()
                if n:
                    settle(n - 1)
        if chips:
            settle(parts - 1)

    def norm_window(dp):
        first = jnp.minimum(dp * share // LANES, width // LANES - 2)
        return pl.ds(pl.multiple_of(first * LANES, LANES), 2 * LANES)

    def norm_line(there, here):
        return to(
            s, 2 * there + c, norm_sum.at[:, norm_window(2 * there + c)], norm_in.at[here],
            nz_send.at[there], nz_recv.at[here],
        )

    def tab_copy():
        return to(s, 2 * z + 1 - c, tab_own, tab_core, tc_sem.at[0], tc_sem.at[1])

    def tab_section(there, here):
        return to(there, d, tab_sum.at[0], tab_sec.at[here], ts_send.at[there], ts_recv.at[here])

    def tab_chip(there, here):
        return to(s, 2 * there + c, tab_sum.at[1], tab_line.at[here], tz_send.at[there], tz_recv.at[here])

    def others(mine, count, act):
        for other in range(count):
            @pl.when(other != mine)
            def _():
                act(other)

    def reduce_all():
        norm_copy().wait_recv()
        norm_sum[...] = g_norm[...] + norm_core[...]
        norm_in[z] = norm_sum[:, norm_window(d)]
        others(z, chips, lambda o: norm_line(o, z).start())

        steps = (chips - 1) * parts
        tab_steps = steps - 6
        tab_each = -(-tab_blocks // tab_steps)

        def end_send(i, act):
            hop, n = i // parts, i % parts

            @pl.when(z == 0)
            def _():
                act(right_copy(n, chips - 1 - hop))

            @pl.when(z == chips - 1)
            def _():
                act(left_copy(n, hop))

        @pl.loop(0, steps)
        def _(i):
            @pl.when(i < tab_steps)
            def _():
                @pl.loop(i * tab_each, jnp.minimum((i + 1) * tab_each, tab_blocks))
                def _(block):
                    table_grads(block)

            @pl.when(i == tab_steps)
            def _():
                wide_tab = jnp.concatenate([g_tab[...], jnp.zeros((DEPTH, LANES - heads), F32)], axis=1)
                tab_own[...] = jnp.transpose(wide_tab)[:heads, :]
                tab_copy().start()

            @pl.when(i == tab_steps + 1)
            def _():
                tab_copy().wait_recv()
                tab_sum[0] = tab_own[...] + tab_core[...]
                tab_sec[s] = tab_sum[0]
                others(s, sections, lambda o: tab_section(o, s).start())

            @pl.when(i == tab_steps + 3)
            def _():
                others(s, sections, lambda o: tab_section(o, o).wait_recv())
                tab_sum[1] = sum(tab_sec[o] for o in range(sections))
                tab_line[z] = tab_sum[1]
                others(z, chips, lambda o: tab_chip(o, z).start())

            at_right, at_left = i - LAG * (z - 1), i - LAG * (chips - 2 - z)
            right, right_n = chips - 1 - at_right // parts, at_right % parts
            left, left_n = at_left // parts, at_left % parts

            @pl.when((z > 0) & (at_right >= 0) & (z <= right))
            def _():
                cols = chunk(right_n)
                right_copy(right_n, right).wait_recv()

                @pl.when(z < right)
                def _():
                    add_in(right, right + 1, cols)
                    right_copy(right_n, right).start()

                @pl.when(z == right)
                def _():
                    sums[:, cols] += line_in[right + 1, :, cols].astype(F32)

            @pl.when((z < chips - 1) & (at_left >= 0) & (z >= left))
            def _():
                cols = chunk(left_n)
                left_copy(left_n, left).wait_recv()

                @pl.when(z > left)
                def _():
                    add_in(left, left, cols)
                    left_copy(left_n, left).start()

                @pl.when(z == left)
                def _():
                    sums[:, cols] += line_in[left, :, cols].astype(F32)

            end_send(i, lambda copy: copy.wait_send())

            @pl.when(i + parts < steps)
            def _():
                end_send(i + parts, lambda copy: copy.start())

        others(z, chips, lambda o: norm_line(o, o).wait_recv())
        s_norm[...] = sum(norm_in[o] for o in range(chips))
        others(z, chips, lambda o: tab_chip(o, o).wait_recv())
        s_tab[...] = sum(tab_line[o] for o in range(chips))

        norm_copy().wait_send()
        tab_copy().wait_send()
        others(z, chips, lambda o: norm_line(o, z).wait_send())
        others(s, sections, lambda o: tab_section(o, s).wait_send())
        others(z, chips, lambda o: tab_chip(o, z).wait_send())

        @pl.loop(0, parts)
        def _(n):
            core_copy(n).wait_send()
            for target in range(chips):
                @pl.when((target > z) & (z > 0))
                def _():
                    right_copy(n, target).wait_send()

                @pl.when((target < z) & (z < chips - 1))
                def _():
                    left_copy(n, target).wait_send()

    total = 4 * micro

    @pl.loop(0, total)
    def _(t):
        ahead = jnp.where(last, micro, jnp.minimum(micro, jnp.where(s == 0, 1, 2 * s * s)))
        gap = micro - ahead
        r = t - 2 * ahead
        mixed = (r >= 0) & (r < 3 * gap)
        unit = jnp.where(r < 0, t, 2 * (ahead + r // 3) + r % 3 - 1)
        is_bias = (r < 0) | (mixed & (r % 3 != 0))
        is_fwd = jnp.where(
            last, (r >= 0) & (r % 2 == 0), (mixed & (r % 3 == 0)) | ((r >= 3 * gap) & (t < 3 * micro))
        )
        m_fwd = jnp.where(last, r // 2, jnp.where(mixed, r // 3, r - 2 * gap))
        is_back = jnp.where(last, (r >= 0) & (r % 2 == 1), t >= 3 * micro)
        m_back = jnp.where(last, r // 2, t - 3 * micro)
        @pl.when(is_bias)
        def _():
            make_bias(unit)

        @pl.when(is_fwd)
        def _():
            @pl.when(m_fwd == 0)
            def _():
                for k in range(len(loads) - 1):
                    load(k).wait()

                @pl.when(s == 0)
                def _():
                    load_tokens().wait()

            if sections > 1:
                @pl.when(s > 0)
                def _():
                    forward_copy(m_fwd).wait_recv()

            forward(m_fwd)
            if sections > 1:
                @pl.when(jnp.logical_not(last))
                def _():
                    forward_copy(m_fwd).start()

        @pl.when(is_back)
        def _():
            @pl.when(m_back == 0)
            def _():
                load(len(loads) - 1).wait()

            if sections > 1:
                @pl.when(jnp.logical_not(last))
                def _():
                    backward_copy(m_back).wait_recv()

            backward(m_back)
            if sections > 1:
                @pl.when(s > 0)
                def _():
                    backward_copy(m_back).start()

    weight_grads()
    if chips:
        reduce_all()
    else:
        pl.loop(0, tab_blocks)(table_grads)

    if sections > 1:
        @pl.loop(0, micro)
        def _(m):
            @pl.when(jnp.logical_not(last))
            def _():
                forward_copy(m).wait_send()

            @pl.when(s > 0)
            def _():
                backward_copy(m).wait_send()


def layer_call(
    sections, chips, tokens, cot, posn, group, counts, path_in, edge_in, win, wout, wup, wdown,
    norm_gain, norm_shift, kernel_proj, path_table, edge_table,
):
    micro, _, atoms = posn.shape
    rows, width = tokens.shape
    kern, heads = kernel_proj.shape
    spd, edges = path_table.shape[0], edge_table.shape[0]
    shape = jax.ShapeDtypeStruct
    vmem, smem = pl.BlockSpec(memory_space=pltpu.VMEM), pl.BlockSpec(memory_space=pltpu.SMEM)
    low = lambda *dims: pltpu.VMEM(dims, BF16)
    wide = lambda *dims: pltpu.VMEM(dims, F32)
    sems = lambda *dims: pltpu.SemaphoreType.DMA(dims)
    parts = 3 + win.shape[1] // width
    all_pairs = heads // 2 * atoms
    outs = [shape((rows, width), BF16), shape((rows, width), BF16)]
    share = width // (2 * chips) if chips else width
    grads = (chips, 2, share, parts * width) if chips else (1, 1, width, parts * width)
    local = [(grads, BF16), ((8, width), F32), ((DEPTH, heads), F32)]
    scratch = []
    if chips:
        outs += [shape((share, parts * width), F32)]
        outs += [shape((8, 2 * LANES), F32), shape((heads, DEPTH), F32)]
        scratch += [pltpu.VMEM(dims, kind) for dims, kind in local]
    else:
        outs += [shape(dims, kind) for dims, kind in local]
    scratch += [
        low(rows, width), low(rows, width), low(rows, width), low(rows, 3 * width), low(rows, width),
        wide(rows, width), low(rows, width), wide(rows, width), low(rows, width), low(rows, width),
        low(rows, width), low(rows, width), low(rows, 3 * width),
        wide(micro, 2 * all_pairs, atoms), low(micro, all_pairs, 2 * atoms),
        wide(micro, atoms, atoms), wide(micro, atoms, atoms), wide(micro, atoms, atoms),
        low(width, atoms), wide(width, atoms), low(8, atoms, 2 * atoms), low(width, rows),
        low(rows, width), low(*win.shape), low(*wout.shape), low(*wup.shape), low(*wdown.shape),
        wide(4, width), wide(heads, DEPTH), low(heads, DEPTH), sems(6),
    ] + [sems(micro)] * 4
    if chips:
        scratch += [
            low(chips, share, parts * width), low(chips + 1, share, parts * width),
            wide(8, width), wide(8, width), wide(chips, 8, 2 * LANES),
            wide(heads, DEPTH), wide(heads, DEPTH), wide(2, heads, DEPTH),
            wide(sections, heads, DEPTH), wide(chips, heads, DEPTH),
            sems(parts), sems(parts), sems(parts, chips), sems(parts, chips), sems(parts, chips), sems(parts, chips),
            sems(2), sems(chips), sems(chips), sems(2), sems(sections), sems(sections), sems(chips), sems(chips),
        ]
    params = dict(vmem_limit_bytes=60 * 2**20, has_side_effects=True)
    if sections > 1:
        params["collective_id"] = 0
    return pl.pallas_call(
        functools.partial(body, sections, chips, micro, atoms, heads, kern, spd, edges),
        out_shape=outs,
        in_specs=[smem, smem] + [vmem] * 8 + [pl.BlockSpec(memory_space=pl.ANY)] * 6,
        out_specs=[vmem] * len(outs),
        scratch_shapes=scratch,
        compiler_params=pltpu.CompilerParams(**params),
        name="sections",
    )(
        group, counts, jnp.transpose(posn, (1, 0, 2)), path_in, edge_in, norm_gain.T, norm_shift.T,
        kernel_proj.T, path_table.T, edge_table, tokens, cot, win, wout, wup, wdown,
    )


def finish_body(
    width, kern, spd, edges, sections,
    place, hidden, igrad, sums, norm, tab,
    hidden_o, igrad_o, in_o, out_o, up_o, down_o, gain_o, shift_o, kern_o, path_o, edge_o, tab_s, norm_s,
):
    hidden_o[...] = hidden[...]
    igrad_o[...] = igrad[...]
    for k, ref in enumerate((down_o, up_o, out_o)):
        ref[...] = sums[:, k * width : (k + 1) * width]
    in_o[...] = sums[:, 3 * width :]
    share = gain_o.shape[1]
    norm_s[...] = jnp.transpose(norm[...])
    rows = norm_s[pl.ds(pl.multiple_of(place[1], 8), share), :]
    rows = jnp.transpose(jnp.concatenate([rows, jnp.zeros((share, LANES - 8), F32)], axis=1))
    gain_o[...] = rows[0:2, :]
    shift_o[...] = rows[2:4, :]
    tab_s[...] = jnp.transpose(tab[...])
    start = 0
    for count, ref in ((kern, kern_o), (spd, path_o), (edges, edge_o)):
        own = count // sections
        ref[...] = tab_s[pl.ds(pl.multiple_of(start + place[0] * own, 8), own), :]
        start += count


def finish(hidden, igrad, sums, norm, tab, place, kern, spd, edges, sections):
    width, heads = hidden.shape[1], tab.shape[0]
    share = sums.shape[0]
    shape = jax.ShapeDtypeStruct
    vmem, smem = pl.BlockSpec(memory_space=pltpu.VMEM), pl.BlockSpec(memory_space=pltpu.SMEM)
    outs = (
        [shape(hidden.shape, BF16), shape(igrad.shape, BF16), shape((share, sums.shape[1] - 3 * width), F32)]
        + [shape((share, width), F32)] * 3
        + [shape((2, share), F32)] * 2
        + [shape((count // sections, heads), F32) for count in (kern, spd, edges)]
    )
    return pl.pallas_call(
        functools.partial(finish_body, width, kern, spd, edges, sections),
        out_shape=outs,
        in_specs=[smem] + [vmem] * 5,
        out_specs=[vmem] * len(outs),
        scratch_shapes=[pltpu.VMEM((DEPTH, heads), F32), pltpu.VMEM((2 * LANES, 8), F32)],
        compiler_params=pltpu.CompilerParams(vmem_limit_bytes=60 * 2**20),
        name="finish",
    )(place, hidden, igrad, sums, norm, tab)


def on_device(
    tokens, cotangent, positions, conformer_group, atom_counts, path_dist, edge_kind, attn_in, attn_out,
    ffn_up, ffn_down, norm_gain, norm_shift, kernel_proj, path_table, edge_table,
):
    sections, count = lax.axis_size("section"), lax.axis_size("dp")
    section, place = lax.axis_index("section"), lax.axis_index("dp")
    kern, heads = kernel_proj.shape
    spd, edges = path_table.shape[0], edge_table.shape[0]
    width = attn_out.shape[1]
    share = width // count
    chips = 4 if count == 8 and share % 16 == 0 and share <= LANES else 0
    hidden, igrad, *sums = layer_call(
        sections, chips, tokens, cotangent[0], positions, conformer_group, atom_counts, path_dist, edge_kind,
        attn_in[0], attn_out[0], ffn_up[0], ffn_down[0], norm_gain[0], norm_shift[0],
        kernel_proj, path_table, edge_table,
    )
    if chips:
        first = jnp.minimum(place * share // LANES, width // LANES - 2) * LANES
        where = jnp.stack([section, place * share - first]).astype(jnp.int32)
        outs = finish(hidden, igrad, *sums, where, kern, spd, edges, sections)
        norms = [jnp.transpose(o) for o in outs[6:8]]
        return tuple(o[None] for o in [*outs[:6], *norms]) + tuple(outs[8:])
    grads, g_norm, g_tab = sums
    split = lambda a, n: grads[0, 0, :, a * width : (a + n) * width]
    sums = [
        lax.psum_scatter(g, "dp", scatter_dimension=0, tiled=True).astype(F32)
        for g in (split(3, 3), split(2, 1), split(1, 1), split(0, 1))
    ]
    norm_sum = lax.psum(g_norm[:4], "dp").T
    norm_sum = lax.dynamic_slice_in_dim(norm_sum, place * share, share, 0)[None]
    tab_sum = lax.psum(g_tab, ("section", "dp"))
    tabs, start = [], 0
    for rows in (kern, spd, edges):
        own = rows // sections
        tabs.append(lax.dynamic_slice_in_dim(tab_sum, start + section * own, own, 0))
        start += rows
    return (hidden[None], igrad[None], *(g[None] for g in sums), norm_sum[:, :, :2], norm_sum[:, :, 2:], *tabs)


def solution(mesh):
    in_specs = (
        P("dp", None),
        P("section", "dp", None),
        P("dp", None, None),
        P("dp"),
        P("dp"),
        P("dp", None, None),
        P("dp", None, None),
        P("section", None, None),
        P("section", None, None),
        P("section", None, None),
        P("section", None, None),
        P("section", None, None),
        P("section", None, None),
        P(),
        P(),
        P(),
    )
    out_specs = (
        P("section", "dp", None),
        P("section", "dp", None),
        P("section", "dp", None),
        P("section", "dp", None),
        P("section", "dp", None),
        P("section", "dp", None),
        P("section", "dp", None),
        P("section", "dp", None),
        P("section", None),
        P("section", None),
        P("section", None),
    )
    return jax.shard_map(
        on_device, mesh=mesh, in_specs=in_specs, out_specs=out_specs, check_vma=False
    )
```

```python
import functools
import math

import jax
import jax.numpy as jnp
from jax import lax
from jax.experimental import pallas as pl
from jax.experimental.pallas import tpu as pltpu
from jax.sharding import PartitionSpec as P

F32, BF16 = jnp.float32, jnp.bfloat16
MESH = pl.DeviceIdType.MESH
EPS = 1e-05
NEG_BIG = -1e30
KERN_SPAN = 8.0
KERN_WIDTH = 0.4
LOG2E = math.log2(math.e)
LANES = 128
DEPTH = 256
LAG = 3
FORWARD_UNIT = 4
BACKWARD_UNIT = 4
BIAS_UNIT = 2
BLOCK = 64
TABLE_BLOCK = 16
SLOTS = 4


def dot(a, b):
    return jnp.dot(a, b, preferred_element_type=F32)


def dot_nt(a, b):
    return lax.dot_general(a, b, (((1,), (1,)), ((), ())), preferred_element_type=F32)


def rows_of(ref, m, n):
    return ref.at[pl.ds(pl.multiple_of(m * n, n), n), :]


def norm_parts(values):
    center = values - jnp.mean(values, axis=-1, keepdims=True)
    inv_std = lax.rsqrt(jnp.mean(center * center, axis=-1, keepdims=True) + EPS)
    return center * inv_std, inv_std


def norm_back(dy, xh, inv_std, gain):
    dxh = dy * gain
    return inv_std * (
        dxh
        - jnp.mean(dxh, axis=-1, keepdims=True)
        - xh * jnp.mean(dxh * xh, axis=-1, keepdims=True)
    )


def gelu(u):
    return 0.5 * u * (1.0 + jnp.tanh(0.7978845608028654 * (u + 0.044715 * u * u * u)))


def gelu_slope(u):
    sq = u * u
    t = jnp.tanh(0.7978845608028654 * (u + 0.044715 * sq * u))
    return 0.5 * (1.0 + t) + 0.5 * u * (1.0 - t * t) * (
        0.7978845608028654 * (1.0 + 3 * 0.044715 * sq)
    )


def pair_windows(head_dim):
    out = []
    for pair in range(8):
        lo, hi = pair * 2 * head_dim, pair * 2 * head_dim + 2 * head_dim - 1
        first = lo // LANES
        out.append((first, hi // LANES - first + 1, lo - first * LANES))
    return out


def in_turn(stages, count, unit):
    units = count // unit
    for step in range(units + len(stages) - 1):
        for late, stage in enumerate(stages):
            if 0 <= step - late < units:
                for pair in range((step - late) * unit, (step - late + 1) * unit):
                    stage(pair)


def both_heads(block, off, head_dim):
    lane = lax.broadcasted_iota(jnp.int32, (1, block.shape[1]), 1)
    one = ((lane >= off) & (lane < off + head_dim)).astype(F32).astype(BF16)
    two = ((lane >= off + head_dim) & (lane < off + 2 * head_dim)).astype(F32).astype(BF16)
    return jnp.concatenate([block * one, block * two], axis=0)


def both_columns(ref, first, tiles, off, head_dim):
    span, atoms = tiles * LANES, ref.shape[1]
    out = []
    for q in range(2):
        at = off + q * head_dim
        own = ref[first + at : first + at + head_dim, :]
        pieces = [jnp.zeros((at, atoms), F32)] * (at > 0) + [own]
        pieces += [jnp.zeros((span - at - head_dim, atoms), F32)] * (at + head_dim < span)
        out.append(jnp.concatenate(pieces, axis=0))
    return jnp.concatenate(out, axis=1).astype(BF16)


def tile_pairs(tile, windows):
    return [
        (pair, (first - tile) * LANES + off)
        for pair, (first, tiles, off) in enumerate(windows)
        if first <= tile < first + tiles
    ]


def features(dist8, path8, edge8, row, spd, edges, kern):
    atoms = dist8.shape[1]
    alpha = math.sqrt(0.5 * LOG2E) / KERN_WIDTH
    center = lax.broadcasted_iota(jnp.int32, (kern, atoms), 0).astype(F32) * (
        KERN_SPAN / kern * alpha
    )
    t = dist8[row : row + 1, :] * alpha - center
    gauss = jnp.exp2(-(t * t))
    path_id = lax.broadcasted_iota(jnp.int32, (spd, atoms), 0).astype(F32)
    edge_id = lax.broadcasted_iota(jnp.int32, (edges, atoms), 0).astype(F32)
    path = jnp.where(path8[row : row + 1, :] == path_id, 1.0, 0.0)
    edge = jnp.where(edge8[row : row + 1, :] == edge_id, 1.0, 0.0)
    rest = jnp.zeros((DEPTH - kern - spd - edges, atoms), F32)
    return jnp.concatenate([gauss, path, edge, rest], axis=0).astype(BF16)


def body(
    sections, chips, micro, atoms, heads, kern, spd, edges,
    group, counts, posn, path_in, edge_in, gains, shifts, kern_in, path_tab, edge_tab,
    tokens, cot_in, win_in, wout_in, wup_in, wdown_in,
    *refs,
):
    hidden, igrad, *refs = refs
    if chips:
        (sums, s_norm, s_tab, grads, g_norm, g_tab, *refs) = refs
    else:
        (grads, g_norm, g_tab, *refs) = refs
    (
        xs, grecv, a_s, qkv_s, o_s, mid_s, c_s, u_s, act_s, df_s, du_s, dat_s, dqkv_s,
        pairs, probs, dist_s, path_s, edge_s, tr_b, tr_f, tr_q, feats_s, ds_s, left_s,
        cot, win, wout, wup, wdown, norms, tab_f, tab, load_sem, fsend, frecv, bsend, brecv, *refs,
    ) = refs
    if chips:
        (
            core_in, line_in, norm_core, norm_sum, norm_in, tab_own, tab_core, tab_sum, tab_sec, tab_line,
            core_send, core_recv, line_send, line_recv, back_send, back_recv,
            nc_sem, nz_send, nz_recv, tc_sem, ts_send, ts_recv, tz_send, tz_recv,
        ) = refs
    width = wout.shape[0]
    head_dim = width // heads
    scale = 1.0 / math.sqrt(head_dim)
    windows = pair_windows(head_dim)
    s = lax.axis_index("section") if sections > 1 else 0
    d = lax.axis_index("dp") if sections > 1 else 0
    last = s == sections - 1

    z, c = d // 2, d % 2

    def to(sec, dp, src, dst, send, recv):
        return pltpu.make_async_remote_copy(
            src_ref=src, dst_ref=dst, send_sem=send, recv_sem=recv, device_id=(sec, dp), device_id_type=MESH
        )

    if chips:
        barrier = pltpu.get_barrier_semaphore()
        pl.semaphore_signal(barrier, inc=1, device_id=(s, 2 * z + 1 - c), device_id_type=MESH)
        for other in range(1, sections):
            pl.semaphore_signal(
                barrier, inc=1, device_id=((s + other) % sections, d), device_id_type=MESH
            )
        for other in range(1, chips):
            pl.semaphore_signal(
                barrier, inc=1, device_id=(s, (d + 2 * other) % (2 * chips)), device_id_type=MESH
            )
        pl.semaphore_wait(barrier, sections + chips - 1)
    elif sections > 1:
        barrier = pltpu.get_barrier_semaphore()

        @pl.when(s > 0)
        def _():
            pl.semaphore_signal(barrier, inc=1, device_id=(s - 1, d), device_id_type=MESH)

        @pl.when(s < sections - 1)
        def _():
            pl.semaphore_signal(barrier, inc=1, device_id=(s + 1, d), device_id_type=MESH)

        pl.semaphore_wait(barrier, jnp.where((s > 0) & (s < sections - 1), 2, 1))

    def forward_copy(m):
        return pltpu.make_async_remote_copy(
            src_ref=rows_of(hidden, m, atoms), dst_ref=rows_of(xs, m, atoms),
            send_sem=fsend.at[m], recv_sem=frecv.at[m],
            device_id=(jnp.minimum(s + 1, sections - 1), d), device_id_type=MESH,
        )

    def backward_copy(m):
        return pltpu.make_async_remote_copy(
            src_ref=rows_of(igrad, m, atoms), dst_ref=rows_of(grecv, m, atoms),
            send_sem=bsend.at[m], recv_sem=brecv.at[m],
            device_id=(jnp.maximum(s - 1, 0), d), device_id_type=MESH,
        )

    def head_rows(head):
        return slice(head * atoms, (head + 1) * atoms)

    pair_rows = head_rows

    loads = [(win_in, win), (wout_in, wout), (wup_in, wup), (wdown_in, wdown), (cot_in, cot)]

    def load(k):
        return pltpu.make_async_copy(*loads[k], load_sem.at[k])

    def load_tokens():
        return pltpu.make_async_copy(tokens, xs, load_sem.at[len(loads)])

    @pl.when(s == 0)
    def _():
        load_tokens().start()

    for k in range(len(loads)):
        load(k).start()

    norms[0:2, :] = gains[...].astype(F32)
    norms[2:4, :] = shifts[...].astype(F32)
    square = jnp.concatenate([edge_tab[...].astype(F32), jnp.zeros((heads, LANES - heads), F32)], axis=1)
    square = jnp.concatenate([square, jnp.zeros((LANES - edges, LANES), F32)], axis=0)
    tab_f[...] = jnp.zeros_like(tab_f)
    tab_f[:, 0:kern] = kern_in[...].astype(F32)
    tab_f[:, kern : kern + spd] = path_tab[...].astype(F32)
    tab_f[:, kern + spd : kern + spd + edges] = jnp.transpose(square)[:heads, :edges]
    tab[...] = tab_f[...].astype(BF16)

    @pl.when(last)
    def _():
        grecv[...] = jnp.zeros_like(grecv)

    g_norm[...] = jnp.zeros_like(g_norm)
    g_tab[...] = jnp.zeros_like(g_tab)

    def make_bias(unit):
        m, half = unit // 2, unit % 2
        mol = group[m]
        count = counts[mol]

        @pl.when(half == 0)
        def _():
            pos = jnp.concatenate([posn[axis, pl.ds(m, 1), :] for axis in range(3)], axis=0)
            pos_t = jnp.transpose(jnp.concatenate([pos, jnp.zeros((5, atoms), F32)], axis=0))
            total = jnp.zeros((atoms, atoms), F32)
            for axis in range(3):
                diff = pos_t[:, axis : axis + 1] - pos[axis : axis + 1, :]
                total = total + diff * diff
            dist_s[m] = jnp.sqrt(total)
            path_s[m] = jnp.transpose(path_in[mol].astype(F32))
            edge_s[m] = jnp.transpose(edge_in[mol].astype(F32))

        out_ref = pairs.at[m]

        @pl.loop(0, atoms // 2 // BLOCK)
        def _(step):
            t = half * (atoms // 2 // BLOCK) + step
            rows = pl.ds(pl.multiple_of(t * BLOCK, BLOCK), BLOCK)
            d8, p8, e8 = dist_s[m, rows, :], path_s[m, rows, :], edge_s[m, rows, :]

            def make(r):
                for q in range(2):
                    feats_s[r % SLOTS, :, q * atoms : (q + 1) * atoms] = features(
                        d8, p8, e8, 2 * r + q, spd, edges, kern
                    )

            def project(r):
                got = dot(tab[...], feats_s[r % SLOTS]) * LOG2E
                for q in range(2):
                    j = t * BLOCK + 2 * r + q
                    row = jnp.where(j < count, got[:, q * atoms : (q + 1) * atoms], NEG_BIG)
                    out_ref[pl.ds(j, heads, stride=atoms), :] = row

            in_turn((make, project), BLOCK // 2, BIAS_UNIT)

    tab_blocks = micro * (atoms // TABLE_BLOCK)

    def table_grads(block):
        m, t = block // (atoms // TABLE_BLOCK), block % (atoms // TABLE_BLOCK)
        in_ref = pairs.at[m]
        rows = pl.ds(pl.multiple_of(t * TABLE_BLOCK, TABLE_BLOCK), TABLE_BLOCK)
        d8, p8, e8 = dist_s[m, rows, :], path_s[m, rows, :], edge_s[m, rows, :]
        acc = [jnp.zeros((DEPTH, heads), F32)]

        def make(r):
            for q in range(2):
                feats_s[r % SLOTS, :, q * atoms : (q + 1) * atoms] = features(
                    d8, p8, e8, 2 * r + q, spd, edges, kern
                )

        def collect(r):
            halves = [
                in_ref[pl.ds(t * TABLE_BLOCK + 2 * r + q, heads, stride=atoms), :] for q in range(2)
            ]
            acc[0] += dot_nt(feats_s[r % SLOTS], jnp.concatenate(halves, axis=1).astype(BF16))

        in_turn((make, collect), TABLE_BLOCK // 2, BIAS_UNIT)
        g_tab[...] += acc[0]

    def turned(n):
        return grads[:, :, :, n * width : (n + 1) * width].reshape(width, width)

    def turn_weights():
        for n, (ref, col) in enumerate([(wdown, 0), (wup, 0), (wout, 0)] + [(win, q) for q in range(3)]):
            for k in range(width // 256):
                block = ref[k * 256 : (k + 1) * 256, col * width : (col + 1) * width].astype(F32)
                block = jnp.transpose(block).astype(BF16)
                first = n * width + k * 256
                grads[:, :, :, first : first + 256] = block.reshape(grads.shape[:3] + (256,))

    def forward(m):
        x = rows_of(xs, m, atoms)[...].astype(F32)
        xh, _ = norm_parts(x)
        a = (xh * norms[0:1, :] + norms[2:3, :]).astype(BF16)
        rows_of(a_s, m, atoms)[...] = a
        qkv = rows_of(qkv_s, m, atoms)
        for blk in range(3):
            got = dot(a, win[:, blk * width : (blk + 1) * width])
            qkv[:, blk * width : (blk + 1) * width] = got.astype(BF16)
            if blk == 0:
                tr_q[...] = jnp.transpose(got.astype(BF16).astype(F32))
            if blk == 2:
                tr_b[...] = jnp.transpose(got).astype(BF16)

        def scores(pair):
            g, (tile, tiles, off) = pair // 8, windows[pair % 8]
            lane = g * 16 * head_dim + tile * LANES
            qm = both_columns(tr_q, lane, tiles, off, head_dim)
            z = dot(qkv[:, width + lane : width + lane + tiles * LANES], qm) * (scale * LOG2E)
            for q in range(2):
                pairs[m, head_rows(2 * pair + q), :] += z[:, q * atoms : (q + 1) * atoms]

        def softmax(pair):
            for q in range(2):
                z = pairs[m, head_rows(2 * pair + q), :]
                e = jnp.exp2(z - jnp.max(z, axis=0, keepdims=True))
                p = (e * (1.0 / jnp.sum(e, axis=0, keepdims=True))).astype(BF16)
                probs[m, pair_rows(pair), q * atoms : (q + 1) * atoms] = p

        def attend(pair):
            first = pair * 2 * head_dim
            got = dot(tr_b[first : first + 2 * head_dim, :], probs[m, pair_rows(pair), :])
            tr_f[first : first + head_dim, :] = got[:head_dim, :atoms]
            tr_f[first + head_dim : first + 2 * head_dim, :] = got[head_dim:, atoms:]

        in_turn((scores, softmax, attend), heads // 2, FORWARD_UNIT)

        o = jnp.transpose(tr_f[...]).astype(BF16)
        rows_of(o_s, m, atoms)[...] = o
        mid = x + dot(o, wout[...])
        rows_of(mid_s, m, atoms)[...] = mid
        xh, _ = norm_parts(mid)
        c = (xh * norms[1:2, :] + norms[3:4, :]).astype(BF16)
        rows_of(c_s, m, atoms)[...] = c
        u = dot(c, wup[...])
        rows_of(u_s, m, atoms)[...] = u
        act = gelu(u).astype(BF16)
        rows_of(act_s, m, atoms)[...] = act
        rows_of(hidden, m, atoms)[...] = (mid + dot(act, wdown[...])).astype(BF16)

    def backward_ffn(m):
        grad = rows_of(cot, m, atoms)[...].astype(F32) + rows_of(grecv, m, atoms)[...].astype(F32)
        df = grad.astype(BF16)
        rows_of(df_s, m, atoms)[...] = df
        du = (dot(df, turned(0)) * gelu_slope(rows_of(u_s, m, atoms)[...])).astype(BF16)
        rows_of(du_s, m, atoms)[...] = du
        dc = dot(du, turned(1))
        xh, inv_std = norm_parts(rows_of(mid_s, m, atoms)[...])
        g_norm[1:2, :] += jnp.sum(dc * xh, axis=0, keepdims=True)
        g_norm[3:4, :] += jnp.sum(dc, axis=0, keepdims=True)
        dmid = grad + norm_back(dc, xh, inv_std, norms[1:2, :])
        rows_of(mid_s, m, atoms)[...] = dmid
        dat = dmid.astype(BF16)
        rows_of(dat_s, m, atoms)[...] = dat
        do = dot(dat, turned(2)).astype(BF16)
        rows_of(dqkv_s, m, atoms)[:, 0:width] = do
        tr_q[...] = jnp.transpose(do.astype(F32))

    def backward_attn(m):
        qkv = rows_of(qkv_s, m, atoms)
        dqkv = rows_of(dqkv_s, m, atoms)
        tr_b[...] = jnp.transpose(qkv[:, width : 2 * width].astype(F32)).astype(BF16)

        def slopes(pair):
            g, (tile, tiles, off) = pair // 8, windows[pair % 8]
            lane = g * 16 * head_dim + tile * LANES
            dom = both_columns(tr_q, lane, tiles, off, head_dim)
            dp = dot(qkv[:, 2 * width + lane : 2 * width + lane + tiles * LANES], dom)
            for q in range(2):
                pairs[m, head_rows(2 * pair + q), :] = dp[:, q * atoms : (q + 1) * atoms]

        def softmax_back(pair):
            for q in range(2):
                half = slice(q * atoms, (q + 1) * atoms)
                p = probs[m, pair_rows(pair), half].astype(F32)
                pd = p * pairs[m, head_rows(2 * pair + q), :]
                ds = pd - p * jnp.sum(pd, axis=0, keepdims=True)
                pairs[m, head_rows(2 * pair + q), :] = ds
                ds_s[pair, :, half] = ds.astype(BF16)

        def products(pair):
            first = pair * 2 * head_dim
            got = dot(tr_b[first : first + 2 * head_dim, :], ds_s[pair])
            tr_f[first : first + head_dim, :] = got[:head_dim, :atoms]
            tr_f[first + head_dim : first + 2 * head_dim, :] = got[head_dim:, atoms:]
            for tile in range(16 * head_dim // LANES):
                inside = tile_pairs(tile, windows)
                if inside[-1][0] != pair % 8:
                    continue
                lane = pair // 8 * 16 * head_dim + tile * LANES
                these = [(pair // 8 * 8 + one, off) for one, off in inside]
                left = jnp.concatenate([probs[m, pair_rows(one), :] for one, _ in these], axis=1)
                block = dqkv[:, lane : lane + LANES]
                right = jnp.concatenate([both_heads(block, off, head_dim) for _, off in these], axis=0)
                dqkv[:, 2 * width + lane : 2 * width + lane + LANES] = dot(left, right).astype(BF16)
                left = jnp.concatenate([ds_s[one] for one, _ in these], axis=1)
                block = qkv[:, lane : lane + LANES]
                right = jnp.concatenate([both_heads(block, off, head_dim) for _, off in these], axis=0)
                dqkv[:, width + lane : width + lane + LANES] = (dot(left, right) * scale).astype(BF16)

        in_turn((slopes, softmax_back, products), heads // 2, BACKWARD_UNIT)

        dqkv[:, 0:width] = (jnp.transpose(tr_f[...]) * scale).astype(BF16)
        da = sum(dot(dqkv[:, q * width : (q + 1) * width], turned(3 + q)) for q in range(3))
        xh, inv_std = norm_parts(rows_of(xs, m, atoms)[...].astype(F32))
        g_norm[0:1, :] += jnp.sum(da * xh, axis=0, keepdims=True)
        g_norm[2:3, :] += jnp.sum(da, axis=0, keepdims=True)
        out = rows_of(mid_s, m, atoms)[...] + norm_back(da, xh, inv_std, norms[0:1, :])
        rows_of(igrad, m, atoms)[...] = out.astype(BF16)

    parts = grads.shape[-1] // width
    share = grads.shape[2]

    def chunk(n):
        return pl.ds(n * width if isinstance(n, int) else pl.multiple_of(n * width, LANES), width)

    def core_copy(n):
        return to(
            s, 2 * z + 1 - c, grads.at[:, 1 - c, :, chunk(n)], core_in.at[:, :, chunk(n)],
            core_send.at[n], core_recv.at[n],
        )

    def right_copy(n, target):
        return to(
            s, jnp.minimum(d + 2, 2 * chips - 1), grads.at[target, c, :, chunk(n)],
            line_in.at[target + 1, :, chunk(n)], line_send.at[n, target], line_recv.at[n, target],
        )

    def left_copy(n, target):
        return to(
            s, jnp.maximum(d - 2, 0), grads.at[target, c, :, chunk(n)],
            line_in.at[target, :, chunk(n)], back_send.at[n, target], back_recv.at[n, target],
        )

    def add_in(target, slot, cols):
        both = grads[target, c, :, cols].astype(F32) + line_in[slot, :, cols].astype(F32)
        grads[target, c, :, cols] = both.astype(BF16)

    def settle(n):
        core_copy(n).wait_recv()
        for target in range(chips):
            both = grads[target, c, :, chunk(n)].astype(F32) + core_in[target, :, chunk(n)].astype(F32)
            grads[target, c, :, chunk(n)] = both.astype(BF16)

            @pl.when(z == target)
            def _():
                sums[:, chunk(n)] = both

        @pl.when(z == 0)
        def _():
            right_copy(n, chips - 1).start()

        @pl.when(z == chips - 1)
        def _():
            left_copy(n, 0).start()

    def norm_copy():
        return to(s, 2 * z + 1 - c, g_norm, norm_core, nc_sem.at[0], nc_sem.at[1])

    def weight_grads(lo, hi):
        jobs = [(act_s, df_s, 0), (c_s, du_s, 0), (o_s, dat_s, 0)] + [(a_s, dqkv_s, q) for q in range(3)]
        for n, (left, right, col) in list(enumerate(jobs))[lo:hi]:
            if col == 0:
                for m in range(micro):
                    part = left[m * atoms : (m + 1) * atoms, :].astype(F32)
                    left_s[:, m * atoms : (m + 1) * atoms] = jnp.transpose(part).astype(BF16)

            @pl.loop(0, width // 256)
            def _(q):
                cols = pl.ds(pl.multiple_of(col * width + q * 256, 256), 256)
                got = dot(left_s[...], right[:, cols]).astype(BF16)
                cols = pl.ds(pl.multiple_of(n * width + q * 256, 256), 256)
                grads[:, :, :, cols] = got.reshape(grads.shape[:3] + (256,))

            if chips:
                core_copy(n).start()
                if n:
                    settle(n - 1)

    def norm_window(dp):
        first = jnp.minimum(dp * share // LANES, width // LANES - 2)
        return pl.ds(pl.multiple_of(first * LANES, LANES), 2 * LANES)

    def norm_line(there, here):
        return to(
            s, 2 * there + c, norm_sum.at[:, norm_window(2 * there + c)], norm_in.at[here],
            nz_send.at[there], nz_recv.at[here],
        )

    def tab_copy():
        return to(s, 2 * z + 1 - c, tab_own, tab_core, tc_sem.at[0], tc_sem.at[1])

    def tab_section(there, here):
        return to(there, d, tab_sum.at[0], tab_sec.at[here], ts_send.at[there], ts_recv.at[here])

    def tab_chip(there, here):
        return to(s, 2 * there + c, tab_sum.at[1], tab_line.at[here], tz_send.at[there], tz_recv.at[here])

    def others(mine, count, act):
        for other in range(count):
            @pl.when(other != mine)
            def _():
                act(other)

    def reduce_all():
        norm_copy().wait_recv()
        norm_sum[...] = g_norm[...] + norm_core[...]
        norm_in[z] = norm_sum[:, norm_window(d)]
        others(z, chips, lambda o: norm_line(o, z).start())

        steps = (chips - 1) * parts
        tab_steps = steps - 6
        tab_each = -(-tab_blocks // tab_steps)

        def end_send(i, act):
            hop, n = i // parts, i % parts

            @pl.when(z == 0)
            def _():
                act(right_copy(n, chips - 1 - hop))

            @pl.when(z == chips - 1)
            def _():
                act(left_copy(n, hop))

        @pl.loop(0, steps)
        def _(i):
            @pl.when(i < tab_steps)
            def _():
                @pl.loop(i * tab_each, jnp.minimum((i + 1) * tab_each, tab_blocks))
                def _(block):
                    table_grads(block)

            @pl.when(i == tab_steps)
            def _():
                wide_tab = jnp.concatenate([g_tab[...], jnp.zeros((DEPTH, LANES - heads), F32)], axis=1)
                tab_own[...] = jnp.transpose(wide_tab)[:heads, :]
                tab_copy().start()

            @pl.when(i == tab_steps + 1)
            def _():
                tab_copy().wait_recv()
                tab_sum[0] = tab_own[...] + tab_core[...]
                tab_sec[s] = tab_sum[0]
                others(s, sections, lambda o: tab_section(o, s).start())

            @pl.when(i == tab_steps + 3)
            def _():
                others(s, sections, lambda o: tab_section(o, o).wait_recv())
                tab_sum[1] = sum(tab_sec[o] for o in range(sections))
                tab_line[z] = tab_sum[1]
                others(z, chips, lambda o: tab_chip(o, z).start())

            at_right, at_left = i - LAG * (z - 1), i - LAG * (chips - 2 - z)
            right, right_n = chips - 1 - at_right // parts, at_right % parts
            left, left_n = at_left // parts, at_left % parts

            @pl.when((z > 0) & (at_right >= 0) & (z <= right))
            def _():
                cols = chunk(right_n)
                right_copy(right_n, right).wait_recv()

                @pl.when(z < right)
                def _():
                    add_in(right, right + 1, cols)
                    right_copy(right_n, right).start()

                @pl.when(z == right)
                def _():
                    sums[:, cols] += line_in[right + 1, :, cols].astype(F32)

            @pl.when((z < chips - 1) & (at_left >= 0) & (z >= left))
            def _():
                cols = chunk(left_n)
                left_copy(left_n, left).wait_recv()

                @pl.when(z > left)
                def _():
                    add_in(left, left, cols)
                    left_copy(left_n, left).start()

                @pl.when(z == left)
                def _():
                    sums[:, cols] += line_in[left, :, cols].astype(F32)

            end_send(i, lambda copy: copy.wait_send())

            @pl.when(i + parts < steps)
            def _():
                end_send(i + parts, lambda copy: copy.start())

        others(z, chips, lambda o: norm_line(o, o).wait_recv())
        s_norm[...] = sum(norm_in[o] for o in range(chips))
        others(z, chips, lambda o: tab_chip(o, o).wait_recv())
        s_tab[...] = sum(tab_line[o] for o in range(chips))

        norm_copy().wait_send()
        tab_copy().wait_send()
        others(z, chips, lambda o: norm_line(o, z).wait_send())
        others(s, sections, lambda o: tab_section(o, s).wait_send())
        others(z, chips, lambda o: tab_chip(o, z).wait_send())

        @pl.loop(0, parts)
        def _(n):
            core_copy(n).wait_send()
            for target in range(chips):
                @pl.when((target > z) & (z > 0))
                def _():
                    right_copy(n, target).wait_send()

                @pl.when((target < z) & (z < chips - 1))
                def _():
                    left_copy(n, target).wait_send()

    total = 4 * micro

    @pl.loop(0, total)
    def _(t):
        ahead = jnp.where(last, micro, jnp.minimum(micro, jnp.where(s == 0, 1, 2 * s * s)))
        gap = micro - ahead
        r = t - 2 * ahead
        mixed = (r >= 0) & (r < 3 * gap)
        unit = jnp.where(r < 0, t, 2 * (ahead + r // 3) + r % 3 - 1)
        is_bias = (r < 0) | (mixed & (r % 3 != 0))
        is_fwd = jnp.where(
            last, (r >= 0) & (r % 2 == 0), (mixed & (r % 3 == 0)) | ((r >= 3 * gap) & (t < 3 * micro))
        )
        m_fwd = jnp.where(last, r // 2, jnp.where(mixed, r // 3, r - 2 * gap))
        is_back = jnp.where(last, (r >= 0) & (r % 2 == 1), t >= 3 * micro)
        m_back = jnp.where(last, r // 2, t - 3 * micro)
        @pl.when(is_bias)
        def _():
            make_bias(unit)

        @pl.when(is_fwd & (m_fwd == 0))
        def _():
            for k in range(len(loads) - 1):
                load(k).wait()

            @pl.when(s == 0)
            def _():
                load_tokens().wait()

        @pl.when(jnp.where(s >= 2, is_fwd & (m_fwd == 0), is_back & (m_back == 0)))
        def _():
            turn_weights()

        @pl.when(is_fwd)
        def _():
            if sections > 1:
                @pl.when(s > 0)
                def _():
                    forward_copy(m_fwd).wait_recv()

            forward(m_fwd)
            if sections > 1:
                @pl.when(jnp.logical_not(last))
                def _():
                    forward_copy(m_fwd).start()

        @pl.when(is_back)
        def _():
            @pl.when(m_back == 0)
            def _():
                load(len(loads) - 1).wait()

            if sections > 1:
                @pl.when(jnp.logical_not(last))
                def _():
                    backward_copy(m_back).wait_recv()

            backward_ffn(m_back)

            @pl.when((s == 0) & (m_back == micro - 1))
            def _():
                weight_grads(0, 3)

            backward_attn(m_back)
            if sections > 1:
                @pl.when(s > 0)
                def _():
                    backward_copy(m_back).start()

    @pl.when(s != 0)
    def _():
        weight_grads(0, 3)

    if chips:
        norm_copy().start()
    weight_grads(3, parts)
    if chips:
        settle(parts - 1)
    if chips:
        reduce_all()
    else:
        pl.loop(0, tab_blocks)(table_grads)

    if sections > 1:
        @pl.loop(0, micro)
        def _(m):
            @pl.when(jnp.logical_not(last))
            def _():
                forward_copy(m).wait_send()

            @pl.when(s > 0)
            def _():
                backward_copy(m).wait_send()


def layer_call(
    sections, chips, tokens, cot, posn, group, counts, path_in, edge_in, win, wout, wup, wdown,
    norm_gain, norm_shift, kernel_proj, path_table, edge_table,
):
    micro, _, atoms = posn.shape
    rows, width = tokens.shape
    kern, heads = kernel_proj.shape
    spd, edges = path_table.shape[0], edge_table.shape[0]
    shape = jax.ShapeDtypeStruct
    vmem, smem = pl.BlockSpec(memory_space=pltpu.VMEM), pl.BlockSpec(memory_space=pltpu.SMEM)
    low = lambda *dims: pltpu.VMEM(dims, BF16)
    wide = lambda *dims: pltpu.VMEM(dims, F32)
    sems = lambda *dims: pltpu.SemaphoreType.DMA(dims)
    parts = 3 + win.shape[1] // width
    all_pairs = heads // 2 * atoms
    outs = [shape((rows, width), BF16), shape((rows, width), BF16)]
    share = width // (2 * chips) if chips else width
    grads = (chips, 2, share, parts * width) if chips else (1, 1, width, parts * width)
    local = [(grads, BF16), ((8, width), F32), ((DEPTH, heads), F32)]
    scratch = []
    if chips:
        outs += [shape((share, parts * width), F32)]
        outs += [shape((8, 2 * LANES), F32), shape((heads, DEPTH), F32)]
        scratch += [pltpu.VMEM(dims, kind) for dims, kind in local]
    else:
        outs += [shape(dims, kind) for dims, kind in local]
    scratch += [
        low(rows, width), low(rows, width), low(rows, width), low(rows, 3 * width), low(rows, width),
        wide(rows, width), low(rows, width), wide(rows, width), low(rows, width), low(rows, width),
        low(rows, width), low(rows, width), low(rows, 3 * width),
        wide(micro, 2 * all_pairs, atoms), low(micro, all_pairs, 2 * atoms),
        wide(micro, atoms, atoms), wide(micro, atoms, atoms), wide(micro, atoms, atoms),
        low(width, atoms), wide(width, atoms), wide(width, atoms), low(SLOTS, DEPTH, 2 * atoms), low(heads // 2, atoms, 2 * atoms), low(width, rows),
        low(rows, width), low(*win.shape), low(*wout.shape), low(*wup.shape), low(*wdown.shape),
        wide(4, width), wide(heads, DEPTH), low(heads, DEPTH), sems(6),
    ] + [sems(micro)] * 4
    if chips:
        scratch += [
            low(chips, share, parts * width), low(chips + 1, share, parts * width),
            wide(8, width), wide(8, width), wide(chips, 8, 2 * LANES),
            wide(heads, DEPTH), wide(heads, DEPTH), wide(2, heads, DEPTH),
            wide(sections, heads, DEPTH), wide(chips, heads, DEPTH),
            sems(parts), sems(parts), sems(parts, chips), sems(parts, chips), sems(parts, chips), sems(parts, chips),
            sems(2), sems(chips), sems(chips), sems(2), sems(sections), sems(sections), sems(chips), sems(chips),
        ]
    params = dict(vmem_limit_bytes=60 * 2**20, has_side_effects=True)
    if sections > 1:
        params["collective_id"] = 0
    return pl.pallas_call(
        functools.partial(body, sections, chips, micro, atoms, heads, kern, spd, edges),
        out_shape=outs,
        in_specs=[smem, smem] + [vmem] * 8 + [pl.BlockSpec(memory_space=pl.ANY)] * 6,
        out_specs=[vmem] * len(outs),
        scratch_shapes=scratch,
        compiler_params=pltpu.CompilerParams(**params),
        name="sections",
    )(
        group, counts, jnp.transpose(posn, (1, 0, 2)), path_in, edge_in, norm_gain.T, norm_shift.T,
        kernel_proj.T, path_table.T, edge_table, tokens, cot, win, wout, wup, wdown,
    )


def finish_body(
    width, kern, spd, edges, sections,
    place, hidden, igrad, sums, norm, tab,
    hidden_o, igrad_o, in_o, out_o, up_o, down_o, gain_o, shift_o, kern_o, path_o, edge_o, tab_s, norm_s,
):
    hidden_o[...] = hidden[...]
    igrad_o[...] = igrad[...]
    for k, ref in enumerate((down_o, up_o, out_o)):
        ref[...] = sums[:, k * width : (k + 1) * width]
    in_o[...] = sums[:, 3 * width :]
    share = gain_o.shape[1]
    norm_s[...] = jnp.transpose(norm[...])
    rows = norm_s[pl.ds(pl.multiple_of(place[1], 8), share), :]
    rows = jnp.transpose(jnp.concatenate([rows, jnp.zeros((share, LANES - 8), F32)], axis=1))
    gain_o[...] = rows[0:2, :]
    shift_o[...] = rows[2:4, :]
    tab_s[...] = jnp.transpose(tab[...])
    start = 0
    for count, ref in ((kern, kern_o), (spd, path_o), (edges, edge_o)):
        own = count // sections
        ref[...] = tab_s[pl.ds(pl.multiple_of(start + place[0] * own, 8), own), :]
        start += count


def finish(hidden, igrad, sums, norm, tab, place, kern, spd, edges, sections):
    width, heads = hidden.shape[1], tab.shape[0]
    share = sums.shape[0]
    shape = jax.ShapeDtypeStruct
    vmem, smem = pl.BlockSpec(memory_space=pltpu.VMEM), pl.BlockSpec(memory_space=pltpu.SMEM)
    outs = (
        [shape(hidden.shape, BF16), shape(igrad.shape, BF16), shape((share, sums.shape[1] - 3 * width), F32)]
        + [shape((share, width), F32)] * 3
        + [shape((2, share), F32)] * 2
        + [shape((count // sections, heads), F32) for count in (kern, spd, edges)]
    )
    return pl.pallas_call(
        functools.partial(finish_body, width, kern, spd, edges, sections),
        out_shape=outs,
        in_specs=[smem] + [vmem] * 5,
        out_specs=[vmem] * len(outs),
        scratch_shapes=[pltpu.VMEM((DEPTH, heads), F32), pltpu.VMEM((2 * LANES, 8), F32)],
        compiler_params=pltpu.CompilerParams(vmem_limit_bytes=60 * 2**20),
        name="finish",
    )(place, hidden, igrad, sums, norm, tab)


def on_device(
    tokens, cotangent, positions, conformer_group, atom_counts, path_dist, edge_kind, attn_in, attn_out,
    ffn_up, ffn_down, norm_gain, norm_shift, kernel_proj, path_table, edge_table,
):
    sections, count = lax.axis_size("section"), lax.axis_size("dp")
    section, place = lax.axis_index("section"), lax.axis_index("dp")
    kern, heads = kernel_proj.shape
    spd, edges = path_table.shape[0], edge_table.shape[0]
    width = attn_out.shape[1]
    share = width // count
    chips = 4 if count == 8 and share % 16 == 0 and share <= LANES else 0
    hidden, igrad, *sums = layer_call(
        sections, chips, tokens, cotangent[0], positions, conformer_group, atom_counts, path_dist, edge_kind,
        attn_in[0], attn_out[0], ffn_up[0], ffn_down[0], norm_gain[0], norm_shift[0],
        kernel_proj, path_table, edge_table,
    )
    if chips:
        first = jnp.minimum(place * share // LANES, width // LANES - 2) * LANES
        where = jnp.stack([section, place * share - first]).astype(jnp.int32)
        outs = finish(hidden, igrad, *sums, where, kern, spd, edges, sections)
        norms = [jnp.transpose(o) for o in outs[6:8]]
        return tuple(o[None] for o in [*outs[:6], *norms]) + tuple(outs[8:])
    grads, g_norm, g_tab = sums
    split = lambda a, n: grads[0, 0, :, a * width : (a + n) * width]
    sums = [
        lax.psum_scatter(g, "dp", scatter_dimension=0, tiled=True).astype(F32)
        for g in (split(3, 3), split(2, 1), split(1, 1), split(0, 1))
    ]
    norm_sum = lax.psum(g_norm[:4], "dp").T
    norm_sum = lax.dynamic_slice_in_dim(norm_sum, place * share, share, 0)[None]
    tab_sum = lax.psum(g_tab, ("section", "dp"))
    tabs, start = [], 0
    for rows in (kern, spd, edges):
        own = rows // sections
        tabs.append(lax.dynamic_slice_in_dim(tab_sum, start + section * own, own, 0))
        start += rows
    return (hidden[None], igrad[None], *(g[None] for g in sums), norm_sum[:, :, :2], norm_sum[:, :, 2:], *tabs)


def solution(mesh):
    in_specs = (
        P("dp", None),
        P("section", "dp", None),
        P("dp", None, None),
        P("dp"),
        P("dp"),
        P("dp", None, None),
        P("dp", None, None),
        P("section", None, None),
        P("section", None, None),
        P("section", None, None),
        P("section", None, None),
        P("section", None, None),
        P("section", None, None),
        P(),
        P(),
        P(),
    )
    out_specs = (
        P("section", "dp", None),
        P("section", "dp", None),
        P("section", "dp", None),
        P("section", "dp", None),
        P("section", "dp", None),
        P("section", "dp", None),
        P("section", "dp", None),
        P("section", "dp", None),
        P("section", None),
        P("section", None),
        P("section", None),
    )
    return jax.shard_map(
        on_device, mesh=mesh, in_specs=in_specs, out_specs=out_specs, check_vma=False
    )
```

```python
import functools
import math

import jax
import jax.numpy as jnp
from jax import lax
from jax.experimental import pallas as pl
from jax.experimental.pallas import tpu as pltpu
from jax.sharding import PartitionSpec as P

F32, BF16 = jnp.float32, jnp.bfloat16
MESH = pl.DeviceIdType.MESH
EPS = 1e-05
NEG_BIG = -1e30
KERN_SPAN = 8.0
KERN_WIDTH = 0.4
LOG2E = math.log2(math.e)
LANES = 128
DEPTH = 256
LAG = 3
FORWARD_UNIT = 4
BACKWARD_UNIT = 4
BIAS_UNIT = 2
BLOCK = 64
TABLE_BLOCK = 16
SLOTS = 4


def dot(a, b):
    return jnp.dot(a, b, preferred_element_type=F32)


def dot_nt(a, b):
    return lax.dot_general(a, b, (((1,), (1,)), ((), ())), preferred_element_type=F32)


def rows_of(ref, m, n):
    return ref.at[pl.ds(pl.multiple_of(m * n, n), n), :]


def norm_parts(values):
    center = values - jnp.mean(values, axis=-1, keepdims=True)
    inv_std = lax.rsqrt(jnp.mean(center * center, axis=-1, keepdims=True) + EPS)
    return center * inv_std, inv_std


def norm_back(dy, xh, inv_std, gain):
    dxh = dy * gain
    return inv_std * (
        dxh
        - jnp.mean(dxh, axis=-1, keepdims=True)
        - xh * jnp.mean(dxh * xh, axis=-1, keepdims=True)
    )


def gelu(u):
    return 0.5 * u * (1.0 + jnp.tanh(0.7978845608028654 * (u + 0.044715 * u * u * u)))


def gelu_slope(u):
    sq = u * u
    t = jnp.tanh(0.7978845608028654 * (u + 0.044715 * sq * u))
    return 0.5 * (1.0 + t) + 0.5 * u * (1.0 - t * t) * (
        0.7978845608028654 * (1.0 + 3 * 0.044715 * sq)
    )


def pair_windows(head_dim):
    out = []
    for pair in range(8):
        lo, hi = pair * 2 * head_dim, pair * 2 * head_dim + 2 * head_dim - 1
        first = lo // LANES
        out.append((first, hi // LANES - first + 1, lo - first * LANES))
    return out


def in_turn(stages, count, unit):
    units = count // unit
    for step in range(units + len(stages) - 1):
        for late, stage in enumerate(stages):
            if 0 <= step - late < units:
                for pair in range((step - late) * unit, (step - late + 1) * unit):
                    stage(pair)


def both_heads(block, off, head_dim):
    lane = lax.broadcasted_iota(jnp.int32, (1, block.shape[1]), 1)
    one = ((lane >= off) & (lane < off + head_dim)).astype(F32).astype(BF16)
    two = ((lane >= off + head_dim) & (lane < off + 2 * head_dim)).astype(F32).astype(BF16)
    return jnp.concatenate([block * one, block * two], axis=0)


def both_columns(ref, first, tiles, off, head_dim):
    span, atoms = tiles * LANES, ref.shape[1]
    out = []
    for q in range(2):
        at = off + q * head_dim
        own = ref[first + at : first + at + head_dim, :]
        pieces = [jnp.zeros((at, atoms), F32)] * (at > 0) + [own]
        pieces += [jnp.zeros((span - at - head_dim, atoms), F32)] * (at + head_dim < span)
        out.append(jnp.concatenate(pieces, axis=0))
    return jnp.concatenate(out, axis=1).astype(BF16)


def tile_pairs(tile, windows):
    return [
        (pair, (first - tile) * LANES + off)
        for pair, (first, tiles, off) in enumerate(windows)
        if first <= tile < first + tiles
    ]


def features(dist8, path8, edge8, row, spd, edges, kern):
    atoms = dist8.shape[1]
    alpha = math.sqrt(0.5 * LOG2E) / KERN_WIDTH
    center = lax.broadcasted_iota(jnp.int32, (kern, atoms), 0).astype(F32) * (
        KERN_SPAN / kern * alpha
    )
    t = dist8[row : row + 1, :] * alpha - center
    gauss = jnp.exp2(-(t * t))
    path_id = lax.broadcasted_iota(jnp.int32, (spd, atoms), 0).astype(F32)
    edge_id = lax.broadcasted_iota(jnp.int32, (edges, atoms), 0).astype(F32)
    path = jnp.where(path8[row : row + 1, :] == path_id, 1.0, 0.0)
    edge = jnp.where(edge8[row : row + 1, :] == edge_id, 1.0, 0.0)
    rest = jnp.zeros((DEPTH - kern - spd - edges, atoms), F32)
    return jnp.concatenate([gauss, path, edge, rest], axis=0).astype(BF16)


def body(
    sections, chips, micro, atoms, heads, kern, spd, edges,
    group, counts, posn, path_in, edge_in, gains, shifts, kern_in, path_tab, edge_tab,
    tokens, cot_in, win_in, wout_in, wup_in, wdown_in,
    *refs,
):
    hidden, igrad, *refs = refs
    if chips:
        (sums, s_norm, s_tab, grads, g_norm, g_tab, *refs) = refs
    else:
        (grads, g_norm, g_tab, *refs) = refs
    (
        xs, grecv, a_s, qkv_s, o_s, mid_s, c_s, u_s, act_s, df_s, du_s, dat_s, dqkv_s,
        pairs, probs, dist_s, path_s, edge_s, tr_b, tr_f, tr_q, feats_s, ds_s,
        cot, win, wout, wup, wdown, norms, tab_f, tab, load_sem, fsend, frecv, bsend, brecv, *refs,
    ) = refs
    if chips:
        (
            core_in, line_in, norm_core, norm_sum, norm_in, tab_own, tab_core, tab_sum, tab_sec, tab_line,
            core_send, core_recv, line_send, line_recv, back_send, back_recv,
            nc_sem, nz_send, nz_recv, tc_sem, ts_send, ts_recv, tz_send, tz_recv,
            guest_in, guest_line, guest_low, gl_send, gl_recv, gb_send, gb_recv, guest_sem,
        ) = refs
    width = wout.shape[0]
    head_dim = width // heads
    scale = 1.0 / math.sqrt(head_dim)
    windows = pair_windows(head_dim)
    s = lax.axis_index("section") if sections > 1 else 0
    d = lax.axis_index("dp") if sections > 1 else 0
    last = s == sections - 1

    z, c = d // 2, d % 2

    def to(sec, dp, src, dst, send, recv):
        return pltpu.make_async_remote_copy(
            src_ref=src, dst_ref=dst, send_sem=send, recv_sem=recv, device_id=(sec, dp), device_id_type=MESH
        )

    if chips:
        barrier = pltpu.get_barrier_semaphore()
        pl.semaphore_signal(barrier, inc=1, device_id=(s, 2 * z + 1 - c), device_id_type=MESH)
        for other in range(1, sections):
            pl.semaphore_signal(
                barrier, inc=1, device_id=((s + other) % sections, d), device_id_type=MESH
            )
        for other in range(1, chips):
            pl.semaphore_signal(
                barrier, inc=1, device_id=(s, (d + 2 * other) % (2 * chips)), device_id_type=MESH
            )
        pl.semaphore_wait(barrier, sections + chips - 1)
    elif sections > 1:
        barrier = pltpu.get_barrier_semaphore()

        @pl.when(s > 0)
        def _():
            pl.semaphore_signal(barrier, inc=1, device_id=(s - 1, d), device_id_type=MESH)

        @pl.when(s < sections - 1)
        def _():
            pl.semaphore_signal(barrier, inc=1, device_id=(s + 1, d), device_id_type=MESH)

        pl.semaphore_wait(barrier, jnp.where((s > 0) & (s < sections - 1), 2, 1))

    def forward_copy(m):
        return pltpu.make_async_remote_copy(
            src_ref=rows_of(hidden, m, atoms), dst_ref=rows_of(xs, m, atoms),
            send_sem=fsend.at[m], recv_sem=frecv.at[m],
            device_id=(jnp.minimum(s + 1, sections - 1), d), device_id_type=MESH,
        )

    def backward_copy(m):
        return pltpu.make_async_remote_copy(
            src_ref=rows_of(igrad, m, atoms), dst_ref=rows_of(grecv, m, atoms),
            send_sem=bsend.at[m], recv_sem=brecv.at[m],
            device_id=(jnp.maximum(s - 1, 0), d), device_id_type=MESH,
        )

    def head_rows(head):
        return slice(head * atoms, (head + 1) * atoms)

    pair_rows = head_rows

    loads = [(win_in, win), (wout_in, wout), (wup_in, wup), (wdown_in, wdown), (cot_in, cot)]

    def load(k):
        return pltpu.make_async_copy(*loads[k], load_sem.at[k])

    def load_tokens():
        return pltpu.make_async_copy(tokens, xs, load_sem.at[len(loads)])

    @pl.when(s == 0)
    def _():
        load_tokens().start()

    for k in range(len(loads)):
        load(k).start()

    norms[0:2, :] = gains[...].astype(F32)
    norms[2:4, :] = shifts[...].astype(F32)
    square = jnp.concatenate([edge_tab[...].astype(F32), jnp.zeros((heads, LANES - heads), F32)], axis=1)
    square = jnp.concatenate([square, jnp.zeros((LANES - edges, LANES), F32)], axis=0)
    tab_f[...] = jnp.zeros_like(tab_f)
    tab_f[:, 0:kern] = kern_in[...].astype(F32)
    tab_f[:, kern : kern + spd] = path_tab[...].astype(F32)
    tab_f[:, kern + spd : kern + spd + edges] = jnp.transpose(square)[:heads, :edges]
    tab[...] = tab_f[...].astype(BF16)

    @pl.when(last)
    def _():
        grecv[...] = jnp.zeros_like(grecv)

    g_norm[...] = jnp.zeros_like(g_norm)
    g_tab[...] = jnp.zeros_like(g_tab)

    def make_bias(unit):
        m, half = unit // 2, unit % 2
        mol = group[m]
        count = counts[mol]

        @pl.when(half == 0)
        def _():
            pos = jnp.concatenate([posn[axis, pl.ds(m, 1), :] for axis in range(3)], axis=0)
            pos_t = jnp.transpose(jnp.concatenate([pos, jnp.zeros((5, atoms), F32)], axis=0))
            total = jnp.zeros((atoms, atoms), F32)
            for axis in range(3):
                diff = pos_t[:, axis : axis + 1] - pos[axis : axis + 1, :]
                total = total + diff * diff
            dist_s[m] = jnp.sqrt(total)
            path_s[m] = jnp.transpose(path_in[mol].astype(F32))
            edge_s[m] = jnp.transpose(edge_in[mol].astype(F32))

        out_ref = pairs.at[m]

        @pl.loop(0, atoms // 2 // BLOCK)
        def _(step):
            t = half * (atoms // 2 // BLOCK) + step
            rows = pl.ds(pl.multiple_of(t * BLOCK, BLOCK), BLOCK)
            d8, p8, e8 = dist_s[m, rows, :], path_s[m, rows, :], edge_s[m, rows, :]

            def make(r):
                for q in range(2):
                    feats_s[r % SLOTS, :, q * atoms : (q + 1) * atoms] = features(
                        d8, p8, e8, 2 * r + q, spd, edges, kern
                    )

            def project(r):
                got = dot(tab[...], feats_s[r % SLOTS]) * LOG2E
                for q in range(2):
                    j = t * BLOCK + 2 * r + q
                    row = jnp.where(j < count, got[:, q * atoms : (q + 1) * atoms], NEG_BIG)
                    out_ref[pl.ds(j, heads, stride=atoms), :] = row

            in_turn((make, project), BLOCK // 2, BIAS_UNIT)

    tab_blocks = micro * (atoms // TABLE_BLOCK)

    def table_grads(block):
        m, t = block // (atoms // TABLE_BLOCK), block % (atoms // TABLE_BLOCK)
        in_ref = pairs.at[m]
        rows = pl.ds(pl.multiple_of(t * TABLE_BLOCK, TABLE_BLOCK), TABLE_BLOCK)
        d8, p8, e8 = dist_s[m, rows, :], path_s[m, rows, :], edge_s[m, rows, :]
        acc = [jnp.zeros((DEPTH, heads), F32)]

        def make(r):
            for q in range(2):
                feats_s[r % SLOTS, :, q * atoms : (q + 1) * atoms] = features(
                    d8, p8, e8, 2 * r + q, spd, edges, kern
                )

        def collect(r):
            halves = [
                in_ref[pl.ds(t * TABLE_BLOCK + 2 * r + q, heads, stride=atoms), :] for q in range(2)
            ]
            acc[0] += dot_nt(feats_s[r % SLOTS], jnp.concatenate(halves, axis=1).astype(BF16))

        in_turn((make, collect), TABLE_BLOCK // 2, BIAS_UNIT)
        g_tab[...] += acc[0]

    def turned(n):
        return grads[:, :, :, n * width : (n + 1) * width].reshape(width, width)

    def turn_weights():
        for n, (ref, col) in enumerate([(wdown, 0), (wup, 0), (wout, 0)] + [(win, q) for q in range(3)]):
            for k in range(width // 256):
                block = ref[k * 256 : (k + 1) * 256, col * width : (col + 1) * width].astype(F32)
                block = jnp.transpose(block).astype(BF16)
                first = n * width + k * 256
                grads[:, :, :, first : first + 256] = block.reshape(grads.shape[:3] + (256,))

    def forward(m):
        x = rows_of(xs, m, atoms)[...].astype(F32)
        xh, _ = norm_parts(x)
        a = (xh * norms[0:1, :] + norms[2:3, :]).astype(BF16)
        rows_of(a_s, m, atoms)[...] = a
        qkv = rows_of(qkv_s, m, atoms)
        for blk in range(3):
            got = dot(a, win[:, blk * width : (blk + 1) * width])
            qkv[:, blk * width : (blk + 1) * width] = got.astype(BF16)
            if blk == 0:
                tr_q[...] = jnp.transpose(got.astype(BF16).astype(F32))
            if blk == 2:
                tr_b[...] = jnp.transpose(got).astype(BF16)

        def scores(pair):
            g, (tile, tiles, off) = pair // 8, windows[pair % 8]
            lane = g * 16 * head_dim + tile * LANES
            qm = both_columns(tr_q, lane, tiles, off, head_dim)
            z = dot(qkv[:, width + lane : width + lane + tiles * LANES], qm) * (scale * LOG2E)
            for q in range(2):
                pairs[m, head_rows(2 * pair + q), :] += z[:, q * atoms : (q + 1) * atoms]

        def softmax(pair):
            for q in range(2):
                z = pairs[m, head_rows(2 * pair + q), :]
                e = jnp.exp2(z - jnp.max(z, axis=0, keepdims=True))
                p = (e * (1.0 / jnp.sum(e, axis=0, keepdims=True))).astype(BF16)
                probs[m, pair_rows(pair), q * atoms : (q + 1) * atoms] = p

        def attend(pair):
            first = pair * 2 * head_dim
            got = dot(tr_b[first : first + 2 * head_dim, :], probs[m, pair_rows(pair), :])
            tr_f[first : first + head_dim, :] = got[:head_dim, :atoms]
            tr_f[first + head_dim : first + 2 * head_dim, :] = got[head_dim:, atoms:]

        in_turn((scores, softmax, attend), heads // 2, FORWARD_UNIT)

        o = jnp.transpose(tr_f[...]).astype(BF16)
        rows_of(o_s, m, atoms)[...] = o
        mid = x + dot(o, wout[...])
        rows_of(mid_s, m, atoms)[...] = mid
        xh, _ = norm_parts(mid)
        c = (xh * norms[1:2, :] + norms[3:4, :]).astype(BF16)
        rows_of(c_s, m, atoms)[...] = c
        u = dot(c, wup[...])
        rows_of(u_s, m, atoms)[...] = u
        act = gelu(u).astype(BF16)
        rows_of(act_s, m, atoms)[...] = act
        rows_of(hidden, m, atoms)[...] = (mid + dot(act, wdown[...])).astype(BF16)

    def backward_ffn(m):
        grad = rows_of(cot, m, atoms)[...].astype(F32) + rows_of(grecv, m, atoms)[...].astype(F32)
        df = grad.astype(BF16)
        rows_of(df_s, m, atoms)[...] = df
        du = (dot(df, turned(0)) * gelu_slope(rows_of(u_s, m, atoms)[...])).astype(BF16)
        rows_of(du_s, m, atoms)[...] = du
        dc = dot(du, turned(1))
        xh, inv_std = norm_parts(rows_of(mid_s, m, atoms)[...])
        g_norm[1:2, :] += jnp.sum(dc * xh, axis=0, keepdims=True)
        g_norm[3:4, :] += jnp.sum(dc, axis=0, keepdims=True)
        dmid = grad + norm_back(dc, xh, inv_std, norms[1:2, :])
        rows_of(mid_s, m, atoms)[...] = dmid
        dat = dmid.astype(BF16)
        rows_of(dat_s, m, atoms)[...] = dat
        do = dot(dat, turned(2)).astype(BF16)
        rows_of(dqkv_s, m, atoms)[:, 0:width] = do
        tr_q[...] = jnp.transpose(do.astype(F32))

    def backward_attn(m):
        qkv = rows_of(qkv_s, m, atoms)
        dqkv = rows_of(dqkv_s, m, atoms)
        tr_b[...] = jnp.transpose(qkv[:, width : 2 * width].astype(F32)).astype(BF16)

        def slopes(pair):
            g, (tile, tiles, off) = pair // 8, windows[pair % 8]
            lane = g * 16 * head_dim + tile * LANES
            dom = both_columns(tr_q, lane, tiles, off, head_dim)
            dp = dot(qkv[:, 2 * width + lane : 2 * width + lane + tiles * LANES], dom)
            for q in range(2):
                pairs[m, head_rows(2 * pair + q), :] = dp[:, q * atoms : (q + 1) * atoms]

        def softmax_back(pair):
            for q in range(2):
                half = slice(q * atoms, (q + 1) * atoms)
                p = probs[m, pair_rows(pair), half].astype(F32)
                pd = p * pairs[m, head_rows(2 * pair + q), :]
                ds = pd - p * jnp.sum(pd, axis=0, keepdims=True)
                pairs[m, head_rows(2 * pair + q), :] = ds
                ds_s[pair_rows(pair), half] = ds.astype(BF16)

        def products(pair):
            first = pair * 2 * head_dim
            got = dot(tr_b[first : first + 2 * head_dim, :], ds_s[pair_rows(pair), :])
            tr_f[first : first + head_dim, :] = got[:head_dim, :atoms]
            tr_f[first + head_dim : first + 2 * head_dim, :] = got[head_dim:, atoms:]
            for tile in range(16 * head_dim // LANES):
                inside = tile_pairs(tile, windows)
                if inside[-1][0] != pair % 8:
                    continue
                lane = pair // 8 * 16 * head_dim + tile * LANES
                these = [(pair // 8 * 8 + one, off) for one, off in inside]
                left = jnp.concatenate([probs[m, pair_rows(one), :] for one, _ in these], axis=1)
                block = dqkv[:, lane : lane + LANES]
                right = jnp.concatenate([both_heads(block, off, head_dim) for _, off in these], axis=0)
                dqkv[:, 2 * width + lane : 2 * width + lane + LANES] = dot(left, right).astype(BF16)
                left = jnp.concatenate([ds_s[pair_rows(one), :] for one, _ in these], axis=1)
                block = qkv[:, lane : lane + LANES]
                right = jnp.concatenate([both_heads(block, off, head_dim) for _, off in these], axis=0)
                dqkv[:, width + lane : width + lane + LANES] = (dot(left, right) * scale).astype(BF16)

        in_turn((slopes, softmax_back, products), heads // 2, BACKWARD_UNIT)

        dqkv[:, 0:width] = (jnp.transpose(tr_f[...]) * scale).astype(BF16)
        da = sum(dot(dqkv[:, q * width : (q + 1) * width], turned(3 + q)) for q in range(3))
        xh, inv_std = norm_parts(rows_of(xs, m, atoms)[...].astype(F32))
        g_norm[0:1, :] += jnp.sum(da * xh, axis=0, keepdims=True)
        g_norm[2:3, :] += jnp.sum(da, axis=0, keepdims=True)
        out = rows_of(mid_s, m, atoms)[...] + norm_back(da, xh, inv_std, norms[0:1, :])
        rows_of(igrad, m, atoms)[...] = out.astype(BF16)

    parts = grads.shape[-1] // width
    share = grads.shape[2]

    def chunk(n):
        return pl.ds(n * width if isinstance(n, int) else pl.multiple_of(n * width, LANES), width)

    def core_copy(n):
        return to(
            s, 2 * z + 1 - c, grads.at[:, 1 - c, :, chunk(n)], core_in.at[:, :, chunk(n)],
            core_send.at[n], core_recv.at[n],
        )

    class Line:
        def __init__(self, ref_of, into, out, sems, cols, count):
            self.ref_of, self.into, self.out, self.sems = ref_of, into, out, sems
            self.cols, self.count, self.steps = cols, count, (chips - 1) * count

        def right(self, n, target):
            return to(
                s, jnp.minimum(d + 2, 2 * chips - 1), self.ref_of(target).at[:, self.cols(n)],
                self.into.at[target + 1, :, self.cols(n)], self.sems[0].at[n, target], self.sems[1].at[n, target],
            )

        def left(self, n, target):
            return to(
                s, jnp.maximum(d - 2, 0), self.ref_of(target).at[:, self.cols(n)],
                self.into.at[target, :, self.cols(n)], self.sems[2].at[n, target], self.sems[3].at[n, target],
            )

        def end_copy(self, hop, n, act):
            @pl.when(z == 0)
            def _():
                act(self.right(n, chips - 1 - hop))

            @pl.when(z == chips - 1)
            def _():
                act(self.left(n, hop))

        def add_in(self, target, slot, cols):
            ref = self.ref_of(target)
            ref[:, cols] = (ref[:, cols].astype(F32) + self.into[slot, :, cols].astype(F32)).astype(BF16)

        def step(self, i):
            at_right, at_left = i - LAG * (z - 1), i - LAG * (chips - 2 - z)
            right, right_n = chips - 1 - at_right // self.count, at_right % self.count
            left, left_n = at_left // self.count, at_left % self.count

            @pl.when((z > 0) & (at_right >= 0) & (z <= right))
            def _():
                cols = self.cols(right_n)
                self.right(right_n, right).wait_recv()

                @pl.when(z < right)
                def _():
                    self.add_in(right, right + 1, cols)
                    self.right(right_n, right).start()

                @pl.when(z == right)
                def _():
                    self.out[:, cols] += self.into[right + 1, :, cols].astype(F32)

            @pl.when((z < chips - 1) & (at_left >= 0) & (z >= left))
            def _():
                cols = self.cols(left_n)
                self.left(left_n, left).wait_recv()

                @pl.when(z > left)
                def _():
                    self.add_in(left, left, cols)
                    self.left(left_n, left).start()

                @pl.when(z == left)
                def _():
                    self.out[:, cols] += self.into[left, :, cols].astype(F32)

            self.end_copy(i // self.count, i % self.count, lambda copy: copy.wait_send())

            @pl.when(i + self.count < self.steps)
            def _():
                self.end_copy(i // self.count + 1, i % self.count, lambda copy: copy.start())

        def drain(self, n):
            for target in range(chips):
                @pl.when((target > z) & (z > 0))
                def _():
                    self.right(n, target).wait_send()

                @pl.when((target < z) & (z < chips - 1))
                def _():
                    self.left(n, target).wait_send()

    donor, helper = s == 0, s == sections - 1
    own_parts = jnp.where(donor, parts - 1, parts)
    if chips:
        main = Line(
            lambda target: grads.at[target, c], line_in, sums, (line_send, line_recv, back_send, back_recv),
            chunk, own_parts,
        )

        def part_cols(n):
            return pl.ds(n * 2 * LANES if isinstance(n, int) else pl.multiple_of(n * 2 * LANES, LANES), 2 * LANES)

        guest_sum = mid_s.at[0:share, :]
        guest = Line(
            lambda target: guest_in.at[target], guest_line, guest_sum, (gl_send, gl_recv, gb_send, gb_recv),
            part_cols, width // (2 * LANES),
        )

    def guest_copy():
        return to(
            sections - 1, d, grads.at[:, c, :, chunk(parts - 1)], guest_in, guest_sem.at[0], guest_sem.at[1]
        )

    def result_copy():
        return to(0, d, guest_low, guest_low, guest_sem.at[2], guest_sem.at[3])

    def settle(n):
        core_copy(n).wait_recv()
        for target in range(chips):
            both = grads[target, c, :, chunk(n)].astype(F32) + core_in[target, :, chunk(n)].astype(F32)
            grads[target, c, :, chunk(n)] = both.astype(BF16)

            @pl.when(z == target)
            def _():
                sums[:, chunk(n)] = both

        if n < parts - 1:
            main.end_copy(0, n, lambda copy: copy.start())
        else:
            @pl.when(donor)
            def _():
                guest_copy().start()

            @pl.when(jnp.logical_not(donor))
            def _():
                main.end_copy(0, n, lambda copy: copy.start())

    def norm_copy():
        return to(s, 2 * z + 1 - c, g_norm, norm_core, nc_sem.at[0], nc_sem.at[1])

    def weight_grads(lo, hi):
        jobs = [(act_s, df_s, 0), (c_s, du_s, 0), (o_s, dat_s, 0)] + [(a_s, dqkv_s, q) for q in range(3)]
        for n, (left, right, col) in list(enumerate(jobs))[lo:hi]:
            if col == 0:
                for m in range(micro):
                    part = left[m * atoms : (m + 1) * atoms, :].astype(F32)
                    first = m // 2 * width
                    ds_s[first : first + width, m % 2 * atoms : (m % 2 + 1) * atoms] = jnp.transpose(
                        part
                    ).astype(BF16)

            @pl.loop(0, width // 256)
            def _(q):
                cols = pl.ds(pl.multiple_of(col * width + q * 256, 256), 256)
                turned_left = [ds_s[k * width : (k + 1) * width, :] for k in range(micro // 2)]
                got = dot(jnp.concatenate(turned_left, axis=1), right[:, cols]).astype(BF16)
                cols = pl.ds(pl.multiple_of(n * width + q * 256, 256), 256)
                grads[:, :, :, cols] = got.reshape(grads.shape[:3] + (256,))

            if chips:
                core_copy(n).start()
                if n:
                    settle(n - 1)

    def norm_window(dp):
        first = jnp.minimum(dp * share // LANES, width // LANES - 2)
        return pl.ds(pl.multiple_of(first * LANES, LANES), 2 * LANES)

    def norm_line(there, here):
        return to(
            s, 2 * there + c, norm_sum.at[:, norm_window(2 * there + c)], norm_in.at[here],
            nz_send.at[there], nz_recv.at[here],
        )

    def tab_copy():
        return to(s, 2 * z + 1 - c, tab_own, tab_core, tc_sem.at[0], tc_sem.at[1])

    def tab_section(there, here):
        return to(there, d, tab_sum.at[0], tab_sec.at[here], ts_send.at[there], ts_recv.at[here])

    def tab_chip(there, here):
        return to(s, 2 * there + c, tab_sum.at[1], tab_line.at[here], tz_send.at[there], tz_recv.at[here])

    def others(mine, count, act):
        for other in range(count):
            @pl.when(other != mine)
            def _():
                act(other)

    def reduce_all():
        norm_copy().wait_recv()
        norm_sum[...] = g_norm[...] + norm_core[...]
        norm_in[z] = norm_sum[:, norm_window(d)]
        others(z, chips, lambda o: norm_line(o, z).start())

        tab_steps = (chips - 1) * (parts - 1) - 6
        tab_each = -(-tab_blocks // tab_steps)

        def tab_over_chips():
            others(s, sections, lambda o: tab_section(o, o).wait_recv())
            tab_sum[1] = sum(tab_sec[o] for o in range(sections))
            tab_line[z] = tab_sum[1]
            others(z, chips, lambda o: tab_chip(o, z).start())

        @pl.loop(0, main.steps)
        def _(i):
            @pl.when(i < tab_steps)
            def _():
                @pl.loop(i * tab_each, jnp.minimum((i + 1) * tab_each, tab_blocks))
                def _(block):
                    table_grads(block)

            @pl.when(i == tab_steps)
            def _():
                wide_tab = jnp.concatenate([g_tab[...], jnp.zeros((DEPTH, LANES - heads), F32)], axis=1)
                tab_own[...] = jnp.transpose(wide_tab)[:heads, :]
                tab_copy().start()

            @pl.when(i == tab_steps + 1)
            def _():
                tab_copy().wait_recv()
                tab_sum[0] = tab_own[...] + tab_core[...]
                tab_sec[s] = tab_sum[0]
                others(s, sections, lambda o: tab_section(o, s).start())

            @pl.when((i == tab_steps + 3) & (s < 2))
            def _():
                tab_over_chips()

            main.step(i)

        @pl.when(helper)
        def _():
            guest_copy().wait_recv()
            guest_sum[...] = guest_in[z].astype(F32)
            for n in range(guest.count):
                guest.end_copy(0, n, lambda copy: copy.start())

            pl.loop(0, guest.steps)(guest.step)
            guest_low[...] = guest_sum[...].astype(BF16)
            result_copy().start()

        @pl.when(s >= 2)
        def _():
            tab_over_chips()

        others(z, chips, lambda o: norm_line(o, o).wait_recv())
        s_norm[...] = sum(norm_in[o] for o in range(chips))
        others(z, chips, lambda o: tab_chip(o, o).wait_recv())
        s_tab[...] = sum(tab_line[o] for o in range(chips))

        norm_copy().wait_send()
        tab_copy().wait_send()
        others(z, chips, lambda o: norm_line(o, z).wait_send())
        others(s, sections, lambda o: tab_section(o, s).wait_send())
        others(z, chips, lambda o: tab_chip(o, z).wait_send())

        @pl.loop(0, parts)
        def _(n):
            core_copy(n).wait_send()

            @pl.when(n < own_parts)
            def _():
                main.drain(n)

        @pl.when(helper)
        def _():
            pl.loop(0, guest.count)(guest.drain)
            result_copy().wait_send()

        @pl.when(donor)
        def _():
            guest_copy().wait_send()
            result_copy().wait_recv()
            sums[:, chunk(parts - 1)] = guest_low[...].astype(F32)

    total = 4 * micro

    @pl.loop(0, total)
    def _(t):
        ahead = jnp.where(last, micro, jnp.minimum(micro, jnp.where(s == 0, 1, 2 * s * s)))
        gap = micro - ahead
        r = t - 2 * ahead
        mixed = (r >= 0) & (r < 3 * gap)
        unit = jnp.where(r < 0, t, 2 * (ahead + r // 3) + r % 3 - 1)
        is_bias = (r < 0) | (mixed & (r % 3 != 0))
        is_fwd = jnp.where(
            last, (r >= 0) & (r % 2 == 0), (mixed & (r % 3 == 0)) | ((r >= 3 * gap) & (t < 3 * micro))
        )
        m_fwd = jnp.where(last, r // 2, jnp.where(mixed, r // 3, r - 2 * gap))
        is_back = jnp.where(last, (r >= 0) & (r % 2 == 1), t >= 3 * micro)
        m_back = jnp.where(last, r // 2, t - 3 * micro)
        @pl.when(is_bias)
        def _():
            make_bias(unit)

        @pl.when(is_fwd & (m_fwd == 0))
        def _():
            for k in range(len(loads) - 1):
                load(k).wait()

            @pl.when(s == 0)
            def _():
                load_tokens().wait()

        @pl.when(jnp.where(s >= 2, is_fwd & (m_fwd == 0), is_back & (m_back == 0)))
        def _():
            turn_weights()

        @pl.when(is_fwd)
        def _():
            if sections > 1:
                @pl.when(s > 0)
                def _():
                    forward_copy(m_fwd).wait_recv()

            forward(m_fwd)
            if sections > 1:
                @pl.when(jnp.logical_not(last))
                def _():
                    forward_copy(m_fwd).start()

        @pl.when(is_back)
        def _():
            @pl.when(m_back == 0)
            def _():
                load(len(loads) - 1).wait()

            if sections > 1:
                @pl.when(jnp.logical_not(last))
                def _():
                    backward_copy(m_back).wait_recv()

            backward_ffn(m_back)

            @pl.when((s == 0) & (m_back == micro - 1))
            def _():
                weight_grads(0, 3)

            backward_attn(m_back)
            if sections > 1:
                @pl.when(s > 0)
                def _():
                    backward_copy(m_back).start()

    @pl.when(s != 0)
    def _():
        weight_grads(0, 3)

    if chips:
        norm_copy().start()
    weight_grads(3, parts)
    if chips:
        settle(parts - 1)
    if chips:
        reduce_all()
    else:
        pl.loop(0, tab_blocks)(table_grads)

    if sections > 1:
        @pl.loop(0, micro)
        def _(m):
            @pl.when(jnp.logical_not(last))
            def _():
                forward_copy(m).wait_send()

            @pl.when(s > 0)
            def _():
                backward_copy(m).wait_send()


def layer_call(
    sections, chips, tokens, cot, posn, group, counts, path_in, edge_in, win, wout, wup, wdown,
    norm_gain, norm_shift, kernel_proj, path_table, edge_table,
):
    micro, _, atoms = posn.shape
    rows, width = tokens.shape
    kern, heads = kernel_proj.shape
    spd, edges = path_table.shape[0], edge_table.shape[0]
    shape = jax.ShapeDtypeStruct
    vmem, smem = pl.BlockSpec(memory_space=pltpu.VMEM), pl.BlockSpec(memory_space=pltpu.SMEM)
    low = lambda *dims: pltpu.VMEM(dims, BF16)
    wide = lambda *dims: pltpu.VMEM(dims, F32)
    sems = lambda *dims: pltpu.SemaphoreType.DMA(dims)
    parts = 3 + win.shape[1] // width
    all_pairs = heads // 2 * atoms
    outs = [shape((rows, width), BF16), shape((rows, width), BF16)]
    share = width // (2 * chips) if chips else width
    grads = (chips, 2, share, parts * width) if chips else (1, 1, width, parts * width)
    local = [(grads, BF16), ((8, width), F32), ((DEPTH, heads), F32)]
    scratch = []
    if chips:
        outs += [shape((share, parts * width), F32)]
        outs += [shape((8, 2 * LANES), F32), shape((heads, DEPTH), F32)]
        scratch += [pltpu.VMEM(dims, kind) for dims, kind in local]
    else:
        outs += [shape(dims, kind) for dims, kind in local]
    scratch += [
        low(rows, width), low(rows, width), low(rows, width), low(rows, 3 * width), low(rows, width),
        wide(rows, width), low(rows, width), wide(rows, width), low(rows, width), low(rows, width),
        low(rows, width), low(rows, width), low(rows, 3 * width),
        wide(micro, 2 * all_pairs, atoms), low(micro, all_pairs, 2 * atoms),
        wide(micro, atoms, atoms), wide(micro, atoms, atoms), wide(micro, atoms, atoms),
        low(width, atoms), wide(width, atoms), wide(width, atoms), low(SLOTS, DEPTH, 2 * atoms), low(all_pairs, 2 * atoms),
        low(rows, width), low(*win.shape), low(*wout.shape), low(*wup.shape), low(*wdown.shape),
        wide(4, width), wide(heads, DEPTH), low(heads, DEPTH), sems(6),
    ] + [sems(micro)] * 4
    if chips:
        scratch += [
            low(chips, share, parts * width), low(chips + 1, share, parts * width),
            wide(8, width), wide(8, width), wide(chips, 8, 2 * LANES),
            wide(heads, DEPTH), wide(heads, DEPTH), wide(2, heads, DEPTH),
            wide(sections, heads, DEPTH), wide(chips, heads, DEPTH),
            sems(parts), sems(parts), sems(parts, chips), sems(parts, chips), sems(parts, chips), sems(parts, chips),
            sems(2), sems(chips), sems(chips), sems(2), sems(sections), sems(sections), sems(chips), sems(chips),
            low(chips, share, width), low(chips + 1, share, width), low(share, width),
        ] + [sems(width // (2 * LANES), chips)] * 4 + [
            sems(4),
        ]
    params = dict(vmem_limit_bytes=60 * 2**20, has_side_effects=True)
    if sections > 1:
        params["collective_id"] = 0
    return pl.pallas_call(
        functools.partial(body, sections, chips, micro, atoms, heads, kern, spd, edges),
        out_shape=outs,
        in_specs=[smem, smem] + [vmem] * 8 + [pl.BlockSpec(memory_space=pl.ANY)] * 6,
        out_specs=[vmem] * len(outs),
        scratch_shapes=scratch,
        compiler_params=pltpu.CompilerParams(**params),
        name="sections",
    )(
        group, counts, jnp.transpose(posn, (1, 0, 2)), path_in, edge_in, norm_gain.T, norm_shift.T,
        kernel_proj.T, path_table.T, edge_table, tokens, cot, win, wout, wup, wdown,
    )


def finish_body(
    width, kern, spd, edges, sections,
    place, hidden, igrad, sums, norm, tab,
    hidden_o, igrad_o, in_o, out_o, up_o, down_o, gain_o, shift_o, kern_o, path_o, edge_o, tab_s, norm_s,
):
    hidden_o[...] = hidden[...]
    igrad_o[...] = igrad[...]
    for k, ref in enumerate((down_o, up_o, out_o)):
        ref[...] = sums[:, k * width : (k + 1) * width]
    in_o[...] = sums[:, 3 * width :]
    share = gain_o.shape[1]
    norm_s[...] = jnp.transpose(norm[...])
    rows = norm_s[pl.ds(pl.multiple_of(place[1], 8), share), :]
    rows = jnp.transpose(jnp.concatenate([rows, jnp.zeros((share, LANES - 8), F32)], axis=1))
    gain_o[...] = rows[0:2, :]
    shift_o[...] = rows[2:4, :]
    tab_s[...] = jnp.transpose(tab[...])
    start = 0
    for count, ref in ((kern, kern_o), (spd, path_o), (edges, edge_o)):
        own = count // sections
        ref[...] = tab_s[pl.ds(pl.multiple_of(start + place[0] * own, 8), own), :]
        start += count


def finish(hidden, igrad, sums, norm, tab, place, kern, spd, edges, sections):
    width, heads = hidden.shape[1], tab.shape[0]
    share = sums.shape[0]
    shape = jax.ShapeDtypeStruct
    vmem, smem = pl.BlockSpec(memory_space=pltpu.VMEM), pl.BlockSpec(memory_space=pltpu.SMEM)
    outs = (
        [shape(hidden.shape, BF16), shape(igrad.shape, BF16), shape((share, sums.shape[1] - 3 * width), F32)]
        + [shape((share, width), F32)] * 3
        + [shape((2, share), F32)] * 2
        + [shape((count // sections, heads), F32) for count in (kern, spd, edges)]
    )
    return pl.pallas_call(
        functools.partial(finish_body, width, kern, spd, edges, sections),
        out_shape=outs,
        in_specs=[smem] + [vmem] * 5,
        out_specs=[vmem] * len(outs),
        scratch_shapes=[pltpu.VMEM((DEPTH, heads), F32), pltpu.VMEM((2 * LANES, 8), F32)],
        compiler_params=pltpu.CompilerParams(vmem_limit_bytes=60 * 2**20),
        name="finish",
    )(place, hidden, igrad, sums, norm, tab)


def on_device(
    tokens, cotangent, positions, conformer_group, atom_counts, path_dist, edge_kind, attn_in, attn_out,
    ffn_up, ffn_down, norm_gain, norm_shift, kernel_proj, path_table, edge_table,
):
    sections, count = lax.axis_size("section"), lax.axis_size("dp")
    section, place = lax.axis_index("section"), lax.axis_index("dp")
    kern, heads = kernel_proj.shape
    spd, edges = path_table.shape[0], edge_table.shape[0]
    width = attn_out.shape[1]
    share = width // count
    chips = 4 if count == 8 and share % 16 == 0 and share <= LANES else 0
    hidden, igrad, *sums = layer_call(
        sections, chips, tokens, cotangent[0], positions, conformer_group, atom_counts, path_dist, edge_kind,
        attn_in[0], attn_out[0], ffn_up[0], ffn_down[0], norm_gain[0], norm_shift[0],
        kernel_proj, path_table, edge_table,
    )
    if chips:
        first = jnp.minimum(place * share // LANES, width // LANES - 2) * LANES
        where = jnp.stack([section, place * share - first]).astype(jnp.int32)
        outs = finish(hidden, igrad, *sums, where, kern, spd, edges, sections)
        norms = [jnp.transpose(o) for o in outs[6:8]]
        return tuple(o[None] for o in [*outs[:6], *norms]) + tuple(outs[8:])
    grads, g_norm, g_tab = sums
    split = lambda a, n: grads[0, 0, :, a * width : (a + n) * width]
    sums = [
        lax.psum_scatter(g, "dp", scatter_dimension=0, tiled=True).astype(F32)
        for g in (split(3, 3), split(2, 1), split(1, 1), split(0, 1))
    ]
    norm_sum = lax.psum(g_norm[:4], "dp").T
    norm_sum = lax.dynamic_slice_in_dim(norm_sum, place * share, share, 0)[None]
    tab_sum = lax.psum(g_tab, ("section", "dp"))
    tabs, start = [], 0
    for rows in (kern, spd, edges):
        own = rows // sections
        tabs.append(lax.dynamic_slice_in_dim(tab_sum, start + section * own, own, 0))
        start += rows
    return (hidden[None], igrad[None], *(g[None] for g in sums), norm_sum[:, :, :2], norm_sum[:, :, 2:], *tabs)


def solution(mesh):
    in_specs = (
        P("dp", None),
        P("section", "dp", None),
        P("dp", None, None),
        P("dp"),
        P("dp"),
        P("dp", None, None),
        P("dp", None, None),
        P("section", None, None),
        P("section", None, None),
        P("section", None, None),
        P("section", None, None),
        P("section", None, None),
        P("section", None, None),
        P(),
        P(),
        P(),
    )
    out_specs = (
        P("section", "dp", None),
        P("section", "dp", None),
        P("section", "dp", None),
        P("section", "dp", None),
        P("section", "dp", None),
        P("section", "dp", None),
        P("section", "dp", None),
        P("section", "dp", None),
        P("section", None),
        P("section", None),
        P("section", None),
    )
    return jax.shard_map(
        on_device, mesh=mesh, in_specs=in_specs, out_specs=out_specs, check_vma=False
    )
```

```python
import functools
import math

import jax
import jax.numpy as jnp
from jax import lax
from jax.experimental import pallas as pl
from jax.experimental.pallas import tpu as pltpu
from jax.sharding import PartitionSpec as P

F32, BF16 = jnp.float32, jnp.bfloat16
MESH = pl.DeviceIdType.MESH
EPS = 1e-05
NEG_BIG = -1e30
KERN_SPAN = 8.0
KERN_WIDTH = 0.4
LOG2E = math.log2(math.e)
LANES = 128
DEPTH = 256
LAG = 3
FORWARD_UNIT = 4
BACKWARD_UNIT = 4
BIAS_UNIT = 2
BLOCK = 64
TABLE_BLOCK = 16
SLOTS = 4


def dot(a, b):
    return jnp.dot(a, b, preferred_element_type=F32)


def dot_nt(a, b):
    return lax.dot_general(a, b, (((1,), (1,)), ((), ())), preferred_element_type=F32)


def rows_of(ref, m, n):
    return ref.at[pl.ds(pl.multiple_of(m * n, n), n), :]


def norm_parts(values):
    center = values - jnp.mean(values, axis=-1, keepdims=True)
    inv_std = lax.rsqrt(jnp.mean(center * center, axis=-1, keepdims=True) + EPS)
    return center * inv_std, inv_std


def norm_back(dy, xh, inv_std, gain):
    dxh = dy * gain
    return inv_std * (
        dxh
        - jnp.mean(dxh, axis=-1, keepdims=True)
        - xh * jnp.mean(dxh * xh, axis=-1, keepdims=True)
    )


def gelu(u):
    return 0.5 * u * (1.0 + jnp.tanh(0.7978845608028654 * (u + 0.044715 * u * u * u)))


def gelu_slope(u):
    sq = u * u
    t = jnp.tanh(0.7978845608028654 * (u + 0.044715 * sq * u))
    return 0.5 * (1.0 + t) + 0.5 * u * (1.0 - t * t) * (
        0.7978845608028654 * (1.0 + 3 * 0.044715 * sq)
    )


def pair_windows(head_dim):
    out = []
    for pair in range(8):
        lo, hi = pair * 2 * head_dim, pair * 2 * head_dim + 2 * head_dim - 1
        first = lo // LANES
        out.append((first, hi // LANES - first + 1, lo - first * LANES))
    return out


def in_turn(stages, count, unit):
    units = count // unit
    for step in range(units + len(stages) - 1):
        for late, stage in enumerate(stages):
            if 0 <= step - late < units:
                for pair in range((step - late) * unit, (step - late + 1) * unit):
                    stage(pair)


def both_heads(block, off, head_dim):
    lane = lax.broadcasted_iota(jnp.int32, (1, block.shape[1]), 1)
    one = ((lane >= off) & (lane < off + head_dim)).astype(F32).astype(BF16)
    two = ((lane >= off + head_dim) & (lane < off + 2 * head_dim)).astype(F32).astype(BF16)
    return jnp.concatenate([block * one, block * two], axis=0)


def both_columns(ref, first, tiles, off, head_dim):
    span, atoms = tiles * LANES, ref.shape[1]
    out = []
    for q in range(2):
        at = off + q * head_dim
        own = ref[first + at : first + at + head_dim, :]
        pieces = [jnp.zeros((at, atoms), F32)] * (at > 0) + [own]
        pieces += [jnp.zeros((span - at - head_dim, atoms), F32)] * (at + head_dim < span)
        out.append(jnp.concatenate(pieces, axis=0))
    return jnp.concatenate(out, axis=1).astype(BF16)


def tile_pairs(tile, windows):
    return [
        (pair, (first - tile) * LANES + off)
        for pair, (first, tiles, off) in enumerate(windows)
        if first <= tile < first + tiles
    ]


def features(dist8, path8, edge8, row, spd, edges, kern):
    atoms = dist8.shape[1]
    alpha = math.sqrt(0.5 * LOG2E) / KERN_WIDTH
    center = lax.broadcasted_iota(jnp.int32, (kern, atoms), 0).astype(F32) * (
        KERN_SPAN / kern * alpha
    )
    t = dist8[row : row + 1, :] * alpha - center
    gauss = jnp.exp2(-(t * t))
    path_id = lax.broadcasted_iota(jnp.int32, (spd, atoms), 0).astype(F32)
    edge_id = lax.broadcasted_iota(jnp.int32, (edges, atoms), 0).astype(F32)
    path = jnp.where(path8[row : row + 1, :] == path_id, 1.0, 0.0)
    edge = jnp.where(edge8[row : row + 1, :] == edge_id, 1.0, 0.0)
    rest = jnp.zeros((DEPTH - kern - spd - edges, atoms), F32)
    return jnp.concatenate([gauss, path, edge, rest], axis=0).astype(BF16)


def body(
    sections, chips, micro, atoms, heads, kern, spd, edges,
    group, counts, posn, path_in, edge_in, gains, shifts, kern_in, path_tab, edge_tab,
    tokens, cot_in, win_in, wout_in, wup_in, wdown_in,
    *refs,
):
    hidden, igrad, *refs = refs
    if chips:
        (sums, s_norm, s_tab, grads, g_norm, g_tab, *refs) = refs
    else:
        (grads, g_norm, g_tab, *refs) = refs
    (
        xs, grecv, a_s, qkv_s, o_s, mid_s, c_s, u_s, act_s, df_s, du_s, dat_s, dqkv_s,
        pairs, probs, dist_s, path_s, edge_s, tr_b, tr_f, tr_q, feats_s, ds_s,
        cot, win, wout, wup, wdown, norms, tab_f, tab, load_sem, fsend, frecv, bsend, brecv, *refs,
    ) = refs
    if chips:
        (
            core_in, line_in, norm_core, norm_sum, norm_in, tab_own, tab_core, tab_sum, tab_sec, tab_line,
            core_send, core_recv, line_send, line_recv, back_send, back_recv,
            nc_sem, nz_send, nz_recv, tc_sem, ts_send, ts_recv, tz_send, tz_recv,
            guest_in, guest_line, guest_low, gl_send, gl_recv, gb_send, gb_recv, guest_sem,
        ) = refs
    width = wout.shape[0]
    head_dim = width // heads
    scale = 1.0 / math.sqrt(head_dim)
    windows = pair_windows(head_dim)
    s = lax.axis_index("section") if sections > 1 else 0
    d = lax.axis_index("dp") if sections > 1 else 0
    last = s == sections - 1

    z, c = d // 2, d % 2

    def to(sec, dp, src, dst, send, recv):
        return pltpu.make_async_remote_copy(
            src_ref=src, dst_ref=dst, send_sem=send, recv_sem=recv, device_id=(sec, dp), device_id_type=MESH
        )

    if chips:
        barrier = pltpu.get_barrier_semaphore()
        pl.semaphore_signal(barrier, inc=1, device_id=(s, 2 * z + 1 - c), device_id_type=MESH)
        for other in range(1, sections):
            pl.semaphore_signal(
                barrier, inc=1, device_id=((s + other) % sections, d), device_id_type=MESH
            )
        for other in range(1, chips):
            pl.semaphore_signal(
                barrier, inc=1, device_id=(s, (d + 2 * other) % (2 * chips)), device_id_type=MESH
            )
    elif sections > 1:
        barrier = pltpu.get_barrier_semaphore()

        @pl.when(s > 0)
        def _():
            pl.semaphore_signal(barrier, inc=1, device_id=(s - 1, d), device_id_type=MESH)

        @pl.when(s < sections - 1)
        def _():
            pl.semaphore_signal(barrier, inc=1, device_id=(s + 1, d), device_id_type=MESH)

    def forward_copy(m):
        return pltpu.make_async_remote_copy(
            src_ref=rows_of(hidden, m, atoms), dst_ref=rows_of(xs, m, atoms),
            send_sem=fsend.at[m], recv_sem=frecv.at[m],
            device_id=(jnp.minimum(s + 1, sections - 1), d), device_id_type=MESH,
        )

    def backward_copy(m):
        return pltpu.make_async_remote_copy(
            src_ref=rows_of(igrad, m, atoms), dst_ref=rows_of(grecv, m, atoms),
            send_sem=bsend.at[m], recv_sem=brecv.at[m],
            device_id=(jnp.maximum(s - 1, 0), d), device_id_type=MESH,
        )

    def head_rows(head):
        return slice(head * atoms, (head + 1) * atoms)

    pair_rows = head_rows

    loads = [(win_in, win), (wout_in, wout), (wup_in, wup), (wdown_in, wdown), (cot_in, cot)]

    def load(k):
        return pltpu.make_async_copy(*loads[k], load_sem.at[k])

    def load_tokens():
        return pltpu.make_async_copy(tokens, xs, load_sem.at[len(loads)])

    @pl.when(s == 0)
    def _():
        load_tokens().start()

    for k in range(len(loads)):
        load(k).start()

    norms[0:2, :] = gains[...].astype(F32)
    norms[2:4, :] = shifts[...].astype(F32)
    square = jnp.concatenate([edge_tab[...].astype(F32), jnp.zeros((heads, LANES - heads), F32)], axis=1)
    square = jnp.concatenate([square, jnp.zeros((LANES - edges, LANES), F32)], axis=0)
    tab_f[...] = jnp.zeros_like(tab_f)
    tab_f[:, 0:kern] = kern_in[...].astype(F32)
    tab_f[:, kern : kern + spd] = path_tab[...].astype(F32)
    tab_f[:, kern + spd : kern + spd + edges] = jnp.transpose(square)[:heads, :edges]
    tab[...] = tab_f[...].astype(BF16)

    @pl.when(last)
    def _():
        grecv[...] = jnp.zeros_like(grecv)

    g_norm[...] = jnp.zeros_like(g_norm)
    g_tab[...] = jnp.zeros_like(g_tab)

    def make_bias(unit):
        m, half = unit // 2, unit % 2
        mol = group[m]
        count = counts[mol]

        @pl.when(half == 0)
        def _():
            pos = jnp.concatenate([posn[axis, pl.ds(m, 1), :] for axis in range(3)], axis=0)
            pos_t = jnp.transpose(jnp.concatenate([pos, jnp.zeros((5, atoms), F32)], axis=0))
            total = jnp.zeros((atoms, atoms), F32)
            for axis in range(3):
                diff = pos_t[:, axis : axis + 1] - pos[axis : axis + 1, :]
                total = total + diff * diff
            dist_s[m] = jnp.sqrt(total)
            path_s[m] = jnp.transpose(path_in[mol].astype(F32))
            edge_s[m] = jnp.transpose(edge_in[mol].astype(F32))

        out_ref = pairs.at[m]

        @pl.loop(0, atoms // 2 // BLOCK)
        def _(step):
            t = half * (atoms // 2 // BLOCK) + step
            rows = pl.ds(pl.multiple_of(t * BLOCK, BLOCK), BLOCK)
            d8, p8, e8 = dist_s[m, rows, :], path_s[m, rows, :], edge_s[m, rows, :]

            def make(r):
                for q in range(2):
                    feats_s[r % SLOTS, :, q * atoms : (q + 1) * atoms] = features(
                        d8, p8, e8, 2 * r + q, spd, edges, kern
                    )

            def project(r):
                got = dot(tab[...], feats_s[r % SLOTS]) * LOG2E
                for q in range(2):
                    j = t * BLOCK + 2 * r + q
                    row = jnp.where(j < count, got[:, q * atoms : (q + 1) * atoms], NEG_BIG)
                    out_ref[pl.ds(j, heads, stride=atoms), :] = row

            in_turn((make, project), BLOCK // 2, BIAS_UNIT)

    tab_blocks = micro * (atoms // TABLE_BLOCK)

    def table_grads(block):
        m, t = block // (atoms // TABLE_BLOCK), block % (atoms // TABLE_BLOCK)
        in_ref = pairs.at[m]
        rows = pl.ds(pl.multiple_of(t * TABLE_BLOCK, TABLE_BLOCK), TABLE_BLOCK)
        d8, p8, e8 = dist_s[m, rows, :], path_s[m, rows, :], edge_s[m, rows, :]
        acc = [jnp.zeros((DEPTH, heads), F32)]

        def make(r):
            for q in range(2):
                feats_s[r % SLOTS, :, q * atoms : (q + 1) * atoms] = features(
                    d8, p8, e8, 2 * r + q, spd, edges, kern
                )

        def collect(r):
            halves = [
                in_ref[pl.ds(t * TABLE_BLOCK + 2 * r + q, heads, stride=atoms), :] for q in range(2)
            ]
            acc[0] += dot_nt(feats_s[r % SLOTS], jnp.concatenate(halves, axis=1).astype(BF16))

        in_turn((make, collect), TABLE_BLOCK // 2, BIAS_UNIT)
        g_tab[...] += acc[0]

    def turned(n):
        return grads[:, :, :, n * width : (n + 1) * width].reshape(width, width)

    def turn_weights():
        for n, (ref, col) in enumerate([(wdown, 0), (wup, 0), (wout, 0)] + [(win, q) for q in range(3)]):
            for k in range(width // 256):
                block = ref[k * 256 : (k + 1) * 256, col * width : (col + 1) * width].astype(F32)
                block = jnp.transpose(block).astype(BF16)
                first = n * width + k * 256
                grads[:, :, :, first : first + 256] = block.reshape(grads.shape[:3] + (256,))

    def forward(m):
        x = rows_of(xs, m, atoms)[...].astype(F32)
        xh, _ = norm_parts(x)
        a = (xh * norms[0:1, :] + norms[2:3, :]).astype(BF16)
        rows_of(a_s, m, atoms)[...] = a
        qkv = rows_of(qkv_s, m, atoms)
        for blk in range(3):
            got = dot(a, win[:, blk * width : (blk + 1) * width])
            qkv[:, blk * width : (blk + 1) * width] = got.astype(BF16)
            if blk == 0:
                tr_q[...] = jnp.transpose(got.astype(BF16).astype(F32))
            if blk == 2:
                tr_b[...] = jnp.transpose(got).astype(BF16)

        def scores(pair):
            g, (tile, tiles, off) = pair // 8, windows[pair % 8]
            lane = g * 16 * head_dim + tile * LANES
            qm = both_columns(tr_q, lane, tiles, off, head_dim)
            z = dot(qkv[:, width + lane : width + lane + tiles * LANES], qm) * (scale * LOG2E)
            for q in range(2):
                pairs[m, head_rows(2 * pair + q), :] += z[:, q * atoms : (q + 1) * atoms]

        def softmax(pair):
            for q in range(2):
                z = pairs[m, head_rows(2 * pair + q), :]
                e = jnp.exp2(z - jnp.max(z, axis=0, keepdims=True))
                p = (e * (1.0 / jnp.sum(e, axis=0, keepdims=True))).astype(BF16)
                probs[m, pair_rows(pair), q * atoms : (q + 1) * atoms] = p

        def attend(pair):
            first = pair * 2 * head_dim
            got = dot(tr_b[first : first + 2 * head_dim, :], probs[m, pair_rows(pair), :])
            tr_f[first : first + head_dim, :] = got[:head_dim, :atoms]
            tr_f[first + head_dim : first + 2 * head_dim, :] = got[head_dim:, atoms:]

        in_turn((scores, softmax, attend), heads // 2, FORWARD_UNIT)

        o = jnp.transpose(tr_f[...]).astype(BF16)
        rows_of(o_s, m, atoms)[...] = o
        mid = x + dot(o, wout[...])
        rows_of(mid_s, m, atoms)[...] = mid
        xh, _ = norm_parts(mid)
        c = (xh * norms[1:2, :] + norms[3:4, :]).astype(BF16)
        rows_of(c_s, m, atoms)[...] = c
        u = dot(c, wup[...])
        rows_of(u_s, m, atoms)[...] = u
        act = gelu(u).astype(BF16)
        rows_of(act_s, m, atoms)[...] = act
        rows_of(hidden, m, atoms)[...] = (mid + dot(act, wdown[...])).astype(BF16)

    def backward_ffn(m):
        grad = rows_of(cot, m, atoms)[...].astype(F32) + rows_of(grecv, m, atoms)[...].astype(F32)
        df = grad.astype(BF16)
        rows_of(df_s, m, atoms)[...] = df
        du = (dot(df, turned(0)) * gelu_slope(rows_of(u_s, m, atoms)[...])).astype(BF16)
        rows_of(du_s, m, atoms)[...] = du
        dc = dot(du, turned(1))
        xh, inv_std = norm_parts(rows_of(mid_s, m, atoms)[...])
        g_norm[1:2, :] += jnp.sum(dc * xh, axis=0, keepdims=True)
        g_norm[3:4, :] += jnp.sum(dc, axis=0, keepdims=True)
        dmid = grad + norm_back(dc, xh, inv_std, norms[1:2, :])
        rows_of(mid_s, m, atoms)[...] = dmid
        dat = dmid.astype(BF16)
        rows_of(dat_s, m, atoms)[...] = dat
        do = dot(dat, turned(2)).astype(BF16)
        rows_of(dqkv_s, m, atoms)[:, 0:width] = do
        tr_q[...] = jnp.transpose(do.astype(F32))

    def backward_attn(m):
        qkv = rows_of(qkv_s, m, atoms)
        dqkv = rows_of(dqkv_s, m, atoms)
        tr_b[...] = jnp.transpose(qkv[:, width : 2 * width].astype(F32)).astype(BF16)

        def slopes(pair):
            g, (tile, tiles, off) = pair // 8, windows[pair % 8]
            lane = g * 16 * head_dim + tile * LANES
            dom = both_columns(tr_q, lane, tiles, off, head_dim)
            dp = dot(qkv[:, 2 * width + lane : 2 * width + lane + tiles * LANES], dom)
            for q in range(2):
                pairs[m, head_rows(2 * pair + q), :] = dp[:, q * atoms : (q + 1) * atoms]

        def softmax_back(pair):
            for q in range(2):
                half = slice(q * atoms, (q + 1) * atoms)
                p = probs[m, pair_rows(pair), half].astype(F32)
                pd = p * pairs[m, head_rows(2 * pair + q), :]
                ds = pd - p * jnp.sum(pd, axis=0, keepdims=True)
                pairs[m, head_rows(2 * pair + q), :] = ds
                ds_s[pair_rows(pair), half] = ds.astype(BF16)

        def products(pair):
            first = pair * 2 * head_dim
            got = dot(tr_b[first : first + 2 * head_dim, :], ds_s[pair_rows(pair), :])
            tr_f[first : first + head_dim, :] = got[:head_dim, :atoms]
            tr_f[first + head_dim : first + 2 * head_dim, :] = got[head_dim:, atoms:]
            for tile in range(16 * head_dim // LANES):
                inside = tile_pairs(tile, windows)
                if inside[-1][0] != pair % 8:
                    continue
                lane = pair // 8 * 16 * head_dim + tile * LANES
                these = [(pair // 8 * 8 + one, off) for one, off in inside]
                left = jnp.concatenate([probs[m, pair_rows(one), :] for one, _ in these], axis=1)
                block = dqkv[:, lane : lane + LANES]
                right = jnp.concatenate([both_heads(block, off, head_dim) for _, off in these], axis=0)
                dqkv[:, 2 * width + lane : 2 * width + lane + LANES] = dot(left, right).astype(BF16)
                left = jnp.concatenate([ds_s[pair_rows(one), :] for one, _ in these], axis=1)
                block = qkv[:, lane : lane + LANES]
                right = jnp.concatenate([both_heads(block, off, head_dim) for _, off in these], axis=0)
                dqkv[:, width + lane : width + lane + LANES] = (dot(left, right) * scale).astype(BF16)

        in_turn((slopes, softmax_back, products), heads // 2, BACKWARD_UNIT)

        dqkv[:, 0:width] = (jnp.transpose(tr_f[...]) * scale).astype(BF16)
        da = sum(dot(dqkv[:, q * width : (q + 1) * width], turned(3 + q)) for q in range(3))
        xh, inv_std = norm_parts(rows_of(xs, m, atoms)[...].astype(F32))
        g_norm[0:1, :] += jnp.sum(da * xh, axis=0, keepdims=True)
        g_norm[2:3, :] += jnp.sum(da, axis=0, keepdims=True)
        out = rows_of(mid_s, m, atoms)[...] + norm_back(da, xh, inv_std, norms[0:1, :])
        rows_of(igrad, m, atoms)[...] = out.astype(BF16)

    parts = grads.shape[-1] // width
    share = grads.shape[2]

    def chunk(n):
        return pl.ds(n * width if isinstance(n, int) else pl.multiple_of(n * width, LANES), width)

    def core_copy(n):
        return to(
            s, 2 * z + 1 - c, grads.at[:, 1 - c, :, chunk(n)], core_in.at[:, :, chunk(n)],
            core_send.at[n], core_recv.at[n],
        )

    class Line:
        def __init__(self, ref_of, into, out, sems, cols, count):
            self.ref_of, self.into, self.out, self.sems = ref_of, into, out, sems
            self.cols, self.count, self.steps = cols, count, (chips - 1) * count

        def right(self, n, target):
            return to(
                s, jnp.minimum(d + 2, 2 * chips - 1), self.ref_of(target).at[:, self.cols(n)],
                self.into.at[target + 1, :, self.cols(n)], self.sems[0].at[n, target], self.sems[1].at[n, target],
            )

        def left(self, n, target):
            return to(
                s, jnp.maximum(d - 2, 0), self.ref_of(target).at[:, self.cols(n)],
                self.into.at[target, :, self.cols(n)], self.sems[2].at[n, target], self.sems[3].at[n, target],
            )

        def end_copy(self, hop, n, act):
            @pl.when(z == 0)
            def _():
                act(self.right(n, chips - 1 - hop))

            @pl.when(z == chips - 1)
            def _():
                act(self.left(n, hop))

        def add_in(self, target, slot, cols):
            ref = self.ref_of(target)
            ref[:, cols] = (ref[:, cols].astype(F32) + self.into[slot, :, cols].astype(F32)).astype(BF16)

        def step(self, i):
            at_right, at_left = i - LAG * (z - 1), i - LAG * (chips - 2 - z)
            right, right_n = chips - 1 - at_right // self.count, at_right % self.count
            left, left_n = at_left // self.count, at_left % self.count

            @pl.when((z > 0) & (at_right >= 0) & (z <= right))
            def _():
                cols = self.cols(right_n)
                self.right(right_n, right).wait_recv()

                @pl.when(z < right)
                def _():
                    self.add_in(right, right + 1, cols)
                    self.right(right_n, right).start()

                @pl.when(z == right)
                def _():
                    self.out[:, cols] += self.into[right + 1, :, cols].astype(F32)

            @pl.when((z < chips - 1) & (at_left >= 0) & (z >= left))
            def _():
                cols = self.cols(left_n)
                self.left(left_n, left).wait_recv()

                @pl.when(z > left)
                def _():
                    self.add_in(left, left, cols)
                    self.left(left_n, left).start()

                @pl.when(z == left)
                def _():
                    self.out[:, cols] += self.into[left, :, cols].astype(F32)

            self.end_copy(i // self.count, i % self.count, lambda copy: copy.wait_send())

            @pl.when(i + self.count < self.steps)
            def _():
                self.end_copy(i // self.count + 1, i % self.count, lambda copy: copy.start())

        def drain(self, n):
            for target in range(chips):
                @pl.when((target > z) & (z > 0))
                def _():
                    self.right(n, target).wait_send()

                @pl.when((target < z) & (z < chips - 1))
                def _():
                    self.left(n, target).wait_send()

    donor, helper = s == 0, s == sections - 1
    own_parts = jnp.where(donor, parts - 1, parts)
    if chips:
        main = Line(
            lambda target: grads.at[target, c], line_in, sums, (line_send, line_recv, back_send, back_recv),
            chunk, own_parts,
        )

        def part_cols(n):
            return pl.ds(n * 2 * LANES if isinstance(n, int) else pl.multiple_of(n * 2 * LANES, LANES), 2 * LANES)

        guest_sum = mid_s.at[0:share, :]
        guest = Line(
            lambda target: guest_in.at[target], guest_line, guest_sum, (gl_send, gl_recv, gb_send, gb_recv),
            part_cols, width // (2 * LANES),
        )

    def guest_copy():
        return to(
            sections - 1, d, grads.at[:, c, :, chunk(parts - 1)], guest_in, guest_sem.at[0], guest_sem.at[1]
        )

    def result_copy():
        return to(0, d, guest_low, guest_low, guest_sem.at[2], guest_sem.at[3])

    def settle(n):
        core_copy(n).wait_recv()
        for target in range(chips):
            both = grads[target, c, :, chunk(n)].astype(F32) + core_in[target, :, chunk(n)].astype(F32)
            grads[target, c, :, chunk(n)] = both.astype(BF16)

            @pl.when(z == target)
            def _():
                sums[:, chunk(n)] = both

        if n < parts - 1:
            main.end_copy(0, n, lambda copy: copy.start())
        else:
            @pl.when(donor)
            def _():
                guest_copy().start()

            @pl.when(jnp.logical_not(donor))
            def _():
                main.end_copy(0, n, lambda copy: copy.start())

    def norm_copy():
        return to(s, 2 * z + 1 - c, g_norm, norm_core, nc_sem.at[0], nc_sem.at[1])

    def weight_grads(lo, hi):
        jobs = [(act_s, df_s, 0), (c_s, du_s, 0), (o_s, dat_s, 0)] + [(a_s, dqkv_s, q) for q in range(3)]
        for n, (left, right, col) in list(enumerate(jobs))[lo:hi]:
            if col == 0:
                for m in range(micro):
                    part = left[m * atoms : (m + 1) * atoms, :].astype(F32)
                    first = m // 2 * width
                    ds_s[first : first + width, m % 2 * atoms : (m % 2 + 1) * atoms] = jnp.transpose(
                        part
                    ).astype(BF16)

            @pl.loop(0, width // 256)
            def _(q):
                cols = pl.ds(pl.multiple_of(col * width + q * 256, 256), 256)
                turned_left = [ds_s[k * width : (k + 1) * width, :] for k in range(micro // 2)]
                got = dot(jnp.concatenate(turned_left, axis=1), right[:, cols]).astype(BF16)
                cols = pl.ds(pl.multiple_of(n * width + q * 256, 256), 256)
                grads[:, :, :, cols] = got.reshape(grads.shape[:3] + (256,))

            if chips:
                core_copy(n).start()
                if n:
                    settle(n - 1)

    def norm_window(dp):
        first = jnp.minimum(dp * share // LANES, width // LANES - 2)
        return pl.ds(pl.multiple_of(first * LANES, LANES), 2 * LANES)

    def norm_line(there, here):
        return to(
            s, 2 * there + c, norm_sum.at[:, norm_window(2 * there + c)], norm_in.at[here],
            nz_send.at[there], nz_recv.at[here],
        )

    def tab_copy():
        return to(s, 2 * z + 1 - c, tab_own, tab_core, tc_sem.at[0], tc_sem.at[1])

    def tab_section(there, here):
        return to(there, d, tab_sum.at[0], tab_sec.at[here], ts_send.at[there], ts_recv.at[here])

    def tab_chip(there, here):
        return to(s, 2 * there + c, tab_sum.at[1], tab_line.at[here], tz_send.at[there], tz_recv.at[here])

    def others(mine, count, act):
        for other in range(count):
            @pl.when(other != mine)
            def _():
                act(other)

    def reduce_all():
        norm_copy().wait_recv()
        norm_sum[...] = g_norm[...] + norm_core[...]
        norm_in[z] = norm_sum[:, norm_window(d)]
        others(z, chips, lambda o: norm_line(o, z).start())

        tab_steps = (chips - 1) * (parts - 1) - 6
        tab_each = -(-tab_blocks // tab_steps)

        def tab_over_chips():
            others(s, sections, lambda o: tab_section(o, o).wait_recv())
            tab_sum[1] = sum(tab_sec[o] for o in range(sections))
            tab_line[z] = tab_sum[1]
            others(z, chips, lambda o: tab_chip(o, z).start())

        @pl.loop(0, main.steps)
        def _(i):
            @pl.when(i < tab_steps)
            def _():
                @pl.loop(i * tab_each, jnp.minimum((i + 1) * tab_each, tab_blocks))
                def _(block):
                    table_grads(block)

            @pl.when(i == tab_steps)
            def _():
                wide_tab = jnp.concatenate([g_tab[...], jnp.zeros((DEPTH, LANES - heads), F32)], axis=1)
                tab_own[...] = jnp.transpose(wide_tab)[:heads, :]
                tab_copy().start()

            @pl.when(i == tab_steps + 1)
            def _():
                tab_copy().wait_recv()
                tab_sum[0] = tab_own[...] + tab_core[...]
                tab_sec[s] = tab_sum[0]
                others(s, sections, lambda o: tab_section(o, s).start())

            @pl.when((i == tab_steps + 3) & (s < 2))
            def _():
                tab_over_chips()

            main.step(i)

        @pl.when(helper)
        def _():
            guest_copy().wait_recv()
            guest_sum[...] = guest_in[z].astype(F32)
            for n in range(guest.count):
                guest.end_copy(0, n, lambda copy: copy.start())

            pl.loop(0, guest.steps)(guest.step)
            guest_low[...] = guest_sum[...].astype(BF16)
            result_copy().start()

        @pl.when(s >= 2)
        def _():
            tab_over_chips()

        others(z, chips, lambda o: norm_line(o, o).wait_recv())
        s_norm[...] = sum(norm_in[o] for o in range(chips))
        others(z, chips, lambda o: tab_chip(o, o).wait_recv())
        s_tab[...] = sum(tab_line[o] for o in range(chips))

        norm_copy().wait_send()
        tab_copy().wait_send()
        others(z, chips, lambda o: norm_line(o, z).wait_send())
        others(s, sections, lambda o: tab_section(o, s).wait_send())
        others(z, chips, lambda o: tab_chip(o, z).wait_send())

        @pl.loop(0, parts)
        def _(n):
            core_copy(n).wait_send()

            @pl.when(n < own_parts)
            def _():
                main.drain(n)

        @pl.when(helper)
        def _():
            pl.loop(0, guest.count)(guest.drain)
            result_copy().wait_send()

        @pl.when(donor)
        def _():
            guest_copy().wait_send()
            result_copy().wait_recv()
            sums[:, chunk(parts - 1)] = guest_low[...].astype(F32)

    pl.loop(0, 2)(make_bias)
    if chips:
        pl.semaphore_wait(barrier, sections + chips - 1)
    elif sections > 1:
        pl.semaphore_wait(barrier, jnp.where((s > 0) & (s < sections - 1), 2, 1))

    total = 4 * micro

    @pl.loop(2, total)
    def _(t):
        ahead = jnp.where(last, micro, jnp.minimum(micro, jnp.where(s == 0, 1, 2 * s * s)))
        gap = micro - ahead
        r = t - 2 * ahead
        mixed = (r >= 0) & (r < 3 * gap)
        unit = jnp.where(r < 0, t, 2 * (ahead + r // 3) + r % 3 - 1)
        is_bias = (r < 0) | (mixed & (r % 3 != 0))
        is_fwd = jnp.where(
            last, (r >= 0) & (r % 2 == 0), (mixed & (r % 3 == 0)) | ((r >= 3 * gap) & (t < 3 * micro))
        )
        m_fwd = jnp.where(last, r // 2, jnp.where(mixed, r // 3, r - 2 * gap))
        is_back = jnp.where(last, (r >= 0) & (r % 2 == 1), t >= 3 * micro)
        m_back = jnp.where(last, r // 2, t - 3 * micro)
        @pl.when(is_bias)
        def _():
            make_bias(unit)

        @pl.when(is_fwd & (m_fwd == 0))
        def _():
            for k in range(len(loads) - 1):
                load(k).wait()

            @pl.when(s == 0)
            def _():
                load_tokens().wait()

        @pl.when(jnp.where(s >= 2, is_fwd & (m_fwd == 0), is_back & (m_back == 0)))
        def _():
            turn_weights()

        @pl.when(is_fwd)
        def _():
            if sections > 1:
                @pl.when(s > 0)
                def _():
                    forward_copy(m_fwd).wait_recv()

            forward(m_fwd)
            if sections > 1:
                @pl.when(jnp.logical_not(last))
                def _():
                    forward_copy(m_fwd).start()

        @pl.when(is_back)
        def _():
            @pl.when(m_back == 0)
            def _():
                load(len(loads) - 1).wait()

            if sections > 1:
                @pl.when(jnp.logical_not(last))
                def _():
                    backward_copy(m_back).wait_recv()

            backward_ffn(m_back)

            @pl.when((s == 0) & (m_back == micro - 1))
            def _():
                weight_grads(0, 3)

            backward_attn(m_back)
            if sections > 1:
                @pl.when(s > 0)
                def _():
                    backward_copy(m_back).start()

    @pl.when(s != 0)
    def _():
        weight_grads(0, 3)

    if chips:
        norm_copy().start()
    weight_grads(3, parts)
    if chips:
        settle(parts - 1)
    if chips:
        reduce_all()
    else:
        pl.loop(0, tab_blocks)(table_grads)

    if sections > 1:
        @pl.loop(0, micro)
        def _(m):
            @pl.when(jnp.logical_not(last))
            def _():
                forward_copy(m).wait_send()

            @pl.when(s > 0)
            def _():
                backward_copy(m).wait_send()


def layer_call(
    sections, chips, tokens, cot, posn, group, counts, path_in, edge_in, win, wout, wup, wdown,
    norm_gain, norm_shift, kernel_proj, path_table, edge_table,
):
    micro, _, atoms = posn.shape
    rows, width = tokens.shape
    kern, heads = kernel_proj.shape
    spd, edges = path_table.shape[0], edge_table.shape[0]
    shape = jax.ShapeDtypeStruct
    vmem, smem = pl.BlockSpec(memory_space=pltpu.VMEM), pl.BlockSpec(memory_space=pltpu.SMEM)
    low = lambda *dims: pltpu.VMEM(dims, BF16)
    wide = lambda *dims: pltpu.VMEM(dims, F32)
    sems = lambda *dims: pltpu.SemaphoreType.DMA(dims)
    parts = 3 + win.shape[1] // width
    all_pairs = heads // 2 * atoms
    outs = [shape((rows, width), BF16), shape((rows, width), BF16)]
    share = width // (2 * chips) if chips else width
    grads = (chips, 2, share, parts * width) if chips else (1, 1, width, parts * width)
    local = [(grads, BF16), ((8, width), F32), ((DEPTH, heads), F32)]
    scratch = []
    if chips:
        outs += [shape((share, parts * width), F32)]
        outs += [shape((8, 2 * LANES), F32), shape((heads, DEPTH), F32)]
        scratch += [pltpu.VMEM(dims, kind) for dims, kind in local]
    else:
        outs += [shape(dims, kind) for dims, kind in local]
    scratch += [
        low(rows, width), low(rows, width), low(rows, width), low(rows, 3 * width), low(rows, width),
        wide(rows, width), low(rows, width), wide(rows, width), low(rows, width), low(rows, width),
        low(rows, width), low(rows, width), low(rows, 3 * width),
        wide(micro, 2 * all_pairs, atoms), low(micro, all_pairs, 2 * atoms),
        wide(micro, atoms, atoms), wide(micro, atoms, atoms), wide(micro, atoms, atoms),
        low(width, atoms), wide(width, atoms), wide(width, atoms), low(SLOTS, DEPTH, 2 * atoms), low(all_pairs, 2 * atoms),
        low(rows, width), low(*win.shape), low(*wout.shape), low(*wup.shape), low(*wdown.shape),
        wide(4, width), wide(heads, DEPTH), low(heads, DEPTH), sems(6),
    ] + [sems(micro)] * 4
    if chips:
        scratch += [
            low(chips, share, parts * width), low(chips + 1, share, parts * width),
            wide(8, width), wide(8, width), wide(chips, 8, 2 * LANES),
            wide(heads, DEPTH), wide(heads, DEPTH), wide(2, heads, DEPTH),
            wide(sections, heads, DEPTH), wide(chips, heads, DEPTH),
            sems(parts), sems(parts), sems(parts, chips), sems(parts, chips), sems(parts, chips), sems(parts, chips),
            sems(2), sems(chips), sems(chips), sems(2), sems(sections), sems(sections), sems(chips), sems(chips),
            low(chips, share, width), low(chips + 1, share, width), low(share, width),
        ] + [sems(width // (2 * LANES), chips)] * 4 + [
            sems(4),
        ]
    params = dict(vmem_limit_bytes=60 * 2**20, has_side_effects=True)
    if sections > 1:
        params["collective_id"] = 0
    return pl.pallas_call(
        functools.partial(body, sections, chips, micro, atoms, heads, kern, spd, edges),
        out_shape=outs,
        in_specs=[smem, smem] + [vmem] * 8 + [pl.BlockSpec(memory_space=pl.ANY)] * 6,
        out_specs=[vmem] * len(outs),
        scratch_shapes=scratch,
        compiler_params=pltpu.CompilerParams(**params),
        name="sections",
    )(
        group, counts, jnp.transpose(posn, (1, 0, 2)), path_in, edge_in, norm_gain.T, norm_shift.T,
        kernel_proj.T, path_table.T, edge_table, tokens, cot, win, wout, wup, wdown,
    )


def finish_body(
    width, kern, spd, edges, sections,
    hidden, igrad, sums, norm, tab,
    hidden_o, igrad_o, in_o, out_o, up_o, down_o, gain_o, shift_o, kern_o, path_o, edge_o, tab_s, norm_s,
):
    hidden_o[...] = hidden[...]
    igrad_o[...] = igrad[...]
    for k, ref in enumerate((down_o, up_o, out_o)):
        ref[...] = sums[:, k * width : (k + 1) * width]
    in_o[...] = sums[:, 3 * width :]
    share = gain_o.shape[1]
    section, first = lax.axis_index("section"), lax.axis_index("dp") * share
    first = first - jnp.minimum(first // LANES, width // LANES - 2) * LANES
    norm_s[...] = jnp.transpose(norm[...])
    rows = norm_s[pl.ds(pl.multiple_of(first, 8), share), :]
    rows = jnp.transpose(jnp.concatenate([rows, jnp.zeros((share, LANES - 8), F32)], axis=1))
    gain_o[...] = rows[0:2, :]
    shift_o[...] = rows[2:4, :]
    tab_s[...] = jnp.transpose(tab[...])
    start = 0
    for count, ref in ((kern, kern_o), (spd, path_o), (edges, edge_o)):
        own = count // sections
        ref[...] = tab_s[pl.ds(pl.multiple_of(start + section * own, 8), own), :]
        start += count


def finish(hidden, igrad, sums, norm, tab, kern, spd, edges, sections):
    width, heads = hidden.shape[1], tab.shape[0]
    share = sums.shape[0]
    shape = jax.ShapeDtypeStruct
    vmem = pl.BlockSpec(memory_space=pltpu.VMEM)
    outs = (
        [shape(hidden.shape, BF16), shape(igrad.shape, BF16), shape((share, sums.shape[1] - 3 * width), F32)]
        + [shape((share, width), F32)] * 3
        + [shape((2, share), F32)] * 2
        + [shape((count // sections, heads), F32) for count in (kern, spd, edges)]
    )
    return pl.pallas_call(
        functools.partial(finish_body, width, kern, spd, edges, sections),
        out_shape=outs,
        in_specs=[vmem] * 5,
        out_specs=[vmem] * len(outs),
        scratch_shapes=[pltpu.VMEM((DEPTH, heads), F32), pltpu.VMEM((2 * LANES, 8), F32)],
        compiler_params=pltpu.CompilerParams(vmem_limit_bytes=60 * 2**20),
        name="finish",
    )(hidden, igrad, sums, norm, tab)


def on_device(
    tokens, cotangent, positions, conformer_group, atom_counts, path_dist, edge_kind, attn_in, attn_out,
    ffn_up, ffn_down, norm_gain, norm_shift, kernel_proj, path_table, edge_table,
):
    sections, count = lax.axis_size("section"), lax.axis_size("dp")
    section, place = lax.axis_index("section"), lax.axis_index("dp")
    kern, heads = kernel_proj.shape
    spd, edges = path_table.shape[0], edge_table.shape[0]
    width = attn_out.shape[1]
    share = width // count
    chips = 4 if count == 8 and share % 16 == 0 and share <= LANES else 0
    hidden, igrad, *sums = layer_call(
        sections, chips, tokens, cotangent[0], positions, conformer_group, atom_counts, path_dist, edge_kind,
        attn_in[0], attn_out[0], ffn_up[0], ffn_down[0], norm_gain[0], norm_shift[0],
        kernel_proj, path_table, edge_table,
    )
    if chips:
        outs = finish(hidden, igrad, *sums, kern, spd, edges, sections)
        norms = [jnp.transpose(o) for o in outs[6:8]]
        return tuple(o[None] for o in [*outs[:6], *norms]) + tuple(outs[8:])
    grads, g_norm, g_tab = sums
    split = lambda a, n: grads[0, 0, :, a * width : (a + n) * width]
    sums = [
        lax.psum_scatter(g, "dp", scatter_dimension=0, tiled=True).astype(F32)
        for g in (split(3, 3), split(2, 1), split(1, 1), split(0, 1))
    ]
    norm_sum = lax.psum(g_norm[:4], "dp").T
    norm_sum = lax.dynamic_slice_in_dim(norm_sum, place * share, share, 0)[None]
    tab_sum = lax.psum(g_tab, ("section", "dp"))
    tabs, start = [], 0
    for rows in (kern, spd, edges):
        own = rows // sections
        tabs.append(lax.dynamic_slice_in_dim(tab_sum, start + section * own, own, 0))
        start += rows
    return (hidden[None], igrad[None], *(g[None] for g in sums), norm_sum[:, :, :2], norm_sum[:, :, 2:], *tabs)


def solution(mesh):
    in_specs = (
        P("dp", None),
        P("section", "dp", None),
        P("dp", None, None),
        P("dp"),
        P("dp"),
        P("dp", None, None),
        P("dp", None, None),
        P("section", None, None),
        P("section", None, None),
        P("section", None, None),
        P("section", None, None),
        P("section", None, None),
        P("section", None, None),
        P(),
        P(),
        P(),
    )
    out_specs = (
        P("section", "dp", None),
        P("section", "dp", None),
        P("section", "dp", None),
        P("section", "dp", None),
        P("section", "dp", None),
        P("section", "dp", None),
        P("section", "dp", None),
        P("section", "dp", None),
        P("section", None),
        P("section", None),
        P("section", None),
    )
    return jax.shard_map(
        on_device, mesh=mesh, in_specs=in_specs, out_specs=out_specs, check_vma=False
    )
```

```python
import functools
import math

import jax
import jax.numpy as jnp
from jax import lax
from jax.experimental import pallas as pl
from jax.experimental.pallas import tpu as pltpu
from jax.sharding import PartitionSpec as P

F32, BF16 = jnp.float32, jnp.bfloat16
MESH = pl.DeviceIdType.MESH
EPS = 1e-05
NEG_BIG = -1e30
KERN_SPAN = 8.0
KERN_WIDTH = 0.4
LOG2E = math.log2(math.e)
LANES = 128
DEPTH = 256
LAG = 3
STRIPS = 2
FORWARD_UNIT = 4
BACKWARD_UNIT = 2
BIAS_UNIT = 2
BLOCK = 64
TABLE_BLOCK = 16
SLOTS = 4


def dot(a, b):
    return jnp.dot(a, b, preferred_element_type=F32)


def dot_nt(a, b):
    return lax.dot_general(a, b, (((1,), (1,)), ((), ())), preferred_element_type=F32)


def rows_of(ref, m, n):
    return ref.at[pl.ds(pl.multiple_of(m * n, n), n), :]


def norm_parts(values):
    center = values - jnp.mean(values, axis=-1, keepdims=True)
    inv_std = lax.rsqrt(jnp.mean(center * center, axis=-1, keepdims=True) + EPS)
    return center * inv_std, inv_std


def norm_back(dy, xh, inv_std, gain):
    dxh = dy * gain
    return inv_std * (
        dxh
        - jnp.mean(dxh, axis=-1, keepdims=True)
        - xh * jnp.mean(dxh * xh, axis=-1, keepdims=True)
    )


def gelu(u):
    return 0.5 * u * (1.0 + jnp.tanh(0.7978845608028654 * (u + 0.044715 * u * u * u)))


def gelu_slope(u):
    sq = u * u
    t = jnp.tanh(0.7978845608028654 * (u + 0.044715 * sq * u))
    return 0.5 * (1.0 + t) + 0.5 * u * (1.0 - t * t) * (
        0.7978845608028654 * (1.0 + 3 * 0.044715 * sq)
    )


def pair_windows(head_dim):
    out = []
    for pair in range(8):
        lo, hi = pair * 2 * head_dim, pair * 2 * head_dim + 2 * head_dim - 1
        first = lo // LANES
        out.append((first, hi // LANES - first + 1, lo - first * LANES))
    return out


def in_turn(stages, count, unit):
    units = count // unit
    for step in range(units + len(stages) - 1):
        for late, stage in enumerate(stages):
            if 0 <= step - late < units:
                for pair in range((step - late) * unit, (step - late + 1) * unit):
                    stage(pair)


def both_heads(block, off, head_dim):
    lane = lax.broadcasted_iota(jnp.int32, (1, block.shape[1]), 1)
    one = ((lane >= off) & (lane < off + head_dim)).astype(F32).astype(BF16)
    two = ((lane >= off + head_dim) & (lane < off + 2 * head_dim)).astype(F32).astype(BF16)
    return jnp.concatenate([block * one, block * two], axis=0)


def both_columns(ref, first, tiles, off, head_dim):
    span, atoms = tiles * LANES, ref.shape[1]
    out = []
    for q in range(2):
        at = off + q * head_dim
        own = ref[first + at : first + at + head_dim, :]
        pieces = [jnp.zeros((at, atoms), F32)] * (at > 0) + [own]
        pieces += [jnp.zeros((span - at - head_dim, atoms), F32)] * (at + head_dim < span)
        out.append(jnp.concatenate(pieces, axis=0))
    return jnp.concatenate(out, axis=1).astype(BF16)


def tile_pairs(tile, windows):
    return [
        (pair, (first - tile) * LANES + off)
        for pair, (first, tiles, off) in enumerate(windows)
        if first <= tile < first + tiles
    ]


def features(dist8, path8, edge8, row, spd, edges, kern):
    atoms = dist8.shape[1]
    alpha = math.sqrt(0.5 * LOG2E) / KERN_WIDTH
    center = lax.broadcasted_iota(jnp.int32, (kern, atoms), 0).astype(F32) * (
        KERN_SPAN / kern * alpha
    )
    t = dist8[row : row + 1, :] * alpha - center
    gauss = jnp.exp2(-(t * t))
    path_id = lax.broadcasted_iota(jnp.int32, (spd, atoms), 0).astype(F32)
    edge_id = lax.broadcasted_iota(jnp.int32, (edges, atoms), 0).astype(F32)
    path = jnp.where(path8[row : row + 1, :] == path_id, 1.0, 0.0)
    edge = jnp.where(edge8[row : row + 1, :] == edge_id, 1.0, 0.0)
    rest = jnp.zeros((DEPTH - kern - spd - edges, atoms), F32)
    return jnp.concatenate([gauss, path, edge, rest], axis=0).astype(BF16)


def body(
    sections, chips, micro, atoms, heads, kern, spd, edges,
    group, counts, posn, path_in, edge_in, gains, shifts, kern_in, path_tab, edge_tab,
    tokens, cot_in, win_in, wout_in, wup_in, wdown_in,
    *refs,
):
    hidden, igrad, *refs = refs
    if chips:
        (sums, s_norm, s_tab, grads, g_norm, g_tab, *refs) = refs
    else:
        (grads, g_norm, g_tab, *refs) = refs
    (
        xs, grecv, a_s, qkv_s, o_s, mid_s, c_s, u_s, act_s, df_s, du_s, dat_s, dqkv_s,
        pairs, probs, dist_s, path_s, edge_s, tr_b, tr_f, tr_q, feats_s, ds_s,
        cot, win, wout, wup, wdown, norms, tab_f, tab, load_sem, fsend, frecv, bsend, brecv, *refs,
    ) = refs
    if chips:
        (
            core_in, line_in, norm_core, norm_sum, norm_in, tab_own, tab_core, tab_sum, tab_sec, tab_line,
            core_send, core_recv, line_send, line_recv, back_send, back_recv,
            nc_sem, nz_send, nz_recv, tc_sem, ts_send, ts_recv, tz_send, tz_recv,
            guest_in, guest_line, guest_low, gl_send, gl_recv, gb_send, gb_recv, guest_sem,
        ) = refs
    width = wout.shape[0]
    head_dim = width // heads
    scale = 1.0 / math.sqrt(head_dim)
    windows = pair_windows(head_dim)
    s = lax.axis_index("section") if sections > 1 else 0
    d = lax.axis_index("dp") if sections > 1 else 0
    last = s == sections - 1

    z, c = d // 2, d % 2

    def to(sec, dp, src, dst, send, recv):
        return pltpu.make_async_remote_copy(
            src_ref=src, dst_ref=dst, send_sem=send, recv_sem=recv, device_id=(sec, dp), device_id_type=MESH
        )

    if chips:
        barrier = pltpu.get_barrier_semaphore()
        pl.semaphore_signal(barrier, inc=1, device_id=(s, 2 * z + 1 - c), device_id_type=MESH)
        for other in range(1, sections):
            pl.semaphore_signal(
                barrier, inc=1, device_id=((s + other) % sections, d), device_id_type=MESH
            )
        for other in range(1, chips):
            pl.semaphore_signal(
                barrier, inc=1, device_id=(s, (d + 2 * other) % (2 * chips)), device_id_type=MESH
            )
    elif sections > 1:
        barrier = pltpu.get_barrier_semaphore()

        @pl.when(s > 0)
        def _():
            pl.semaphore_signal(barrier, inc=1, device_id=(s - 1, d), device_id_type=MESH)

        @pl.when(s < sections - 1)
        def _():
            pl.semaphore_signal(barrier, inc=1, device_id=(s + 1, d), device_id_type=MESH)

    def forward_copy(m):
        return pltpu.make_async_remote_copy(
            src_ref=rows_of(hidden, m, atoms), dst_ref=rows_of(xs, m, atoms),
            send_sem=fsend.at[m], recv_sem=frecv.at[m],
            device_id=(jnp.minimum(s + 1, sections - 1), d), device_id_type=MESH,
        )

    def backward_copy(m):
        return pltpu.make_async_remote_copy(
            src_ref=rows_of(igrad, m, atoms), dst_ref=rows_of(grecv, m, atoms),
            send_sem=bsend.at[m], recv_sem=brecv.at[m],
            device_id=(jnp.maximum(s - 1, 0), d), device_id_type=MESH,
        )

    def head_rows(head):
        return slice(head * atoms, (head + 1) * atoms)

    pair_rows = head_rows

    loads = [(win_in, win), (wout_in, wout), (wup_in, wup), (wdown_in, wdown), (cot_in, cot)]

    def load(k):
        return pltpu.make_async_copy(*loads[k], load_sem.at[k])

    def load_tokens():
        return pltpu.make_async_copy(tokens, xs, load_sem.at[len(loads)])

    @pl.when(s == 0)
    def _():
        load_tokens().start()

    for k in range(len(loads)):
        load(k).start()

    norms[0:2, :] = gains[...].astype(F32)
    norms[2:4, :] = shifts[...].astype(F32)
    square = jnp.concatenate([edge_tab[...].astype(F32), jnp.zeros((heads, LANES - heads), F32)], axis=1)
    square = jnp.concatenate([square, jnp.zeros((LANES - edges, LANES), F32)], axis=0)
    tab_f[...] = jnp.zeros_like(tab_f)
    tab_f[:, 0:kern] = kern_in[...].astype(F32)
    tab_f[:, kern : kern + spd] = path_tab[...].astype(F32)
    tab_f[:, kern + spd : kern + spd + edges] = jnp.transpose(square)[:heads, :edges]
    tab[...] = tab_f[...].astype(BF16)

    @pl.when(last)
    def _():
        grecv[...] = jnp.zeros_like(grecv)

    g_norm[...] = jnp.zeros_like(g_norm)
    g_tab[...] = jnp.zeros_like(g_tab)

    def make_bias(unit):
        m, half = unit // 2, unit % 2
        mol = group[m]
        count = counts[mol]

        @pl.when(half == 0)
        def _():
            pos = jnp.concatenate([posn[axis, pl.ds(m, 1), :] for axis in range(3)], axis=0)
            pos_t = jnp.transpose(jnp.concatenate([pos, jnp.zeros((5, atoms), F32)], axis=0))
            total = jnp.zeros((atoms, atoms), F32)
            for axis in range(3):
                diff = pos_t[:, axis : axis + 1] - pos[axis : axis + 1, :]
                total = total + diff * diff
            dist_s[m] = jnp.sqrt(total)
            path_s[m] = jnp.transpose(path_in[mol].astype(F32))
            edge_s[m] = jnp.transpose(edge_in[mol].astype(F32))

        out_ref = pairs.at[m]

        @pl.loop(0, atoms // 2 // BLOCK)
        def _(step):
            t = half * (atoms // 2 // BLOCK) + step
            rows = pl.ds(pl.multiple_of(t * BLOCK, BLOCK), BLOCK)
            d8, p8, e8 = dist_s[m, rows, :], path_s[m, rows, :], edge_s[m, rows, :]

            def make(r):
                for q in range(2):
                    feats_s[r % SLOTS, :, q * atoms : (q + 1) * atoms] = features(
                        d8, p8, e8, 2 * r + q, spd, edges, kern
                    )

            def project(r):
                got = dot(tab[...], feats_s[r % SLOTS]) * LOG2E
                for q in range(2):
                    j = t * BLOCK + 2 * r + q
                    row = jnp.where(j < count, got[:, q * atoms : (q + 1) * atoms], NEG_BIG)
                    out_ref[pl.ds(j, heads, stride=atoms), :] = row

            in_turn((make, project), BLOCK // 2, BIAS_UNIT)

    tab_blocks = micro * (atoms // TABLE_BLOCK)

    def table_grads(block):
        m, t = block // (atoms // TABLE_BLOCK), block % (atoms // TABLE_BLOCK)
        in_ref = pairs.at[m]
        rows = pl.ds(pl.multiple_of(t * TABLE_BLOCK, TABLE_BLOCK), TABLE_BLOCK)
        d8, p8, e8 = dist_s[m, rows, :], path_s[m, rows, :], edge_s[m, rows, :]
        acc = [jnp.zeros((DEPTH, heads), F32)]

        def make(r):
            for q in range(2):
                feats_s[r % SLOTS, :, q * atoms : (q + 1) * atoms] = features(
                    d8, p8, e8, 2 * r + q, spd, edges, kern
                )

        def collect(r):
            halves = [
                in_ref[pl.ds(t * TABLE_BLOCK + 2 * r + q, heads, stride=atoms), :] for q in range(2)
            ]
            acc[0] += dot_nt(feats_s[r % SLOTS], jnp.concatenate(halves, axis=1).astype(BF16))

        in_turn((make, collect), TABLE_BLOCK // 2, BIAS_UNIT)
        g_tab[...] += acc[0]

    def turned(n):
        return grads[:, :, :, n * width : (n + 1) * width].reshape(width, width)

    def turn_weights():
        for n, (ref, col) in enumerate([(wdown, 0), (wup, 0), (wout, 0)] + [(win, q) for q in range(3)]):
            for k in range(width // 256):
                block = ref[k * 256 : (k + 1) * 256, col * width : (col + 1) * width].astype(F32)
                block = jnp.transpose(block).astype(BF16)
                first = n * width + k * 256
                grads[:, :, :, first : first + 256] = block.reshape(grads.shape[:3] + (256,))

    def forward(m):
        x = rows_of(xs, m, atoms)[...].astype(F32)
        xh, _ = norm_parts(x)
        a = (xh * norms[0:1, :] + norms[2:3, :]).astype(BF16)
        rows_of(a_s, m, atoms)[...] = a
        qkv = rows_of(qkv_s, m, atoms)
        for blk in range(3):
            got = dot(a, win[:, blk * width : (blk + 1) * width])
            qkv[:, blk * width : (blk + 1) * width] = got.astype(BF16)
            if blk == 0:
                tr_q[...] = jnp.transpose(got.astype(BF16).astype(F32))
            if blk == 2:
                tr_b[...] = jnp.transpose(got).astype(BF16)

        def scores(pair):
            g, (tile, tiles, off) = pair // 8, windows[pair % 8]
            lane = g * 16 * head_dim + tile * LANES
            qm = both_columns(tr_q, lane, tiles, off, head_dim)
            z = dot(qkv[:, width + lane : width + lane + tiles * LANES], qm) * (scale * LOG2E)
            for q in range(2):
                pairs[m, head_rows(2 * pair + q), :] += z[:, q * atoms : (q + 1) * atoms]

        def softmax(pair):
            for q in range(2):
                z = pairs[m, head_rows(2 * pair + q), :]
                e = jnp.exp2(z - jnp.max(z, axis=0, keepdims=True))
                p = (e * (1.0 / jnp.sum(e, axis=0, keepdims=True))).astype(BF16)
                probs[m, pair_rows(pair), q * atoms : (q + 1) * atoms] = p

        def attend(pair):
            first = pair * 2 * head_dim
            got = dot(tr_b[first : first + 2 * head_dim, :], probs[m, pair_rows(pair), :])
            tr_f[first : first + head_dim, :] = got[:head_dim, :atoms]
            tr_f[first + head_dim : first + 2 * head_dim, :] = got[head_dim:, atoms:]

        in_turn((scores, softmax, attend), heads // 2, FORWARD_UNIT)

        o = jnp.transpose(tr_f[...]).astype(BF16)
        rows_of(o_s, m, atoms)[...] = o
        mid = x + dot(o, wout[...])
        rows_of(mid_s, m, atoms)[...] = mid
        xh, _ = norm_parts(mid)
        c = (xh * norms[1:2, :] + norms[3:4, :]).astype(BF16)
        rows_of(c_s, m, atoms)[...] = c
        u = dot(c, wup[...])
        rows_of(u_s, m, atoms)[...] = u
        act = gelu(u).astype(BF16)
        rows_of(act_s, m, atoms)[...] = act
        rows_of(hidden, m, atoms)[...] = (mid + dot(act, wdown[...])).astype(BF16)

    def backward_ffn(m):
        grad = rows_of(cot, m, atoms)[...].astype(F32) + rows_of(grecv, m, atoms)[...].astype(F32)
        df = grad.astype(BF16)
        rows_of(df_s, m, atoms)[...] = df
        du = (dot(df, turned(0)) * gelu_slope(rows_of(u_s, m, atoms)[...])).astype(BF16)
        rows_of(du_s, m, atoms)[...] = du
        dc = dot(du, turned(1))
        xh, inv_std = norm_parts(rows_of(mid_s, m, atoms)[...])
        g_norm[1:2, :] += jnp.sum(dc * xh, axis=0, keepdims=True)
        g_norm[3:4, :] += jnp.sum(dc, axis=0, keepdims=True)
        dmid = grad + norm_back(dc, xh, inv_std, norms[1:2, :])
        rows_of(mid_s, m, atoms)[...] = dmid
        dat = dmid.astype(BF16)
        rows_of(dat_s, m, atoms)[...] = dat
        do = dot(dat, turned(2)).astype(BF16)
        rows_of(dqkv_s, m, atoms)[:, 0:width] = do
        tr_q[...] = jnp.transpose(do.astype(F32))

    def backward_attn(m):
        qkv = rows_of(qkv_s, m, atoms)
        dqkv = rows_of(dqkv_s, m, atoms)
        tr_b[...] = jnp.transpose(qkv[:, width : 2 * width].astype(F32)).astype(BF16)

        def slopes(pair):
            g, (tile, tiles, off) = pair // 8, windows[pair % 8]
            lane = g * 16 * head_dim + tile * LANES
            dom = both_columns(tr_q, lane, tiles, off, head_dim)
            dp = dot(qkv[:, 2 * width + lane : 2 * width + lane + tiles * LANES], dom)
            for q in range(2):
                pairs[m, head_rows(2 * pair + q), :] = dp[:, q * atoms : (q + 1) * atoms]

        def softmax_back(pair):
            for q in range(2):
                half = slice(q * atoms, (q + 1) * atoms)
                p = probs[m, pair_rows(pair), half].astype(F32)
                pd = p * pairs[m, head_rows(2 * pair + q), :]
                ds = pd - p * jnp.sum(pd, axis=0, keepdims=True)
                pairs[m, head_rows(2 * pair + q), :] = ds
                ds_s[pair_rows(pair), half] = ds.astype(BF16)

        def products(pair):
            first = pair * 2 * head_dim
            got = dot(tr_b[first : first + 2 * head_dim, :], ds_s[pair_rows(pair), :])
            tr_f[first : first + head_dim, :] = got[:head_dim, :atoms]
            tr_f[first + head_dim : first + 2 * head_dim, :] = got[head_dim:, atoms:]
            for tile in range(16 * head_dim // LANES):
                inside = tile_pairs(tile, windows)
                if inside[-1][0] != pair % 8:
                    continue
                lane = pair // 8 * 16 * head_dim + tile * LANES
                these = [(pair // 8 * 8 + one, off) for one, off in inside]
                left = jnp.concatenate([probs[m, pair_rows(one), :] for one, _ in these], axis=1)
                block = dqkv[:, lane : lane + LANES]
                right = jnp.concatenate([both_heads(block, off, head_dim) for _, off in these], axis=0)
                dqkv[:, 2 * width + lane : 2 * width + lane + LANES] = dot(left, right).astype(BF16)
                left = jnp.concatenate([ds_s[pair_rows(one), :] for one, _ in these], axis=1)
                block = qkv[:, lane : lane + LANES]
                right = jnp.concatenate([both_heads(block, off, head_dim) for _, off in these], axis=0)
                dqkv[:, width + lane : width + lane + LANES] = (dot(left, right) * scale).astype(BF16)

        in_turn((slopes, softmax_back, products), heads // 2, BACKWARD_UNIT)

        dqkv[:, 0:width] = (jnp.transpose(tr_f[...]) * scale).astype(BF16)
        da = sum(dot(dqkv[:, q * width : (q + 1) * width], turned(3 + q)) for q in range(3))
        xh, inv_std = norm_parts(rows_of(xs, m, atoms)[...].astype(F32))
        g_norm[0:1, :] += jnp.sum(da * xh, axis=0, keepdims=True)
        g_norm[2:3, :] += jnp.sum(da, axis=0, keepdims=True)
        out = rows_of(mid_s, m, atoms)[...] + norm_back(da, xh, inv_std, norms[0:1, :])
        rows_of(igrad, m, atoms)[...] = out.astype(BF16)

    parts = grads.shape[-1] // width
    share = grads.shape[2]

    def chunk(n):
        return pl.ds(n * width if isinstance(n, int) else pl.multiple_of(n * width, LANES), width)

    def core_copy(n):
        return to(
            s, 2 * z + 1 - c, grads.at[:, 1 - c, :, chunk(n)], core_in.at[:, :, chunk(n)],
            core_send.at[n], core_recv.at[n],
        )

    class Line:
        def __init__(self, ref_of, into, out, sems, cols, count):
            self.ref_of, self.into, self.out, self.sems = ref_of, into, out, sems
            self.cols, self.count, self.steps = cols, count, (chips - 1) * count

        def right(self, n, target):
            return to(
                s, jnp.minimum(d + 2, 2 * chips - 1), self.ref_of(target).at[:, self.cols(n)],
                self.into.at[target + 1, :, self.cols(n)], self.sems[0].at[n, target], self.sems[1].at[n, target],
            )

        def left(self, n, target):
            return to(
                s, jnp.maximum(d - 2, 0), self.ref_of(target).at[:, self.cols(n)],
                self.into.at[target, :, self.cols(n)], self.sems[2].at[n, target], self.sems[3].at[n, target],
            )

        def end_copy(self, hop, n, act):
            @pl.when(z == 0)
            def _():
                act(self.right(n, chips - 1 - hop))

            @pl.when(z == chips - 1)
            def _():
                act(self.left(n, hop))

        def add_in(self, target, slot, cols):
            ref = self.ref_of(target)
            ref[:, cols] = (ref[:, cols].astype(F32) + self.into[slot, :, cols].astype(F32)).astype(BF16)

        def step(self, i):
            at_right, at_left = i - LAG * (z - 1), i - LAG * (chips - 2 - z)
            right, right_n = chips - 1 - at_right // self.count, at_right % self.count
            left, left_n = at_left // self.count, at_left % self.count

            @pl.when((z > 0) & (at_right >= 0) & (z <= right))
            def _():
                cols = self.cols(right_n)
                self.right(right_n, right).wait_recv()

                @pl.when(z < right)
                def _():
                    self.add_in(right, right + 1, cols)
                    self.right(right_n, right).start()

                @pl.when(z == right)
                def _():
                    self.out[:, cols] += self.into[right + 1, :, cols].astype(F32)

            @pl.when((z < chips - 1) & (at_left >= 0) & (z >= left))
            def _():
                cols = self.cols(left_n)
                self.left(left_n, left).wait_recv()

                @pl.when(z > left)
                def _():
                    self.add_in(left, left, cols)
                    self.left(left_n, left).start()

                @pl.when(z == left)
                def _():
                    self.out[:, cols] += self.into[left, :, cols].astype(F32)

            self.end_copy(i // self.count, i % self.count, lambda copy: copy.wait_send())

            @pl.when(i + self.count < self.steps)
            def _():
                self.end_copy(i // self.count + 1, i % self.count, lambda copy: copy.start())

        def drain(self, n):
            for target in range(chips):
                @pl.when((target > z) & (z > 0))
                def _():
                    self.right(n, target).wait_send()

                @pl.when((target < z) & (z < chips - 1))
                def _():
                    self.left(n, target).wait_send()

    donor, helper = s == 0, s == sections - 1
    own_parts = jnp.where(donor, parts - 1, parts)
    if chips:
        main = Line(
            lambda target: grads.at[target, c], line_in, sums, (line_send, line_recv, back_send, back_recv),
            chunk, own_parts,
        )

        def part_cols(n):
            return pl.ds(n * 2 * LANES if isinstance(n, int) else pl.multiple_of(n * 2 * LANES, LANES), 2 * LANES)

        guest_sum = mid_s.at[0:share, :]
        guest = Line(
            lambda target: guest_in.at[target], guest_line, guest_sum, (gl_send, gl_recv, gb_send, gb_recv),
            part_cols, width // (2 * LANES),
        )

    def guest_copy():
        return to(
            sections - 1, d, grads.at[:, c, :, chunk(parts - 1)], guest_in, guest_sem.at[0], guest_sem.at[1]
        )

    def result_copy():
        return to(0, d, guest_low, guest_low, guest_sem.at[2], guest_sem.at[3])

    def settle(n):
        core_copy(n).wait_recv()
        for target in range(chips):
            both = grads[target, c, :, chunk(n)].astype(F32) + core_in[target, :, chunk(n)].astype(F32)
            grads[target, c, :, chunk(n)] = both.astype(BF16)

            @pl.when(z == target)
            def _():
                sums[:, chunk(n)] = both

        if n < parts - 1:
            main.end_copy(0, n, lambda copy: copy.start())
        else:
            @pl.when(donor)
            def _():
                guest_copy().start()

            @pl.when(jnp.logical_not(donor))
            def _():
                main.end_copy(0, n, lambda copy: copy.start())

    def norm_copy():
        return to(s, 2 * z + 1 - c, g_norm, norm_core, nc_sem.at[0], nc_sem.at[1])

    def weight_grads(lo, hi):
        jobs = [(act_s, df_s, 0), (c_s, du_s, 0), (o_s, dat_s, 0)] + [(a_s, dqkv_s, q) for q in range(3)]
        for n, (left, right, col) in list(enumerate(jobs))[lo:hi]:
            if col == 0:
                for m in range(micro):
                    part = left[m * atoms : (m + 1) * atoms, :].astype(F32)
                    first = m // 2 * width
                    ds_s[first : first + width, m % 2 * atoms : (m % 2 + 1) * atoms] = jnp.transpose(
                        part
                    ).astype(BF16)

            @pl.loop(0, width // 256)
            def _(q):
                cols = pl.ds(pl.multiple_of(col * width + q * 256, 256), 256)
                turned_left = [ds_s[k * width : (k + 1) * width, :] for k in range(micro // 2)]
                got = dot(jnp.concatenate(turned_left, axis=1), right[:, cols]).astype(BF16)
                cols = pl.ds(pl.multiple_of(n * width + q * 256, 256), 256)
                grads[:, :, :, cols] = got.reshape(grads.shape[:3] + (256,))

            if chips:
                core_copy(n).start()
                if n:
                    settle(n - 1)

    def norm_window(dp):
        first = jnp.minimum(dp * share // LANES, width // LANES - 2)
        return pl.ds(pl.multiple_of(first * LANES, LANES), 2 * LANES)

    def norm_line(there, here):
        return to(
            s, 2 * there + c, norm_sum.at[:, norm_window(2 * there + c)], norm_in.at[here],
            nz_send.at[there], nz_recv.at[here],
        )

    def tab_copy():
        return to(s, 2 * z + 1 - c, tab_own, tab_core, tc_sem.at[0], tc_sem.at[1])

    def tab_section(there, here):
        return to(there, d, tab_sum.at[0], tab_sec.at[here], ts_send.at[there], ts_recv.at[here])

    def tab_chip(there, here):
        return to(s, 2 * there + c, tab_sum.at[1], tab_line.at[here], tz_send.at[there], tz_recv.at[here])

    def others(mine, count, act):
        for other in range(count):
            @pl.when(other != mine)
            def _():
                act(other)

    def reduce_all():
        norm_copy().wait_recv()
        norm_sum[...] = g_norm[...] + norm_core[...]
        norm_in[z] = norm_sum[:, norm_window(d)]
        others(z, chips, lambda o: norm_line(o, z).start())

        tab_steps = (chips - 1) * (parts - 1) - 6
        tab_each = -(-tab_blocks // tab_steps)

        def tab_over_chips():
            others(s, sections, lambda o: tab_section(o, o).wait_recv())
            tab_sum[1] = sum(tab_sec[o] for o in range(sections))
            tab_line[z] = tab_sum[1]
            others(z, chips, lambda o: tab_chip(o, z).start())

        @pl.loop(0, main.steps)
        def _(i):
            @pl.when(i < tab_steps)
            def _():
                @pl.loop(i * tab_each, jnp.minimum((i + 1) * tab_each, tab_blocks))
                def _(block):
                    table_grads(block)

            @pl.when(i == tab_steps)
            def _():
                wide_tab = jnp.concatenate([g_tab[...], jnp.zeros((DEPTH, LANES - heads), F32)], axis=1)
                tab_own[...] = jnp.transpose(wide_tab)[:heads, :]
                tab_copy().start()

            @pl.when(i == tab_steps + 1)
            def _():
                tab_copy().wait_recv()
                tab_sum[0] = tab_own[...] + tab_core[...]
                tab_sec[s] = tab_sum[0]
                others(s, sections, lambda o: tab_section(o, s).start())

            @pl.when((i == tab_steps + 3) & (s < 2))
            def _():
                tab_over_chips()

            main.step(i)

        @pl.when(helper)
        def _():
            guest_copy().wait_recv()
            guest_sum[...] = guest_in[z].astype(F32)
            for n in range(guest.count):
                guest.end_copy(0, n, lambda copy: copy.start())

            pl.loop(0, guest.steps)(guest.step)
            guest_low[...] = guest_sum[...].astype(BF16)
            result_copy().start()

        @pl.when(s >= 2)
        def _():
            tab_over_chips()

        others(z, chips, lambda o: norm_line(o, o).wait_recv())
        s_norm[...] = sum(norm_in[o] for o in range(chips))
        others(z, chips, lambda o: tab_chip(o, o).wait_recv())
        s_tab[...] = sum(tab_line[o] for o in range(chips))

        norm_copy().wait_send()
        tab_copy().wait_send()
        others(z, chips, lambda o: norm_line(o, z).wait_send())
        others(s, sections, lambda o: tab_section(o, s).wait_send())
        others(z, chips, lambda o: tab_chip(o, z).wait_send())

        @pl.loop(0, parts)
        def _(n):
            core_copy(n).wait_send()

            @pl.when(n < own_parts)
            def _():
                main.drain(n)

        @pl.when(helper)
        def _():
            pl.loop(0, guest.count)(guest.drain)
            result_copy().wait_send()

        @pl.when(donor)
        def _():
            guest_copy().wait_send()
            result_copy().wait_recv()
            sums[:, chunk(parts - 1)] = guest_low[...].astype(F32)

    pl.loop(0, 2)(make_bias)
    if chips:
        pl.semaphore_wait(barrier, sections + chips - 1)
    elif sections > 1:
        pl.semaphore_wait(barrier, jnp.where((s > 0) & (s < sections - 1), 2, 1))

    total = 4 * micro

    @pl.loop(2, total)
    def _(t):
        ahead = jnp.where(last, micro, jnp.minimum(micro, jnp.where(s == 0, 1, 2 * s * s)))
        gap = micro - ahead
        r = t - 2 * ahead
        mixed = (r >= 0) & (r < 3 * gap)
        unit = jnp.where(r < 0, t, 2 * (ahead + r // 3) + r % 3 - 1)
        is_bias = (r < 0) | (mixed & (r % 3 != 0))
        is_fwd = jnp.where(
            last, (r >= 0) & (r % 2 == 0), (mixed & (r % 3 == 0)) | ((r >= 3 * gap) & (t < 3 * micro))
        )
        m_fwd = jnp.where(last, r // 2, jnp.where(mixed, r // 3, r - 2 * gap))
        is_back = jnp.where(last, (r >= 0) & (r % 2 == 1), t >= 3 * micro)
        m_back = jnp.where(last, r // 2, t - 3 * micro)
        @pl.when(is_bias)
        def _():
            make_bias(unit)

        @pl.when(is_fwd & (m_fwd == 0))
        def _():
            for k in range(len(loads) - 1):
                load(k).wait()

            @pl.when(s == 0)
            def _():
                load_tokens().wait()

        @pl.when(jnp.where(s >= 2, is_fwd & (m_fwd == 0), is_back & (m_back == 0)))
        def _():
            turn_weights()

        @pl.when(is_fwd)
        def _():
            if sections > 1:
                @pl.when(s > 0)
                def _():
                    forward_copy(m_fwd).wait_recv()

            forward(m_fwd)
            if sections > 1:
                @pl.when(jnp.logical_not(last))
                def _():
                    forward_copy(m_fwd).start()

        @pl.when(is_back)
        def _():
            @pl.when(m_back == 0)
            def _():
                load(len(loads) - 1).wait()

            if sections > 1:
                @pl.when(jnp.logical_not(last))
                def _():
                    backward_copy(m_back).wait_recv()

            backward_ffn(m_back)

            @pl.when((s == 0) & (m_back == micro - 1))
            def _():
                weight_grads(0, 3)

            backward_attn(m_back)
            if sections > 1:
                @pl.when(s > 0)
                def _():
                    backward_copy(m_back).start()

    @pl.when(s != 0)
    def _():
        weight_grads(0, 3)

    if chips:
        norm_copy().start()
    weight_grads(3, parts)
    if chips:
        settle(parts - 1)
    if chips:
        reduce_all()
    else:
        pl.loop(0, tab_blocks)(table_grads)

    if sections > 1:
        @pl.loop(0, micro)
        def _(m):
            @pl.when(jnp.logical_not(last))
            def _():
                forward_copy(m).wait_send()

            @pl.when(s > 0)
            def _():
                backward_copy(m).wait_send()


def layer_call(
    sections, chips, tokens, cot, posn, group, counts, path_in, edge_in, win, wout, wup, wdown,
    norm_gain, norm_shift, kernel_proj, path_table, edge_table,
):
    micro, _, atoms = posn.shape
    rows, width = tokens.shape
    kern, heads = kernel_proj.shape
    spd, edges = path_table.shape[0], edge_table.shape[0]
    shape = jax.ShapeDtypeStruct
    vmem, smem = pl.BlockSpec(memory_space=pltpu.VMEM), pl.BlockSpec(memory_space=pltpu.SMEM)
    low = lambda *dims: pltpu.VMEM(dims, BF16)
    wide = lambda *dims: pltpu.VMEM(dims, F32)
    sems = lambda *dims: pltpu.SemaphoreType.DMA(dims)
    parts = 3 + win.shape[1] // width
    all_pairs = heads // 2 * atoms
    outs = [shape((rows, width), BF16), shape((rows, width), BF16)]
    share = width // (2 * chips) if chips else width
    grads = (chips, 2, share, parts * width) if chips else (1, 1, width, parts * width)
    local = [(grads, BF16), ((8, width), F32), ((DEPTH, heads), F32)]
    scratch = []
    if chips:
        outs += [shape((share, parts * width), F32)]
        outs += [shape((8, 2 * LANES), F32), shape((heads, DEPTH), F32)]
        scratch += [pltpu.VMEM(dims, kind) for dims, kind in local]
    else:
        outs += [shape(dims, kind) for dims, kind in local]
    scratch += [
        low(rows, width), low(rows, width), low(rows, width), low(rows, 3 * width), low(rows, width),
        wide(rows, width), low(rows, width), wide(rows, width), low(rows, width), low(rows, width),
        low(rows, width), low(rows, width), low(rows, 3 * width),
        wide(micro, 2 * all_pairs, atoms), low(micro, all_pairs, 2 * atoms),
        wide(micro, atoms, atoms), wide(micro, atoms, atoms), wide(micro, atoms, atoms),
        low(width, atoms), wide(width, atoms), wide(width, atoms), low(SLOTS, DEPTH, 2 * atoms), low(all_pairs, 2 * atoms),
        low(rows, width), low(*win.shape), low(*wout.shape), low(*wup.shape), low(*wdown.shape),
        wide(4, width), wide(heads, DEPTH), low(heads, DEPTH), sems(6),
    ] + [sems(micro)] * 4
    if chips:
        scratch += [
            low(chips, share, parts * width), low(chips + 1, share, parts * width),
            wide(8, width), wide(8, width), wide(chips, 8, 2 * LANES),
            wide(heads, DEPTH), wide(heads, DEPTH), wide(2, heads, DEPTH),
            wide(sections, heads, DEPTH), wide(chips, heads, DEPTH),
            sems(parts), sems(parts), sems(parts, chips), sems(parts, chips), sems(parts, chips), sems(parts, chips),
            sems(2), sems(chips), sems(chips), sems(2), sems(sections), sems(sections), sems(chips), sems(chips),
            low(chips, share, width), low(chips + 1, share, width), low(share, width),
        ] + [sems(width // (2 * LANES), chips)] * 4 + [
            sems(4),
        ]
    params = dict(vmem_limit_bytes=60 * 2**20, has_side_effects=True)
    if sections > 1:
        params["collective_id"] = 0
    return pl.pallas_call(
        functools.partial(body, sections, chips, micro, atoms, heads, kern, spd, edges),
        out_shape=outs,
        in_specs=[smem, smem] + [vmem] * 8 + [pl.BlockSpec(memory_space=pl.ANY)] * 6,
        out_specs=[vmem] * len(outs),
        scratch_shapes=scratch,
        compiler_params=pltpu.CompilerParams(**params),
        name="sections",
    )(
        group, counts, jnp.transpose(posn, (1, 0, 2)), path_in, edge_in, norm_gain.T, norm_shift.T,
        kernel_proj.T, path_table.T, edge_table, tokens, cot, win, wout, wup, wdown,
    )


def finish_body(
    width, kern, spd, edges, sections,
    hidden, igrad, sums, norm, tab,
    hidden_o, igrad_o, in_o, out_o, up_o, down_o, gain_o, shift_o, kern_o, path_o, edge_o, tab_s, norm_s,
):
    hidden_o[...] = hidden[...]
    igrad_o[...] = igrad[...]
    for k, ref in enumerate((down_o, up_o, out_o)):
        ref[...] = sums[:, k * width : (k + 1) * width]
    in_o[...] = sums[:, 3 * width :]
    @pl.when(pl.program_id(0) == 0)
    def _():
        share = gain_o.shape[1]
        section, first = lax.axis_index("section"), lax.axis_index("dp") * share
        first = first - jnp.minimum(first // LANES, width // LANES - 2) * LANES
        norm_s[...] = jnp.transpose(norm[...])
        rows = norm_s[pl.ds(pl.multiple_of(first, 8), share), :]
        rows = jnp.transpose(jnp.concatenate([rows, jnp.zeros((share, LANES - 8), F32)], axis=1))
        gain_o[...] = rows[0:2, :]
        shift_o[...] = rows[2:4, :]
        tab_s[...] = jnp.transpose(tab[...])
        start = 0
        for count, ref in ((kern, kern_o), (spd, path_o), (edges, edge_o)):
            own = count // sections
            ref[...] = tab_s[pl.ds(pl.multiple_of(start + section * own, 8), own), :]
            start += count


def finish(hidden, igrad, sums, norm, tab, kern, spd, edges, sections):
    width, heads = hidden.shape[1], tab.shape[0]
    share = sums.shape[0]
    shape = jax.ShapeDtypeStruct
    strip = lambda a: pl.BlockSpec((a.shape[0] // STRIPS, a.shape[1]), lambda i: (i, 0))
    whole = lambda a: pl.BlockSpec(a.shape, lambda i: (0, 0))
    outs = (
        [shape(hidden.shape, BF16), shape(igrad.shape, BF16), shape((share, sums.shape[1] - 3 * width), F32)]
        + [shape((share, width), F32)] * 3
        + [shape((2, share), F32)] * 2
        + [shape((count // sections, heads), F32) for count in (kern, spd, edges)]
    )
    return pl.pallas_call(
        functools.partial(finish_body, width, kern, spd, edges, sections),
        out_shape=outs,
        grid=(STRIPS,),
        in_specs=[strip(a) for a in (hidden, igrad, sums)] + [whole(a) for a in (norm, tab)],
        out_specs=[strip(a) for a in outs[:6]] + [whole(a) for a in outs[6:]],
        scratch_shapes=[pltpu.VMEM((DEPTH, heads), F32), pltpu.VMEM((2 * LANES, 8), F32)],
        compiler_params=pltpu.CompilerParams(vmem_limit_bytes=60 * 2**20),
        name="finish",
    )(hidden, igrad, sums, norm, tab)


def on_device(
    tokens, cotangent, positions, conformer_group, atom_counts, path_dist, edge_kind, attn_in, attn_out,
    ffn_up, ffn_down, norm_gain, norm_shift, kernel_proj, path_table, edge_table,
):
    sections, count = lax.axis_size("section"), lax.axis_size("dp")
    section, place = lax.axis_index("section"), lax.axis_index("dp")
    kern, heads = kernel_proj.shape
    spd, edges = path_table.shape[0], edge_table.shape[0]
    width = attn_out.shape[1]
    share = width // count
    chips = 4 if count == 8 and share % 16 == 0 and share <= LANES else 0
    hidden, igrad, *sums = layer_call(
        sections, chips, tokens, cotangent[0], positions, conformer_group, atom_counts, path_dist, edge_kind,
        attn_in[0], attn_out[0], ffn_up[0], ffn_down[0], norm_gain[0], norm_shift[0],
        kernel_proj, path_table, edge_table,
    )
    if chips:
        outs = finish(hidden, igrad, *sums, kern, spd, edges, sections)
        norms = [jnp.transpose(o) for o in outs[6:8]]
        return tuple(o[None] for o in [*outs[:6], *norms]) + tuple(outs[8:])
    grads, g_norm, g_tab = sums
    split = lambda a, n: grads[0, 0, :, a * width : (a + n) * width]
    sums = [
        lax.psum_scatter(g, "dp", scatter_dimension=0, tiled=True).astype(F32)
        for g in (split(3, 3), split(2, 1), split(1, 1), split(0, 1))
    ]
    norm_sum = lax.psum(g_norm[:4], "dp").T
    norm_sum = lax.dynamic_slice_in_dim(norm_sum, place * share, share, 0)[None]
    tab_sum = lax.psum(g_tab, ("section", "dp"))
    tabs, start = [], 0
    for rows in (kern, spd, edges):
        own = rows // sections
        tabs.append(lax.dynamic_slice_in_dim(tab_sum, start + section * own, own, 0))
        start += rows
    return (hidden[None], igrad[None], *(g[None] for g in sums), norm_sum[:, :, :2], norm_sum[:, :, 2:], *tabs)


def solution(mesh):
    in_specs = (
        P("dp", None),
        P("section", "dp", None),
        P("dp", None, None),
        P("dp"),
        P("dp"),
        P("dp", None, None),
        P("dp", None, None),
        P("section", None, None),
        P("section", None, None),
        P("section", None, None),
        P("section", None, None),
        P("section", None, None),
        P("section", None, None),
        P(),
        P(),
        P(),
    )
    out_specs = (
        P("section", "dp", None),
        P("section", "dp", None),
        P("section", "dp", None),
        P("section", "dp", None),
        P("section", "dp", None),
        P("section", "dp", None),
        P("section", "dp", None),
        P("section", "dp", None),
        P("section", None),
        P("section", None),
        P("section", None),
    )
    return jax.shard_map(
        on_device, mesh=mesh, in_specs=in_specs, out_specs=out_specs, check_vma=False
    )
```
